32 devices in a mesh: row: 4 (over y, core), col: 8 (over z, x).
Axes of the slice: x: 2, y: 2, z: 4, core: 2. Of those that a mesh axis runs over, the one named last changes fastest.
Arguments:
- cond_orbitals: bfloat16 [32, 48, 2304], P(('row', 'col')), may hold values from -6 to 6
- occ_orbitals: bfloat16 [32, 48, 2304], P(('row', 'col')), may hold values from -6 to 6
- cond_energy: float32 [32], replicated, may hold values from 0.02 to 1
- occ_energy: float32 [32], replicated, may hold values from -1 to -0.02
- occ_band: int32 [32], replicated, may hold values from 0 to 31, each once
- sphere_index: int32 [3, 8192], replicated, may hold values from 0 to 47, as said below
Outputs:
- chi_zero: float32 [16384, 16384], P('row', 'col')
The draws below stay inside these ranges and needn't reach their ends.
Inputs may be any that keep to these rules, and one draw needn't show every extreme that they name: `sphere_index`: columns are 8192 distinct wave vectors (gx, gy, gz) stored modulo 48, with gx and gy from -18 to 18 and gz from 1 to 18. `occ_band`: each occupied band number appears once.
All inputs are finite; a program needn't handle non-finite values.
Results may differ from the reference program's by a relative error of at most 0.013.
Values may be sent and summed in bfloat16 or wider, within the bound.
No kernel may reach another device: no remote copies, remote signals or barrier semaphores. Data moves between devices by JAX's collectives and lax.ppermute only.
A program may use at most 128 MiB of HBM per device.

```python
import jax
import jax.numpy as jnp
from jax import lax

GRID = 48
GMAX = 18
NHALF = 8192
OCC_DEV = 1
STEPS = 2
NC = 32
NV = 32
N_COL = 8


def draw_sphere_index(key, part):
    key = jax.random.fold_in(key, 7)
    span_count = 2 * GMAX + 1
    chosen = jax.random.permutation(key, span_count * span_count * GMAX)[:NHALF]
    z_index = chosen % GMAX + 1
    y_index = chosen // GMAX % span_count - GMAX
    x_index = chosen // (GMAX * span_count) - GMAX
    return jnp.stack([x_index % GRID, y_index % GRID, z_index]).astype(jnp.int32)


def levels(own_key, extent, split, low, top_value):
    factor_of = 1.0
    for position, blocks in split:
        heights = jax.random.uniform(jax.random.fold_in(jax.random.fold_in(own_key, 6), position), (blocks,), jnp.float32, low / len(split), top_value / len(split))
        factor_of = factor_of * jnp.repeat(jnp.exp(heights), extent[position] // blocks).reshape((-1,) + (1,) * (len(extent) - 1 - position))
    return factor_of


def noise(rng, shape, width, reach, split=(), held_as=jnp.bfloat16):
    array = width * jax.random.normal(rng, shape, jnp.float32)
    if split:
        array = array * levels(rng, shape, split, -0.22, 0.18)
    return jnp.clip(array, -reach, reach).astype(held_as)


def setup_inputs(seed: int = 0) -> dict:
    key_list = jax.random.split(jax.random.key(seed), 7)
    cond_orbitals = noise(key_list[0], (NC, GRID, GRID * GRID), 1.0, 6.0, ((0, 32),))
    occ_orbitals = noise(key_list[1], (NV, GRID, GRID * GRID), 1.0, 6.0, ((0, 32),))
    cond_energy = jnp.clip(jax.random.uniform(key_list[2], (NC,), jnp.float32, 0.02, 1.0), 0.02, 1.0)
    occ_energy = jnp.clip(jax.random.uniform(key_list[3], (NV,), jnp.float32, -1.0, -0.02), -1.0, -0.02)
    occ_band = jax.random.permutation(key_list[4], NV).astype(jnp.int32)
    sphere_index = draw_sphere_index(jax.random.fold_in(key_list[6], 71), 0)
    return dict(cond_orbitals=cond_orbitals, occ_orbitals=occ_orbitals, cond_energy=cond_energy, occ_energy=occ_energy, occ_band=occ_band, sphere_index=sphere_index)


omega_squared = 0.0625


def reference(cond_orbitals, occ_orbitals, cond_energy, occ_energy, occ_band, sphere_index):
    cond_total = cond_orbitals.shape[0]
    grid_size = cond_orbitals.shape[1]
    per_band = STEPS * OCC_DEV
    pair_total = cond_total * per_band
    occ_blocks = occ_orbitals.reshape(cond_total, OCC_DEV, grid_size, grid_size * grid_size)
    band_energy = jnp.take(occ_energy, occ_band).reshape(cond_total, OCC_DEV)
    norm_factor = grid_size ** -1.5

    def one_band(band_number):
        offsets = jnp.arange(STEPS, dtype=jnp.int32) * N_COL
        block_ids = ((band_number - offsets) % cond_total).astype(jnp.int32)
        occupied = jnp.take(occ_blocks, block_ids, axis=0).reshape(per_band, grid_size, grid_size * grid_size)
        energies = jnp.take(band_energy, block_ids, axis=0).reshape(per_band)
        conduction = jnp.take(cond_orbitals, band_number, axis=0)
        density = (conduction.astype(jnp.float32)[None] * occupied.astype(jnp.float32)).astype(jnp.bfloat16)
        density = lax.optimization_barrier(density).astype(jnp.float32)
        density = density.reshape(per_band, grid_size, grid_size, grid_size)
        spectrum = jnp.fft.fftn(density, axes=(1, 2, 3))
        picked = spectrum[:, sphere_index[0], sphere_index[1], sphere_index[2]]
        coef_parts = jnp.concatenate([jnp.real(picked), jnp.imag(picked)], axis=1) * norm_factor
        coefficients = coef_parts.astype(jnp.float32).astype(jnp.bfloat16)
        energy_gap = jnp.take(cond_energy, band_number) - energies
        weight = -4.0 * energy_gap / (energy_gap * energy_gap + omega_squared) / pair_total
        scaled = (weight[:, None] * coefficients.astype(jnp.float32)).astype(jnp.bfloat16)
        return coefficients, scaled

    coefficients, scaled = lax.map(one_band, jnp.arange(cond_total, dtype=jnp.int32))
    coef_width = coefficients.shape[-1]
    coefficients = coefficients.reshape(pair_total, coef_width).astype(jnp.float32)
    scaled = scaled.reshape(pair_total, coef_width).astype(jnp.float32)
    return jnp.dot(coefficients.T, scaled, preferred_element_type=jnp.float32)
```

```python
import functools
import math

import jax
import jax.numpy as jnp
import numpy as np
from jax import lax
from jax.experimental import pallas as pl
from jax.experimental.pallas import tpu as pltpu
from jax.sharding import PartitionSpec as P

GMAX = 18
STEPS = 2
RADIX = 6
SPAN = 2 * GMAX + 1
KX_ROWS = 40
LANES = 128
OMEGA_SQUARED = 0.0625
TILE = 512


def split_table(table):
    upper = table.astype(jnp.bfloat16)
    lower = (table - upper.astype(np.float64)).astype(jnp.bfloat16)
    return upper, lower


def tables(grid):
    y_lo_count = grid // RADIX
    turn = 2.0 * np.pi / grid
    kx = np.arange(SPAN) - GMAX
    angle = turn * (kx[:, None] * np.arange(grid)[None, :] % grid)
    x_table = np.zeros((2 * KX_ROWS, grid))
    x_table[:SPAN] = np.cos(angle)
    x_table[KX_ROWS : KX_ROWS + SPAN] = -np.sin(angle)
    x_table = np.concatenate(split_table(x_table), axis=1)

    width = y_lo_count * grid
    y_lo = np.arange(width) // grid
    z = np.arange(width) % grid
    angle = turn * (np.arange(RADIX)[:, None] * y_lo[None, :] % grid)
    twiddle = np.concatenate([np.cos(angle), -np.sin(angle)], axis=0).astype(np.float32)

    column = np.arange((2 * GMAX // RADIX + 1) * GMAX)
    q = column // GMAX - GMAX // RADIX
    kz = column % GMAX + 1
    phase = (RADIX * q[None, :] * y_lo[:, None] + kz[None, :] * z[:, None]) % grid
    cos_part = np.zeros((width, LANES))
    sin_part = np.zeros((width, LANES))
    cos_part[:, : column.size] = np.cos(turn * phase)
    sin_part[:, : column.size] = -np.sin(turn * phase)
    last = np.block([[cos_part, sin_part], [-sin_part, cos_part]])
    upper, lower = split_table(last)
    return x_table, twiddle, upper, lower


def dft_six(re, im):
    half = 0.5
    root = math.sqrt(3.0) / 2.0
    s_re = [re[h] + re[h + 3] for h in range(3)]
    s_im = [im[h] + im[h + 3] for h in range(3)]
    d_re = [re[h] - re[h + 3] for h in range(3)]
    d_im = [im[h] - im[h + 3] for h in range(3)]
    out = [None] * 6
    sum_re, sum_im = s_re[1] + s_re[2], s_im[1] + s_im[2]
    dif_re, dif_im = (s_re[1] - s_re[2]) * root, (s_im[1] - s_im[2]) * root
    out[0] = (s_re[0] + sum_re, s_im[0] + sum_im)
    mid_re, mid_im = s_re[0] - half * sum_re, s_im[0] - half * sum_im
    out[2] = (mid_re + dif_im, mid_im - dif_re)
    out[4] = (mid_re - dif_im, mid_im + dif_re)
    sum_re, sum_im = (d_re[1] + d_re[2]) * root, (d_im[1] + d_im[2]) * root
    dif_re, dif_im = d_re[1] - d_re[2], d_im[1] - d_im[2]
    out[3] = (d_re[0] - dif_re, d_im[0] - dif_im)
    mid_re, mid_im = d_re[0] + half * dif_re, d_im[0] + half * dif_im
    out[1] = (mid_re + sum_im, mid_im - sum_re)
    out[5] = (mid_re - sum_im, mid_im + sum_re)
    return out


def dot(a, b):
    return jnp.dot(a, b, preferred_element_type=jnp.float32)


def transform_kernel(grid, cond_ref, occ0_ref, occ1_ref, sphere_ref, x_table_ref, twiddle_ref, upper_ref, lower_ref, out_ref, cube_ref):
    norm = np.float32(grid ** (-1.5))
    width = (grid // RADIX) * grid
    for pair, occ_ref in enumerate((occ0_ref, occ1_ref)):
        density = (cond_ref[0].astype(jnp.float32) * occ_ref[0].astype(jnp.float32)).astype(jnp.bfloat16)
        section = dot(x_table_ref[...], jnp.concatenate([density, density], axis=0))
        re = [section[:KX_ROWS, h * width : (h + 1) * width] for h in range(RADIX)]
        im = [section[KX_ROWS:, h * width : (h + 1) * width] for h in range(RADIX)]
        rows = []
        for residue, (d_re, d_im) in enumerate(dft_six(re, im)):
            if residue > 0:
                t_re = twiddle_ref[residue : residue + 1, :]
                t_im = twiddle_ref[RADIX + residue : RADIX + residue + 1, :]
                d_re, d_im = d_re * t_re - d_im * t_im, d_re * t_im + d_im * t_re
            rows.append(jnp.concatenate([d_re, d_im], axis=1))
        whole = jnp.concatenate(rows, axis=0)
        whole_hi = whole.astype(jnp.bfloat16)
        whole_lo = (whole - whole_hi.astype(jnp.float32)).astype(jnp.bfloat16)
        spectrum = dot(whole_hi, upper_ref[...]) + dot(whole_lo, upper_ref[...]) + dot(whole_hi, lower_ref[...])
        spectrum = spectrum * norm
        parts = []
        for side in range(2):
            own = spectrum[:, side * LANES : (side + 1) * LANES]
            for group in range(RADIX // 2):
                first = 2 * group * KX_ROWS
                parts.append(jnp.concatenate([own[first : first + KX_ROWS], own[first + KX_ROWS : first + 2 * KX_ROWS]], axis=1))
        rows_per_pair = RADIX * KX_ROWS
        cube_ref[pair * rows_per_pair : (pair + 1) * rows_per_pair, :] = jnp.concatenate(parts, axis=0).astype(jnp.bfloat16)

    half = grid // 2
    picks = RADIX // 2 * KX_ROWS
    half_count = sphere_ref.shape[1]
    for first in range(0, half_count, TILE):
        here = slice(first, first + TILE)
        sx, sy, kz = sphere_ref[0:1, here], sphere_ref[1:2, here], sphere_ref[2:3, here]
        kx = jnp.where(sx >= half, sx - grid, sx) + GMAX
        ky = jnp.where(sy >= half, sy - grid, sy) + GMAX
        q = (ky * 43) >> 8
        residue = ky - q * RADIX
        lane = (residue & 1) * LANES + q * GMAX + kz - 1
        row = (residue >> 1) * KX_ROWS + kx
        one_hot = (lax.broadcasted_iota(jnp.int32, (2 * LANES, TILE), 0) == lane).astype(jnp.float32).astype(jnp.bfloat16)
        chosen = lax.broadcasted_iota(jnp.int32, (picks, TILE), 0) == row
        found = dot(cube_ref[...], one_hot)
        for pair in range(2):
            for side in range(2):
                start = (pair * 2 + side) * picks
                value = jnp.sum(jnp.where(chosen, found[start : start + picks], 0.0), axis=0, keepdims=True)
                out_ref[pair : pair + 1, side * half_count + first : side * half_count + first + TILE] = value.astype(jnp.bfloat16)


def transform(cond_orbitals, occ_first, occ_second, sphere_index):
    grid = cond_orbitals.shape[1]
    held = [jnp.asarray(t) for t in tables(grid)]
    half_count = sphere_index.shape[1]
    return pl.pallas_call(
        functools.partial(transform_kernel, grid),
        out_shape=jax.ShapeDtypeStruct((STEPS, 2 * half_count), jnp.bfloat16),
        scratch_shapes=[pltpu.VMEM((STEPS * 2 * RADIX // 2 * KX_ROWS, 2 * LANES), jnp.bfloat16)],
        compiler_params=pltpu.CompilerParams(vmem_limit_bytes=40 * 2**20),
        name="transform",
    )(cond_orbitals, occ_first, occ_second, sphere_index, *held)


def pack_kernel(rows, cols, sources, place_ref, cond_energy_ref, occ_energy_ref, occ_band_ref, *refs):
    arrived, outs, mixed_ref = refs[: len(sources)], refs[len(sources) : -1], refs[-1]
    r, c = place_ref[0], place_ref[1]
    devices = rows * cols
    pairs = STEPS * len(sources)
    total = 2 * mixed_ref.shape[1]
    entries = mixed_ref.shape[1]
    row_width, col_width = entries // rows, entries // cols
    line = lax.broadcasted_iota(jnp.int32, (pairs, LANES), 0)
    gap = jnp.zeros((pairs, LANES), jnp.float32)
    for j, (ref, source) in enumerate(zip(arrived, sources)):
        mixed_ref[STEPS * j : STEPS * (j + 1), :] = ref[...].astype(jnp.float32)
        band = r * cols + source(c)
        for step in range(STEPS):
            slot = lax.rem(band - step * cols + devices, devices)
            value = cond_energy_ref[band] - occ_energy_ref[occ_band_ref[slot]]
            gap = jnp.where(line == STEPS * j + step, value, gap)
    weight = -4.0 * gap / (gap * gap + OMEGA_SQUARED) / (devices * STEPS)
    weight = weight[:, :1]
    column = mixed_ref[:, pl.ds(pl.multiple_of(c * col_width, LANES), col_width)]
    column = (weight * column).astype(jnp.bfloat16)
    for k, out_ref in enumerate(outs):
        block = lax.rem(r + k, rows)
        out_ref[:, :row_width] = mixed_ref[:, pl.ds(pl.multiple_of(block * row_width, LANES), row_width)].astype(jnp.bfloat16)
        out_ref[:, row_width:] = column


def pack(arrived, sources, place, cond_energy, occ_energy, occ_band, rows, cols):
    entries = arrived[0].shape[1]
    pairs = STEPS * len(arrived)
    message = jax.ShapeDtypeStruct((pairs, entries // rows + entries // cols), jnp.bfloat16)
    smem = pl.BlockSpec(memory_space=pltpu.SMEM)
    vmem = pl.BlockSpec(memory_space=pltpu.VMEM)
    return pl.pallas_call(
        functools.partial(pack_kernel, rows, cols, sources),
        out_shape=[message] * rows,
        in_specs=[smem] * 4 + [vmem] * len(arrived),
        out_specs=[vmem] * rows,
        scratch_shapes=[pltpu.VMEM((pairs, entries), jnp.float32)],
        compiler_params=pltpu.CompilerParams(vmem_limit_bytes=40 * 2**20),
        name="pack",
    )(place, cond_energy, occ_energy, occ_band, *arrived)


def outer_kernel(row_width, block, *refs):
    messages, out_ref, left_ref, right_ref = refs[:-3], refs[-3], refs[-2], refs[-1]
    depth = messages[0].shape[0]

    @pl.when(pl.program_id(0) == 0)
    def _():
        for j, ref in enumerate(messages):
            left_ref[depth * j : depth * (j + 1), :] = ref[:, :row_width]
            right_ref[depth * j : depth * (j + 1), :] = ref[:, row_width:]

    here = pl.ds(pl.multiple_of(pl.program_id(0) * block, block), block)
    out_ref[...] = lax.dot_general(
        left_ref[:, here], right_ref[...], (((0,), (0,)), ((), ())), preferred_element_type=jnp.float32
    )


def outer(messages, row_width):
    depth, width = messages[0].shape
    col_width = width - row_width
    block = min(256, row_width)
    vmem = pl.BlockSpec(memory_space=pltpu.VMEM)
    return pl.pallas_call(
        functools.partial(outer_kernel, row_width, block),
        grid=(row_width // block,),
        out_shape=jax.ShapeDtypeStruct((row_width, col_width), jnp.float32),
        in_specs=[vmem] * len(messages),
        out_specs=pl.BlockSpec((block, col_width), lambda i: (i, 0)),
        scratch_shapes=[
            pltpu.VMEM((depth * len(messages), row_width), jnp.bfloat16),
            pltpu.VMEM((depth * len(messages), col_width), jnp.bfloat16),
        ],
        compiler_params=pltpu.CompilerParams(vmem_limit_bytes=40 * 2**20),
        name="outer",
    )(*messages)


def shifted(value, axis, by):
    devices = lax.axis_size(axis)
    return lax.ppermute(value, axis, [(i, (i + by) % devices) for i in range(devices)])


def swapped(value, axis):
    devices = lax.axis_size(axis)
    return lax.ppermute(value, axis, [(i, i ^ 1) for i in range(devices)])


def on_device(cond_orbitals, occ_orbitals, cond_energy, occ_energy, occ_band, sphere_index):
    rows = lax.axis_size("row")
    cols = lax.axis_size("col")
    place = jnp.stack([lax.axis_index("row"), lax.axis_index("col")]).astype(jnp.int32)
    occ_second = shifted(occ_orbitals, "row", 1)
    own = transform(cond_orbitals, occ_orbitals, occ_second, sphere_index)
    arrived = [own]
    sources = [lambda c: c]
    for k in range(1, cols // 2):
        arrived.append(shifted(own, "col", 2 * k))
        sources.append(lambda c, k=k: lax.rem(c - 2 * k + cols, cols))
    arrived += [swapped(value, "col") for value in arrived]
    sources += [lambda c, source=source: source(c ^ 1) for source in sources]
    messages = pack(arrived, sources, place, cond_energy, occ_energy, occ_band, rows, cols)
    gathered = [messages[0]] + [shifted(messages[k], "row", k) for k in range(1, rows)]
    return outer(gathered, own.shape[1] // rows)


def solution(mesh):
    placed = (P(("row", "col"), None, None), P(("row", "col"), None, None), P(), P(), P(), P())
    return jax.shard_map(
        on_device, mesh=mesh, in_specs=placed, out_specs=P("row", "col"), check_vma=False
    )
```

```python
import functools
import math

import jax
import jax.numpy as jnp
import numpy as np
from jax import lax
from jax.experimental import pallas as pl
from jax.experimental.pallas import tpu as pltpu
from jax.sharding import PartitionSpec as P

GMAX = 18
STEPS = 2
RADIX = 6
SPAN = 2 * GMAX + 1
KX_ROWS = 40
LANES = 128
OMEGA_SQUARED = 0.0625
TILE = 512
FULL_VMEM = 56 * 2**20


def split_table(table):
    upper = table.astype(jnp.bfloat16)
    lower = (table - upper.astype(np.float64)).astype(jnp.bfloat16)
    return upper, lower


def tables(grid):
    y_lo_count = grid // RADIX
    turn = 2.0 * np.pi / grid
    kx = np.arange(SPAN) - GMAX
    angle = turn * (kx[:, None] * np.arange(grid)[None, :] % grid)
    x_table = np.zeros((2 * KX_ROWS, grid))
    x_table[:SPAN] = np.cos(angle)
    x_table[KX_ROWS : KX_ROWS + SPAN] = -np.sin(angle)
    x_table = np.concatenate(split_table(x_table), axis=1)

    width = y_lo_count * grid
    y_lo = np.arange(width) // grid
    z = np.arange(width) % grid
    angle = turn * (np.arange(RADIX)[:, None] * y_lo[None, :] % grid)
    twiddle = np.concatenate([np.cos(angle), -np.sin(angle)], axis=0).astype(np.float32)

    column = np.arange((2 * GMAX // RADIX + 1) * GMAX)
    q = column // GMAX - GMAX // RADIX
    kz = column % GMAX + 1
    phase = (RADIX * q[None, :] * y_lo[:, None] + kz[None, :] * z[:, None]) % grid
    cos_part = np.zeros((width, LANES))
    sin_part = np.zeros((width, LANES))
    cos_part[:, : column.size] = np.cos(turn * phase)
    sin_part[:, : column.size] = -np.sin(turn * phase)
    last = np.block([[cos_part, sin_part], [-sin_part, cos_part]])
    upper, lower = split_table(last)
    return x_table, twiddle, upper, lower


def dft_six(re, im):
    half = 0.5
    root = math.sqrt(3.0) / 2.0
    s_re = [re[h] + re[h + 3] for h in range(3)]
    s_im = [im[h] + im[h + 3] for h in range(3)]
    d_re = [re[h] - re[h + 3] for h in range(3)]
    d_im = [im[h] - im[h + 3] for h in range(3)]
    out = [None] * 6
    sum_re, sum_im = s_re[1] + s_re[2], s_im[1] + s_im[2]
    dif_re, dif_im = (s_re[1] - s_re[2]) * root, (s_im[1] - s_im[2]) * root
    out[0] = (s_re[0] + sum_re, s_im[0] + sum_im)
    mid_re, mid_im = s_re[0] - half * sum_re, s_im[0] - half * sum_im
    out[2] = (mid_re + dif_im, mid_im - dif_re)
    out[4] = (mid_re - dif_im, mid_im + dif_re)
    sum_re, sum_im = (d_re[1] + d_re[2]) * root, (d_im[1] + d_im[2]) * root
    dif_re, dif_im = d_re[1] - d_re[2], d_im[1] - d_im[2]
    out[3] = (d_re[0] - dif_re, d_im[0] - dif_im)
    mid_re, mid_im = d_re[0] + half * dif_re, d_im[0] + half * dif_im
    out[1] = (mid_re + sum_im, mid_im - sum_re)
    out[5] = (mid_re - sum_im, mid_im + sum_re)
    return out


def dot(a, b):
    return jnp.dot(a, b, preferred_element_type=jnp.float32)


def spectrum_of(grid, cond_ref, occ_ref, x_table_ref, twiddle_ref, upper_ref, lower_ref):
    norm = np.float32(grid ** (-1.5))
    width = (grid // RADIX) * grid
    density = (cond_ref[0].astype(jnp.float32) * occ_ref[0].astype(jnp.float32)).astype(jnp.bfloat16)
    section = dot(x_table_ref[...], jnp.concatenate([density, density], axis=0))
    re = [section[:KX_ROWS, h * width : (h + 1) * width] for h in range(RADIX)]
    im = [section[KX_ROWS:, h * width : (h + 1) * width] for h in range(RADIX)]
    rows = []
    for residue, (d_re, d_im) in enumerate(dft_six(re, im)):
        if residue > 0:
            t_re = twiddle_ref[residue : residue + 1, :]
            t_im = twiddle_ref[RADIX + residue : RADIX + residue + 1, :]
            d_re, d_im = d_re * t_re - d_im * t_im, d_re * t_im + d_im * t_re
        rows.append(jnp.concatenate([d_re, d_im], axis=1))
    whole = jnp.concatenate(rows, axis=0)
    whole_hi = whole.astype(jnp.bfloat16)
    whole_lo = (whole - whole_hi.astype(jnp.float32)).astype(jnp.bfloat16)
    spectrum = dot(whole_hi, upper_ref[...]) + dot(whole_lo, upper_ref[...]) + dot(whole_hi, lower_ref[...])
    spectrum = spectrum * norm
    parts = []
    for side in range(2):
        own = spectrum[:, side * LANES : (side + 1) * LANES]
        for group in range(RADIX // 2):
            first = 2 * group * KX_ROWS
            parts.append(jnp.concatenate([own[first : first + KX_ROWS], own[first + KX_ROWS : first + 2 * KX_ROWS]], axis=1))
    return jnp.concatenate(parts, axis=0).astype(jnp.bfloat16)


def cube_places(grid, sphere):
    half = grid // 2
    sx, sy, kz = sphere[0:1], sphere[1:2], sphere[2:3]
    kx = jnp.where(sx >= half, sx - grid, sx) + GMAX
    ky = jnp.where(sy >= half, sy - grid, sy) + GMAX
    q = (ky * 43) >> 8
    residue = ky - q * RADIX
    lane = (residue & 1) * LANES + q * GMAX + kz - 1
    row = (residue >> 1) * KX_ROWS + kx
    return lane, row


def pick(cube_ref, places_ref, pair, out_ref):
    picks = RADIX // 2 * KX_ROWS
    half_count = places_ref.shape[1]
    for first in range(0, half_count, TILE):
        here = slice(first, first + TILE)
        lane, row = places_ref[0:1, here], places_ref[1:2, here]
        one_hot = (lax.broadcasted_iota(jnp.int32, (2 * LANES, TILE), 0) == lane).astype(jnp.float32).astype(jnp.bfloat16)
        chosen = lax.broadcasted_iota(jnp.int32, (picks, TILE), 0) == row
        found = dot(cube_ref[...], one_hot)
        for side in range(2):
            part = found[side * picks : (side + 1) * picks]
            value = jnp.sum(jnp.where(chosen, part, 0.0), axis=0, keepdims=True)
            out_ref[pair : pair + 1, side * half_count + first : side * half_count + first + TILE] = value.astype(jnp.bfloat16)


def own_place():
    return lax.axis_index("row"), lax.axis_index("col")


def weight_line(step, levels_ref, occ_levels_ref, bands_ref):
    rows, cols = lax.axis_size("row"), lax.axis_size("col")
    r, c = own_place()
    devices = rows * cols
    band = r * cols + c
    slot = lax.rem(band - step * cols + devices, devices)
    gap = jnp.full((1, LANES), levels_ref[band] - occ_levels_ref[bands_ref[slot]], jnp.float32)
    weight = -4.0 * gap / (gap * gap + OMEGA_SQUARED) / (devices * STEPS)
    lane = lax.broadcasted_iota(jnp.int32, weight.shape, 1)
    line = jnp.zeros_like(weight)
    for i in range(3):
        piece = weight.astype(jnp.bfloat16).astype(jnp.float32)
        line = jnp.where(lane == i, piece, line)
        weight = weight - piece
    return line.astype(jnp.bfloat16)


def start_all(sources, targets, sems):
    copies = [pltpu.make_async_copy(source, target, sems.at[i]) for i, (source, target) in enumerate(zip(sources, targets))]
    for copy in copies:
        copy.start()
    return copies


def pair_row(grid, step, copies, held, cube_ref, places_ref, out_ref):
    cond_ref, occ_ref, x_ref, twiddle_ref, upper_ref, lower_ref, vectors_ref, levels_ref, occ_levels_ref, bands_ref = held
    ready = len(copies) - 4 - step
    for copy in copies[:ready]:
        copy.wait()
    cube_ref[...] = spectrum_of(grid, cond_ref, occ_ref, x_ref, twiddle_ref, upper_ref, lower_ref)
    for copy in copies[ready:]:
        copy.wait()
    if step == 0:
        lane, row = cube_places(grid, vectors_ref[...])
        places_ref[0:1, :] = lane
        places_ref[1:2, :] = row
    else:
        places_ref = vectors_ref
    out_ref[step : step + 1, 2 * places_ref.shape[1] :] = weight_line(step, levels_ref, occ_levels_ref, bands_ref)
    pick(cube_ref, places_ref, step, out_ref)


def first_kernel(grid, *refs):
    sources, (out_ref, places_ref, *held, cube_ref, sems) = refs[:10], refs[10:]
    copies = start_all(sources, held, sems)
    pair_row(grid, 0, copies, held, cube_ref, places_ref, out_ref)


def second_kernel(grid, *refs):
    (cond_in, occ_ref, *sources), (out_ref, cond_ref, *held, first_ref, cube_ref, sems) = refs[:11], refs[11:]
    copies = start_all((cond_in, *sources), (cond_ref, *held, first_ref), sems)
    pair_row(grid, 1, copies, (cond_ref, occ_ref, *held), cube_ref, None, out_ref)
    out_ref[0:1, :] = first_ref[...]


def transform(cond_orbitals, occ_orbitals, occ_second, sphere_index, levels):
    grid = cond_orbitals.shape[1]
    tabled = [jnp.asarray(t) for t in tables(grid)]
    half_count = sphere_index.shape[1]
    width = 2 * half_count + LANES
    hbm = pl.BlockSpec(memory_space=pltpu.HBM)
    vmem = pl.BlockSpec(memory_space=pltpu.VMEM)
    places = jax.ShapeDtypeStruct((2, half_count), jnp.int32)

    def scratch(kept, more=()):
        return [
            *[pltpu.VMEM(a.shape, a.dtype) for a in kept],
            *[pltpu.SMEM(a.shape, a.dtype) for a in levels],
            *more,
            pltpu.VMEM((RADIX * KX_ROWS, 2 * LANES), jnp.bfloat16),
            pltpu.SemaphoreType.DMA((11,)),
        ]

    params = dict(
        compiler_params=pltpu.CompilerParams(vmem_limit_bytes=FULL_VMEM),
        cost_estimate=pl.CostEstimate(flops=2 * 10**9, bytes_accessed=2 * 10**6, transcendentals=0),
    )
    first_row = jax.ShapeDtypeStruct((1, width), jnp.bfloat16)
    first, places = pl.pallas_call(
        functools.partial(first_kernel, grid),
        out_shape=[first_row, places],
        in_specs=[hbm] * 10,
        out_specs=[vmem] * 2,
        scratch_shapes=scratch([cond_orbitals, occ_orbitals, *tabled, sphere_index]),
        name="first_pair",
        **params,
    )(cond_orbitals, occ_orbitals, *tabled, sphere_index, *levels)
    return pl.pallas_call(
        functools.partial(second_kernel, grid),
        out_shape=jax.ShapeDtypeStruct((STEPS, width), jnp.bfloat16),
        in_specs=[hbm, vmem] + [hbm] * 9,
        out_specs=vmem,
        scratch_shapes=scratch([cond_orbitals, *tabled, places], [pltpu.VMEM(first_row.shape, first_row.dtype)]),
        name="second_pair",
        **params,
    )(cond_orbitals, occ_second, *tabled, places, *levels, first)


def pack_kernel(rows, cols, *refs):
    arrived, outs, mixed_ref = refs[: -1 - rows], refs[-1 - rows : -1], refs[-1]
    r, c = own_place()
    entries = mixed_ref.shape[1] - LANES
    row_width, col_width = entries // rows, entries // cols
    for j, ref in enumerate(arrived):
        mixed_ref[STEPS * j : STEPS * (j + 1), :] = ref[...].astype(jnp.float32)
    weight = mixed_ref[:, entries : entries + 1]
    for i in range(1, 3):
        weight = weight + mixed_ref[:, entries + i : entries + i + 1]
    column = mixed_ref[:, pl.ds(pl.multiple_of(c * col_width, LANES), col_width)]
    column = (weight * column).astype(jnp.bfloat16)
    for k, out_ref in enumerate(outs):
        block = lax.rem(r + k, rows)
        out_ref[:, :row_width] = mixed_ref[:, pl.ds(pl.multiple_of(block * row_width, LANES), row_width)].astype(jnp.bfloat16)
        out_ref[:, row_width:] = column


def pack(arrived, rows, cols):
    entries = arrived[0].shape[1] - LANES
    pairs = STEPS * len(arrived)
    message = jax.ShapeDtypeStruct((pairs, entries // rows + entries // cols), jnp.bfloat16)
    vmem = pl.BlockSpec(memory_space=pltpu.VMEM)
    return pl.pallas_call(
        functools.partial(pack_kernel, rows, cols),
        out_shape=[message] * rows,
        in_specs=[vmem] * len(arrived),
        out_specs=[vmem] * rows,
        scratch_shapes=[pltpu.VMEM((pairs, entries + LANES), jnp.float32)],
        compiler_params=pltpu.CompilerParams(vmem_limit_bytes=30 * 2**20),
        cost_estimate=pl.CostEstimate(flops=4 * 10**9, bytes_accessed=2 * 10**6, transcendentals=0),
        name="pack",
    )(*arrived)


def outer_kernel(row_width, block, slots, *refs):
    messages, (out_ref, left_ref, right_ref, held_ref, sems) = refs[:-5], refs[-5:]
    depth = messages[0].shape[0]
    merge = max(1, 16 // depth)
    for j in range(0, len(messages), merge):
        whole = jnp.concatenate([ref[...].astype(jnp.float32) for ref in messages[j : j + merge]], axis=0).astype(jnp.bfloat16)
        left_ref[depth * j : depth * (j + merge), :] = whole[:, :row_width]
        right_ref[depth * j : depth * (j + merge), :] = whole[:, row_width:]
    count = row_width // block

    def copy_out(i, slot):
        rows = pl.ds(pl.multiple_of(i * block, block), block)
        return pltpu.make_async_copy(held_ref.at[slot], out_ref.at[rows], sems.at[slot])

    def step(i, carry):
        slot = lax.rem(i, slots)

        @pl.when(i >= slots)
        def _():
            copy_out(i - slots, slot).wait()

        here = pl.ds(pl.multiple_of(i * block, block), block)
        held_ref[slot] = lax.dot_general(
            left_ref[:, here], right_ref[...], (((0,), (0,)), ((), ())), preferred_element_type=jnp.float32
        )
        copy_out(i, slot).start()
        return carry

    lax.fori_loop(0, count, step, 0)
    for i in range(max(0, count - slots), count):
        copy_out(i, i % slots).wait()


def outer(messages, row_width):
    depth, width = messages[0].shape
    col_width = width - row_width
    block = min(256, row_width)
    slots = min(4, row_width // block)
    vmem = pl.BlockSpec(memory_space=pltpu.VMEM)
    return pl.pallas_call(
        functools.partial(outer_kernel, row_width, block, slots),
        out_shape=jax.ShapeDtypeStruct((row_width, col_width), jnp.float32),
        in_specs=[vmem] * len(messages),
        out_specs=pl.BlockSpec(memory_space=pltpu.HBM),
        scratch_shapes=[
            pltpu.VMEM((depth * len(messages), row_width), jnp.bfloat16),
            pltpu.VMEM((depth * len(messages), col_width), jnp.bfloat16),
            pltpu.VMEM((slots, block, col_width), jnp.float32),
            pltpu.SemaphoreType.DMA((slots,)),
        ],
        compiler_params=pltpu.CompilerParams(vmem_limit_bytes=30 * 2**20),
        name="outer",
    )(*messages)


def shifted(value, axis, by):
    devices = lax.axis_size(axis)
    return lax.ppermute(value, axis, [(i, (i + by) % devices) for i in range(devices)])


def swapped(value, axis):
    devices = lax.axis_size(axis)
    return lax.ppermute(value, axis, [(i, i ^ 1) for i in range(devices)])


def on_device(cond_orbitals, occ_orbitals, cond_energy, occ_energy, occ_band, sphere_index):
    rows = lax.axis_size("row")
    cols = lax.axis_size("col")
    occ_second = shifted(occ_orbitals, "row", 1)
    own = transform(cond_orbitals, occ_orbitals, occ_second, sphere_index, (cond_energy, occ_energy, occ_band))
    straight = [own] + [shifted(own, "col", 2 * k) for k in range(1, cols // 2)]
    crossed = [swapped(value, "col") for value in straight]
    gathered = []
    for arrived in (straight, crossed):
        messages = pack(arrived, rows, cols)
        gathered += [messages[0]] + [shifted(messages[k], "row", k) for k in range(1, rows)]
    return outer(gathered, 2 * sphere_index.shape[1] // rows)


def solution(mesh):
    placed = (P(("row", "col"), None, None), P(("row", "col"), None, None), P(), P(), P(), P())
    return jax.shard_map(
        on_device, mesh=mesh, in_specs=placed, out_specs=P("row", "col"), check_vma=False
    )
```

```python
import functools
import math

import jax
import jax.numpy as jnp
import ml_dtypes
import numpy as np
from jax import lax
from jax.experimental import pallas as pl
from jax.experimental.pallas import tpu as pltpu
from jax.sharding import PartitionSpec as P

GMAX = 18
STEPS = 2
RADIX = 6
SPAN = 2 * GMAX + 1
KX_ROWS = 40
LANES = 128
OMEGA_SQUARED = 0.0625
TILE = 512
VMEM_LIMIT = 40 * 2**20


def split(values, count):
    parts = []
    for _ in range(count):
        parts.append(values.astype(ml_dtypes.bfloat16))
        values = values - parts[-1].astype(np.float64)
    return parts


def table_rows(grid):
    width = (grid // RADIX) * grid
    x_first = 4 * width
    twiddle_first = x_first + 2 * KX_ROWS
    return width, x_first, twiddle_first


def packed_tables(grid):
    turn = 2.0 * np.pi / grid
    width, _, _ = table_rows(grid)
    y_lo = np.arange(width) // grid
    z = np.arange(width) % grid

    column = np.arange((2 * GMAX // RADIX + 1) * GMAX)
    q = column // GMAX - GMAX // RADIX
    kz = column % GMAX + 1
    phase = (RADIX * q[None, :] * y_lo[:, None] + kz[None, :] * z[:, None]) % grid
    last = np.zeros((2 * width, LANES))
    last[:width, : column.size] = np.cos(turn * phase)
    last[width:, : column.size] = -np.sin(turn * phase)
    pieces = split(last, 2)

    kx = np.arange(SPAN) - GMAX
    angle = turn * (kx[:, None] * np.arange(grid)[None, :] % grid)
    x_table = np.zeros((2 * KX_ROWS, grid))
    x_table[:SPAN] = np.cos(angle)
    x_table[KX_ROWS : KX_ROWS + SPAN] = -np.sin(angle)
    x_table = np.concatenate(split(x_table, 2), axis=1)
    pieces.append(np.pad(x_table, ((0, 0), (0, LANES - 2 * grid))))

    angle = turn * (np.arange(RADIX)[:, None] * y_lo[None, :] % grid)
    twiddle = np.zeros((16, width))
    twiddle[:RADIX] = np.cos(angle)
    twiddle[RADIX : 2 * RADIX] = -np.sin(angle)
    for part in split(twiddle, 3):
        pieces += [part[:, first : first + LANES] for first in range(0, width, LANES)]
    return np.concatenate(pieces, axis=0)


def dft_six(re, im):
    half = 0.5
    root = math.sqrt(3.0) / 2.0
    s_re = [re[h] + re[h + 3] for h in range(3)]
    s_im = [im[h] + im[h + 3] for h in range(3)]
    d_re = [re[h] - re[h + 3] for h in range(3)]
    d_im = [im[h] - im[h + 3] for h in range(3)]
    out = [None] * 6
    sum_re, sum_im = s_re[1] + s_re[2], s_im[1] + s_im[2]
    dif_re, dif_im = (s_re[1] - s_re[2]) * root, (s_im[1] - s_im[2]) * root
    out[0] = (s_re[0] + sum_re, s_im[0] + sum_im)
    mid_re, mid_im = s_re[0] - half * sum_re, s_im[0] - half * sum_im
    out[2] = (mid_re + dif_im, mid_im - dif_re)
    out[4] = (mid_re - dif_im, mid_im + dif_re)
    sum_re, sum_im = (d_re[1] + d_re[2]) * root, (d_im[1] + d_im[2]) * root
    dif_re, dif_im = d_re[1] - d_re[2], d_im[1] - d_im[2]
    out[3] = (d_re[0] - dif_re, d_im[0] - dif_im)
    mid_re, mid_im = d_re[0] + half * dif_re, d_im[0] + half * dif_im
    out[1] = (mid_re + sum_im, mid_im - sum_re)
    out[5] = (mid_re - sum_im, mid_im + sum_re)
    return out


def dot(a, b):
    return jnp.dot(a, b, preferred_element_type=jnp.float32)


def own_place():
    return lax.axis_index("row"), lax.axis_index("col")


def spectrum_of(grid, cond, occ, table_ref):
    norm = np.float32(grid ** (-1.5))
    width, x_first, twiddle_first = table_rows(grid)
    density = (cond.astype(jnp.float32) * occ.astype(jnp.float32)).astype(jnp.bfloat16)
    x_table = table_ref[x_first:twiddle_first, : 2 * grid]
    section = dot(x_table, jnp.concatenate([density, density], axis=0))
    re = [section[:KX_ROWS, h * width : (h + 1) * width] for h in range(RADIX)]
    im = [section[KX_ROWS:, h * width : (h + 1) * width] for h in range(RADIX)]
    chunks = width // LANES
    twiddle = 0.0
    for part in range(3):
        first = twiddle_first + 16 * chunks * part
        whole = [table_ref[first + 16 * i : first + 16 * (i + 1), :].astype(jnp.float32) for i in range(chunks)]
        twiddle = twiddle + jnp.concatenate(whole, axis=1)
    rows = []
    for residue, (d_re, d_im) in enumerate(dft_six(re, im)):
        if residue > 0:
            t_re = twiddle[residue : residue + 1, :]
            t_im = twiddle[RADIX + residue : RADIX + residue + 1, :]
            d_re, d_im = d_re * t_re - d_im * t_im, d_re * t_im + d_im * t_re
        rows.append(jnp.concatenate([d_re, d_im], axis=1))
    whole = jnp.concatenate(rows, axis=0)
    whole_hi = whole.astype(jnp.bfloat16)
    whole_lo = (whole - whole_hi.astype(jnp.float32)).astype(jnp.bfloat16)

    def rotation(first):
        cos_part = table_ref[first : first + width, :]
        sin_part = table_ref[first + width : first + 2 * width, :]
        upper = jnp.concatenate([cos_part, sin_part], axis=1)
        return jnp.concatenate([upper, jnp.concatenate([-sin_part, cos_part], axis=1)], axis=0)

    upper, lower = rotation(0), rotation(2 * width)
    spectrum = (dot(whole_hi, upper) + dot(whole_lo, upper) + dot(whole_hi, lower)) * norm
    parts = []
    for side in range(2):
        own = spectrum[:, side * LANES : (side + 1) * LANES]
        for group in range(RADIX // 2):
            first = 2 * group * KX_ROWS
            parts.append(jnp.concatenate([own[first : first + KX_ROWS], own[first + KX_ROWS : first + 2 * KX_ROWS]], axis=1))
    return jnp.concatenate(parts, axis=0).astype(jnp.bfloat16)


def pair_weight(step, levels_ref):
    rows, cols = lax.axis_size("row"), lax.axis_size("col")
    r, c = own_place()
    devices = rows * cols
    band = r * cols + c
    slot = lax.rem(band - step * cols + devices, devices)
    lane = lax.broadcasted_iota(jnp.int32, (1, levels_ref.shape[1]), 1)

    def at(line, chosen):
        return jnp.sum(jnp.where(chosen, levels_ref[line : line + 1, :], 0.0), axis=1, keepdims=True)

    occ_band = at(2, lane == slot).astype(jnp.int32)
    gap = at(0, lane == band) - at(1, lane == occ_band)
    gap = jnp.broadcast_to(gap, (1, LANES))
    return -4.0 * gap / (gap * gap + OMEGA_SQUARED) / (devices * STEPS)


def first_kernel(grid, orbitals_ref, table_ref, levels_ref, sphere_ref, cube_ref, weight_ref, places_ref, table_out):
    half = grid // 2
    sx, sy, kz = sphere_ref[0:1, :], sphere_ref[1:2, :], sphere_ref[2:3, :]
    kx = jnp.where(sx >= half, sx - grid, sx) + GMAX
    ky = jnp.where(sy >= half, sy - grid, sy) + GMAX
    q = (ky * 43) >> 8
    residue = ky - q * RADIX
    places_ref[0:1, :] = (residue & 1) * LANES + q * GMAX + kz - 1
    places_ref[1:2, :] = (residue >> 1) * KX_ROWS + kx
    table_out[...] = table_ref[...]
    cube_ref[...] = spectrum_of(grid, orbitals_ref[0], orbitals_ref[1], table_ref)
    for step in range(STEPS):
        weight_ref[step : step + 1, :] = pair_weight(step, levels_ref)


def pick(cube_ref, places_ref, coef_ref):
    groups = RADIX // 2 * KX_ROWS // 8
    half_count = places_ref.shape[1]
    counted = lax.broadcasted_iota(jnp.int32, (2 * LANES, TILE), 0).astype(jnp.float32).astype(jnp.bfloat16)
    line = lax.broadcasted_iota(jnp.int32, (8, TILE), 0)
    for first in range(0, half_count, TILE):
        here = slice(first, first + TILE)
        lane = places_ref[0:1, here].astype(jnp.float32).astype(jnp.bfloat16)
        row = places_ref[1:2, here]
        one_hot = jnp.where(counted == lane, jnp.bfloat16(1), jnp.bfloat16(0))
        found = dot(cube_ref[...], one_hot)
        away = line - row
        values = [jnp.zeros((8, TILE), jnp.float32)] * 4
        for group in range(groups):
            chosen = away == -8 * group
            for which in range(4):
                start = (which * groups + group) * 8
                values[which] = jnp.where(chosen, found[start : start + 8], values[which])
        for which in range(4):
            pair, side = divmod(which, 2)
            value = jnp.sum(values[which], axis=0, keepdims=True)
            coef_ref[pair : pair + 1, side * half_count + first : side * half_count + first + TILE] = value


def second_kernel(grid, plan, orbitals_ref, occ_ref, first_ref, weight_ref, places_ref, table_ref, *refs):
    outs, coef_ref, cube_ref = refs[:-2], refs[-2], refs[-1]
    rows, cols, groups, row_width, group_width = plan
    r, _ = own_place()
    picks = RADIX * KX_ROWS
    cube_ref[:picks, :] = first_ref[...]
    cube_ref[picks:, :] = spectrum_of(grid, orbitals_ref[0], occ_ref[0], table_ref)
    pick(cube_ref, places_ref, coef_ref)
    weight = weight_ref[:, :1]
    for k, out_ref in enumerate(outs):
        block = lax.rem(r + k, rows)
        group = lax.rem(block, groups)
        start = pl.multiple_of(block * row_width, LANES)
        out_ref[:, :row_width] = coef_ref[:, pl.ds(start, row_width)].astype(jnp.bfloat16)
        for c in range(cols):
            start = pl.multiple_of((c * groups + group) * group_width, LANES)
            part = weight * coef_ref[:, pl.ds(start, group_width)]
            out_ref[:, row_width + c * group_width : row_width + (c + 1) * group_width] = part.astype(jnp.bfloat16)


def cost(flops, data):
    return pl.CostEstimate(flops=flops, bytes_accessed=data, transcendentals=0)


def in_vmem(count):
    return [pl.BlockSpec(memory_space=pltpu.VMEM)] * count


def transform(cond_orbitals, occ_orbitals, occ_second, sphere_index, levels, plan):
    rows, cols, groups, row_width, group_width = plan
    grid = cond_orbitals.shape[1]
    table = jnp.asarray(packed_tables(grid))
    orbitals = jnp.concatenate([cond_orbitals, occ_orbitals], axis=0)
    picks = RADIX * KX_ROWS
    params = dict(
        compiler_params=pltpu.CompilerParams(vmem_limit_bytes=VMEM_LIMIT),
        cost_estimate=cost(2 * 10**9, 2 * 10**6),
    )
    handed = pl.pallas_call(
        functools.partial(first_kernel, grid),
        out_shape=[
            jax.ShapeDtypeStruct((picks, 2 * LANES), jnp.bfloat16),
            jax.ShapeDtypeStruct((STEPS, LANES), jnp.float32),
            jax.ShapeDtypeStruct((2, sphere_index.shape[1]), jnp.int32),
            jax.ShapeDtypeStruct(table.shape, table.dtype),
        ],
        in_specs=in_vmem(4),
        out_specs=in_vmem(4),
        name="first_pair",
        **params,
    )(orbitals, table, levels, sphere_index)
    message = jax.ShapeDtypeStruct((STEPS, row_width + cols * group_width), jnp.bfloat16)
    return pl.pallas_call(
        functools.partial(second_kernel, grid, plan),
        out_shape=[message] * rows,
        in_specs=in_vmem(6),
        out_specs=in_vmem(rows),
        scratch_shapes=[
            pltpu.VMEM((STEPS, 2 * sphere_index.shape[1]), jnp.float32),
            pltpu.VMEM((STEPS * picks, 2 * LANES), jnp.bfloat16),
        ],
        name="second_pair",
        **params,
    )(orbitals, occ_second, *handed)


def pack_kernel(plan, *refs):
    rows, cols, groups, row_width, group_width = plan
    arrived, outs, staged_ref, mixed_ref = refs[:rows], refs[rows:-2], refs[-2], refs[-1]
    r, c = own_place()
    for k, ref in enumerate(arrived):
        staged_ref[lax.rem(r - k + rows, rows)] = ref[...].astype(jnp.float32)
    for block in range(rows):
        mixed_ref[STEPS * block : STEPS * (block + 1), :] = staged_ref[block]
    for k, out_ref in enumerate(outs):
        out_ref[:, :row_width] = mixed_ref[:, :row_width].astype(jnp.bfloat16)
        z = lax.rem(c // 2 + k, cols // 2)
        start = pl.multiple_of(row_width + z * (2 * group_width), LANES)
        out_ref[:, row_width:] = mixed_ref[:, pl.ds(start, 2 * group_width)].astype(jnp.bfloat16)


def pack(arrived, plan):
    rows, cols, groups, row_width, group_width = plan
    message = jax.ShapeDtypeStruct((rows * STEPS, row_width + 2 * group_width), jnp.bfloat16)
    width = arrived[0].shape[1]
    return pl.pallas_call(
        functools.partial(pack_kernel, plan),
        out_shape=[message] * (cols // 2),
        in_specs=in_vmem(rows),
        out_specs=in_vmem(cols // 2),
        scratch_shapes=[pltpu.VMEM((rows, STEPS, width), jnp.float32), pltpu.VMEM((rows * STEPS, width), jnp.float32)],
        compiler_params=pltpu.CompilerParams(vmem_limit_bytes=VMEM_LIMIT),
        cost_estimate=cost(10**9, 10**6),
        name="pack",
    )(*arrived)


def stacked(refs, lanes):
    return jnp.concatenate([ref[:, lanes].astype(jnp.float32) for ref in refs], axis=0).astype(jnp.bfloat16)


def column_kernel(plan, *refs):
    rows, cols, groups, row_width, group_width = plan
    messages, out_ref = refs[:-1], refs[-1]
    _, c = own_place()
    start = pl.multiple_of(row_width + (c & 1) * group_width, LANES)
    out_ref[...] = stacked(messages, pl.ds(start, group_width))


def own_columns(messages, plan):
    rows, cols, groups, row_width, group_width = plan
    return pl.pallas_call(
        functools.partial(column_kernel, plan),
        out_shape=jax.ShapeDtypeStruct((cols * rows * STEPS, group_width), jnp.bfloat16),
        in_specs=in_vmem(cols),
        out_specs=in_vmem(1)[0],
        compiler_params=pltpu.CompilerParams(vmem_limit_bytes=VMEM_LIMIT),
        cost_estimate=cost(10**6, 10**5),
        name="own_columns",
    )(*messages)


def write_products(left_ref, right, out_ref, held_ref, sems, places, block, slots, group_width):
    count = left_ref.shape[1] // block

    def copies(i, slot):
        rows = pl.ds(pl.multiple_of(i * block, block), block)
        return [
            pltpu.make_async_copy(
                held_ref.at[slot, :, pl.ds(j * group_width, group_width)],
                out_ref.at[rows, pl.ds(place, group_width)],
                sems.at[slot, j],
            )
            for j, place in enumerate(places)
        ]

    def step(i, carry):
        slot = lax.rem(i, slots)

        @pl.when(i >= slots)
        def _():
            for copy in copies(i - slots, slot):
                copy.wait()

        here = pl.ds(pl.multiple_of(i * block, block), block)
        held_ref[slot] = lax.dot_general(left_ref[:, here], right[...], (((0,), (0,)), ((), ())), preferred_element_type=jnp.float32)
        for copy in copies(i, slot):
            copy.start()
        return carry

    lax.fori_loop(0, count, step, 0)
    for i in range(max(0, count - slots), count):
        for copy in copies(i, i % slots):
            copy.wait()


def first_outer_kernel(plan, block, slots, *refs):
    rows, cols, groups, row_width, group_width = plan
    messages, (columns_ref, out_ref, left_ref, held_ref, sems) = refs[:cols], refs[cols:]
    r, _ = own_place()
    left_ref[...] = stacked(messages, slice(0, row_width))
    place = pl.multiple_of(lax.rem(r, groups) * group_width, LANES)
    write_products(left_ref, columns_ref, out_ref, held_ref, sems, [place], block, slots, group_width)


def second_outer_kernel(plan, block, slots, *refs):
    rows, cols, groups, row_width, group_width = plan
    arrived, (left_ref, _, out_ref, right_ref, held_ref, sems) = refs[: groups - 1], refs[groups - 1 :]
    r, _ = own_place()
    places = []
    for j, ref in enumerate(arrived):
        right_ref[:, j * group_width : (j + 1) * group_width] = ref[...]
        places.append(pl.multiple_of(lax.rem(lax.rem(r, groups) - j - 1 + groups, groups) * group_width, LANES))
    write_products(left_ref, right_ref, out_ref, held_ref, sems, places, block, slots, group_width)


def outer(messages, columns, arrived, plan):
    rows, cols, groups, row_width, group_width = plan
    depth = columns.shape[0]
    hbm = pl.BlockSpec(memory_space=pltpu.HBM)
    tile = jax.ShapeDtypeStruct((row_width, groups * group_width), jnp.float32)

    def shapes(block, width, copies):
        slots = min(4, row_width // block)
        return slots, [pltpu.VMEM((slots, block, width), jnp.float32), pltpu.SemaphoreType.DMA((slots, copies))]

    block = min(512, row_width)
    slots, scratch = shapes(block, group_width, 1)
    part, left = pl.pallas_call(
        functools.partial(first_outer_kernel, plan, block, slots),
        out_shape=[tile, jax.ShapeDtypeStruct((depth, row_width), jnp.bfloat16)],
        in_specs=in_vmem(cols + 1),
        out_specs=[hbm] + in_vmem(1),
        scratch_shapes=scratch,
        compiler_params=pltpu.CompilerParams(vmem_limit_bytes=VMEM_LIMIT),
        cost_estimate=cost(4 * 10**9, 10**7),
        name="own_outer",
    )(*messages, columns)
    block = min(256, row_width)
    width = (groups - 1) * group_width
    slots, scratch = shapes(block, width, groups - 1)
    return pl.pallas_call(
        functools.partial(second_outer_kernel, plan, block, slots),
        out_shape=tile,
        in_specs=in_vmem(groups) + [hbm],
        out_specs=hbm,
        input_output_aliases={groups: 0},
        scratch_shapes=[pltpu.VMEM((depth, width), jnp.bfloat16)] + scratch,
        compiler_params=pltpu.CompilerParams(vmem_limit_bytes=VMEM_LIMIT),
        cost_estimate=cost(10**10, 3 * 10**7),
        name="other_outer",
    )(*arrived, left, part)


def shifted(value, axis, by, within=None):
    devices = lax.axis_size(axis)
    within = within or devices
    return lax.ppermute(value, axis, [(i, i // within * within + (i + by) % within) for i in range(devices)])


def swapped(value, axis):
    devices = lax.axis_size(axis)
    return lax.ppermute(value, axis, [(i, i ^ 1) for i in range(devices)])


def on_device(cond_orbitals, occ_orbitals, cond_energy, occ_energy, occ_band, sphere_index):
    rows = lax.axis_size("row")
    cols = lax.axis_size("col")
    entries = 2 * sphere_index.shape[1]
    groups = rows
    while groups > 1 and (rows % groups or entries // cols % (groups * LANES)):
        groups -= 1
    plan = (rows, cols, groups, entries // rows, entries // cols // groups)
    occ_second = shifted(occ_orbitals, "row", 1)
    levels = jnp.stack([cond_energy, occ_energy, occ_band.astype(jnp.float32)])
    sent = transform(cond_orbitals, occ_orbitals, occ_second, sphere_index, levels, plan)
    packed = pack([sent[0]] + [shifted(sent[k], "row", k) for k in range(1, rows)], plan)
    messages = [packed[0]] + [shifted(packed[k], "col", 2 * k) for k in range(1, cols // 2)]
    messages += [swapped(value, "col") for value in messages]
    columns = own_columns(messages, plan)
    arrived = [shifted(columns, "row", k, groups) for k in range(1, groups)]
    return outer(messages, columns, arrived, plan)


def solution(mesh):
    placed = (P(("row", "col"), None, None), P(("row", "col"), None, None), P(), P(), P(), P())
    return jax.shard_map(
        on_device, mesh=mesh, in_specs=placed, out_specs=P("row", "col"), check_vma=False
    )
```

```python
import functools
import math

import jax
import jax.numpy as jnp
import ml_dtypes
import numpy as np
from jax import lax
from jax.experimental import pallas as pl
from jax.experimental.pallas import tpu as pltpu
from jax.sharding import PartitionSpec as P

GMAX = 18
STEPS = 2
RADIX = 6
SPAN = 2 * GMAX + 1
KX_ROWS = 40
LANES = 128
OMEGA_SQUARED = 0.0625
TILE = 512
VMEM_LIMIT = 40 * 2**20


def split(values, count):
    parts = []
    for _ in range(count):
        parts.append(values.astype(ml_dtypes.bfloat16))
        values = values - parts[-1].astype(np.float64)
    return parts


def table_rows(grid):
    width = (grid // RADIX) * grid
    x_first = 4 * width
    twiddle_first = x_first + 2 * KX_ROWS
    return width, x_first, twiddle_first


def packed_tables(grid):
    turn = 2.0 * np.pi / grid
    width, _, _ = table_rows(grid)
    y_lo = np.arange(width) // grid
    z = np.arange(width) % grid

    column = np.arange((2 * GMAX // RADIX + 1) * GMAX)
    q = column // GMAX - GMAX // RADIX
    kz = column % GMAX + 1
    phase = (RADIX * q[None, :] * y_lo[:, None] + kz[None, :] * z[:, None]) % grid
    last = np.zeros((2 * width, LANES))
    last[:width, : column.size] = np.cos(turn * phase)
    last[width:, : column.size] = -np.sin(turn * phase)
    pieces = split(last, 2)

    kx = np.arange(SPAN) - GMAX
    angle = turn * (kx[:, None] * np.arange(grid)[None, :] % grid)
    x_table = np.zeros((2 * KX_ROWS, grid))
    x_table[:SPAN] = np.cos(angle)
    x_table[KX_ROWS : KX_ROWS + SPAN] = -np.sin(angle)
    x_table = np.concatenate(split(x_table, 2), axis=1)
    pieces.append(np.pad(x_table, ((0, 0), (0, LANES - 2 * grid))))

    angle = turn * (np.arange(RADIX)[:, None] * y_lo[None, :] % grid)
    twiddle = np.zeros((16, width))
    twiddle[:RADIX] = np.cos(angle)
    twiddle[RADIX : 2 * RADIX] = -np.sin(angle)
    for part in split(twiddle, 3):
        pieces += [part[:, first : first + LANES] for first in range(0, width, LANES)]
    return np.concatenate(pieces, axis=0)


def dft_six(re, im):
    half = 0.5
    root = math.sqrt(3.0) / 2.0
    s_re = [re[h] + re[h + 3] for h in range(3)]
    s_im = [im[h] + im[h + 3] for h in range(3)]
    d_re = [re[h] - re[h + 3] for h in range(3)]
    d_im = [im[h] - im[h + 3] for h in range(3)]
    out = [None] * 6
    sum_re, sum_im = s_re[1] + s_re[2], s_im[1] + s_im[2]
    dif_re, dif_im = (s_re[1] - s_re[2]) * root, (s_im[1] - s_im[2]) * root
    out[0] = (s_re[0] + sum_re, s_im[0] + sum_im)
    mid_re, mid_im = s_re[0] - half * sum_re, s_im[0] - half * sum_im
    out[2] = (mid_re + dif_im, mid_im - dif_re)
    out[4] = (mid_re - dif_im, mid_im + dif_re)
    sum_re, sum_im = (d_re[1] + d_re[2]) * root, (d_im[1] + d_im[2]) * root
    dif_re, dif_im = d_re[1] - d_re[2], d_im[1] - d_im[2]
    out[3] = (d_re[0] - dif_re, d_im[0] - dif_im)
    mid_re, mid_im = d_re[0] + half * dif_re, d_im[0] + half * dif_im
    out[1] = (mid_re + sum_im, mid_im - sum_re)
    out[5] = (mid_re - sum_im, mid_im + sum_re)
    return out


def dot(a, b):
    return jnp.dot(a, b, preferred_element_type=jnp.float32)


def own_place():
    return lax.axis_index("row"), lax.axis_index("col")


def spectrum_of(grid, cond, occ, table_ref):
    norm = np.float32(grid ** (-1.5))
    width, x_first, twiddle_first = table_rows(grid)
    density = (cond.astype(jnp.float32) * occ.astype(jnp.float32)).astype(jnp.bfloat16)
    x_table = table_ref[x_first:twiddle_first, : 2 * grid]
    section = dot(x_table, jnp.concatenate([density, density], axis=0))
    re = [section[:KX_ROWS, h * width : (h + 1) * width] for h in range(RADIX)]
    im = [section[KX_ROWS:, h * width : (h + 1) * width] for h in range(RADIX)]
    chunks = width // LANES
    twiddle = 0.0
    for part in range(3):
        first = twiddle_first + 16 * chunks * part
        whole = [table_ref[first + 16 * i : first + 16 * (i + 1), :].astype(jnp.float32) for i in range(chunks)]
        twiddle = twiddle + jnp.concatenate(whole, axis=1)
    rows = []
    for residue, (d_re, d_im) in enumerate(dft_six(re, im)):
        if residue > 0:
            t_re = twiddle[residue : residue + 1, :]
            t_im = twiddle[RADIX + residue : RADIX + residue + 1, :]
            d_re, d_im = d_re * t_re - d_im * t_im, d_re * t_im + d_im * t_re
        rows.append(jnp.concatenate([d_re, d_im], axis=1))
    whole = jnp.concatenate(rows, axis=0)
    whole_hi = whole.astype(jnp.bfloat16)
    whole_lo = (whole - whole_hi.astype(jnp.float32)).astype(jnp.bfloat16)

    def rotation(first):
        cos_part = table_ref[first : first + width, :]
        sin_part = table_ref[first + width : first + 2 * width, :]
        upper = jnp.concatenate([cos_part, sin_part], axis=1)
        return jnp.concatenate([upper, jnp.concatenate([-sin_part, cos_part], axis=1)], axis=0)

    upper, lower = rotation(0), rotation(2 * width)
    spectrum = (dot(whole_hi, upper) + dot(whole_lo, upper) + dot(whole_hi, lower)) * norm
    parts = []
    for side in range(2):
        own = spectrum[:, side * LANES : (side + 1) * LANES]
        for group in range(RADIX // 2):
            first = 2 * group * KX_ROWS
            parts.append(jnp.concatenate([own[first : first + KX_ROWS], own[first + KX_ROWS : first + 2 * KX_ROWS]], axis=1))
    return jnp.concatenate(parts, axis=0).astype(jnp.bfloat16)


def pair_weights(sources, levels_ref):
    rows, cols = lax.axis_size("row"), lax.axis_size("col")
    r, _ = own_place()
    devices = rows * cols
    pairs = STEPS * len(sources)
    line = lax.broadcasted_iota(jnp.int32, (pairs, 1), 0)
    band = jnp.zeros((pairs, 1), jnp.int32)
    slot = jnp.zeros((pairs, 1), jnp.int32)
    for j, source in enumerate(sources):
        place = r * cols + source
        for step in range(STEPS):
            here = line == STEPS * j + step
            band = jnp.where(here, place, band)
            slot = jnp.where(here, lax.rem(place - step * cols + devices, devices), slot)
    lane = lax.broadcasted_iota(jnp.int32, (pairs, levels_ref.shape[1]), 1)

    def at(which, chosen):
        return jnp.sum(jnp.where(lane == chosen, levels_ref[which : which + 1, :], 0.0), axis=1, keepdims=True)

    gap = at(0, band) - at(1, at(2, slot).astype(jnp.int32))
    return -4.0 * gap / (gap * gap + OMEGA_SQUARED) / (devices * STEPS)


def first_kernel(grid, orbitals_ref, table_ref, sphere_ref, cube_ref, places_ref, table_out):
    half = grid // 2
    sx, sy, kz = sphere_ref[0:1, :], sphere_ref[1:2, :], sphere_ref[2:3, :]
    kx = jnp.where(sx >= half, sx - grid, sx) + GMAX
    ky = jnp.where(sy >= half, sy - grid, sy) + GMAX
    q = (ky * 43) >> 8
    residue = ky - q * RADIX
    places_ref[0:1, :] = (residue & 1) * LANES + q * GMAX + kz - 1
    places_ref[1:2, :] = (residue >> 1) * KX_ROWS + kx
    table_out[...] = table_ref[...]
    cube_ref[...] = spectrum_of(grid, orbitals_ref[0], orbitals_ref[1], table_ref)


def pick(cube_ref, places_ref, coef_ref):
    groups = RADIX // 2 * KX_ROWS // 8
    half_count = places_ref.shape[1]
    counted = lax.broadcasted_iota(jnp.int32, (2 * LANES, TILE), 0).astype(jnp.float32).astype(jnp.bfloat16)
    line = lax.broadcasted_iota(jnp.int32, (8, TILE), 0)
    for first in range(0, half_count, TILE):
        here = slice(first, first + TILE)
        lane = places_ref[0:1, here].astype(jnp.float32).astype(jnp.bfloat16)
        row = places_ref[1:2, here]
        one_hot = jnp.where(counted == lane, jnp.bfloat16(1), jnp.bfloat16(0))
        found = dot(cube_ref[...], one_hot)
        away = line - row
        values = [jnp.zeros((8, TILE), jnp.float32)] * 4
        for group in range(groups):
            chosen = away == -8 * group
            for which in range(4):
                start = (which * groups + group) * 8
                values[which] = jnp.where(chosen, found[start : start + 8], values[which])
        for which in range(4):
            pair, side = divmod(which, 2)
            value = jnp.sum(values[which], axis=0, keepdims=True)
            coef_ref[pair : pair + 1, side * half_count + first : side * half_count + first + TILE] = value.astype(jnp.bfloat16)


def second_kernel(grid, orbitals_ref, occ_ref, first_ref, places_ref, table_ref, coef_ref, cube_ref):
    picks = RADIX * KX_ROWS
    cube_ref[:picks, :] = first_ref[...]
    cube_ref[picks:, :] = spectrum_of(grid, orbitals_ref[0], occ_ref[0], table_ref)
    pick(cube_ref, places_ref, coef_ref)


def cost(flops, data):
    return pl.CostEstimate(flops=flops, bytes_accessed=data, transcendentals=0)


def in_vmem(count):
    return [pl.BlockSpec(memory_space=pltpu.VMEM)] * count


def transform(cond_orbitals, occ_orbitals, occ_second, sphere_index):
    grid = cond_orbitals.shape[1]
    half_count = sphere_index.shape[1]
    table = jnp.asarray(packed_tables(grid))
    orbitals = jnp.concatenate([cond_orbitals, occ_orbitals], axis=0)
    picks = RADIX * KX_ROWS
    params = dict(
        compiler_params=pltpu.CompilerParams(vmem_limit_bytes=VMEM_LIMIT),
        cost_estimate=cost(2 * 10**9, 2 * 10**6),
    )
    handed = pl.pallas_call(
        functools.partial(first_kernel, grid),
        out_shape=[
            jax.ShapeDtypeStruct((picks, 2 * LANES), jnp.bfloat16),
            jax.ShapeDtypeStruct((2, half_count), jnp.int32),
            jax.ShapeDtypeStruct(table.shape, table.dtype),
        ],
        in_specs=in_vmem(3),
        out_specs=in_vmem(3),
        name="first_pair",
        **params,
    )(orbitals, table, sphere_index)
    return pl.pallas_call(
        functools.partial(second_kernel, grid),
        out_shape=jax.ShapeDtypeStruct((STEPS, 2 * half_count), jnp.bfloat16),
        in_specs=in_vmem(5),
        out_specs=in_vmem(1)[0],
        scratch_shapes=[pltpu.VMEM((STEPS * picks, 2 * LANES), jnp.bfloat16)],
        name="second_pair",
        **params,
    )(orbitals, occ_second, *handed)


def pack_kernel(plan, targets, levels_ref, *refs):
    rows, cols, row_width, col_width = plan
    arrived, outs, mixed_ref = refs[: cols // 2], refs[cols // 2 : -1], refs[-1]
    r, c = own_place()
    for j, ref in enumerate(arrived):
        mixed_ref[STEPS * j : STEPS * (j + 1), :] = ref[...].astype(jnp.float32)
    weight = pair_weights([lax.rem(c - 2 * k + cols, cols) for k in range(cols // 2)], levels_ref)
    columns = []
    for side in range(2):
        start = pl.multiple_of((c ^ side) * col_width, LANES)
        columns.append((weight * mixed_ref[:, pl.ds(start, col_width)]).astype(jnp.bfloat16))
    for (step, side), out_ref in zip(targets, outs):
        start = pl.multiple_of(lax.rem(r + step, rows) * row_width, LANES)
        out_ref[:, :row_width] = mixed_ref[:, pl.ds(start, row_width)].astype(jnp.bfloat16)
        out_ref[:, row_width:] = columns[side]


def pack(arrived, levels, targets, plan):
    rows, cols, row_width, col_width = plan
    pairs = STEPS * len(arrived)
    return pl.pallas_call(
        functools.partial(pack_kernel, plan, targets),
        out_shape=[jax.ShapeDtypeStruct((pairs, row_width + col_width), jnp.bfloat16)] * len(targets),
        in_specs=in_vmem(1 + len(arrived)),
        out_specs=in_vmem(len(targets)),
        scratch_shapes=[pltpu.VMEM((pairs, arrived[0].shape[1]), jnp.float32)],
        compiler_params=pltpu.CompilerParams(vmem_limit_bytes=VMEM_LIMIT),
        cost_estimate=cost(10**9, 10**6),
        name="pack",
    )(levels, *arrived)


def outer_kernel(row_width, block, slots, *refs):
    messages, (out_ref, left_ref, right_ref, held_ref, sems) = refs[:-5], refs[-5:]
    depth = messages[0].shape[0]
    merge = max(1, 16 // depth)
    for j in range(0, len(messages), merge):
        whole = jnp.concatenate([ref[...].astype(jnp.float32) for ref in messages[j : j + merge]], axis=0).astype(jnp.bfloat16)
        left_ref[depth * j : depth * (j + merge), :] = whole[:, :row_width]
        right_ref[depth * j : depth * (j + merge), :] = whole[:, row_width:]
    count = row_width // block

    def copy_out(i, slot):
        rows = pl.ds(pl.multiple_of(i * block, block), block)
        return pltpu.make_async_copy(held_ref.at[slot], out_ref.at[rows], sems.at[slot])

    def step(i, carry):
        slot = lax.rem(i, slots)

        @pl.when(i >= slots)
        def _():
            copy_out(i - slots, slot).wait()

        here = pl.ds(pl.multiple_of(i * block, block), block)
        held_ref[slot] = lax.dot_general(
            left_ref[:, here], right_ref[...], (((0,), (0,)), ((), ())), preferred_element_type=jnp.float32
        )
        copy_out(i, slot).start()
        return carry

    lax.fori_loop(0, count, step, 0)
    for i in range(max(0, count - slots), count):
        copy_out(i, i % slots).wait()


def outer(messages, plan):
    rows, cols, row_width, col_width = plan
    depth = messages[0].shape[0]
    block = min(256, row_width)
    slots = min(4, row_width // block)
    return pl.pallas_call(
        functools.partial(outer_kernel, row_width, block, slots),
        out_shape=jax.ShapeDtypeStruct((row_width, col_width), jnp.float32),
        in_specs=in_vmem(len(messages)),
        out_specs=pl.BlockSpec(memory_space=pltpu.HBM),
        scratch_shapes=[
            pltpu.VMEM((depth * len(messages), row_width), jnp.bfloat16),
            pltpu.VMEM((depth * len(messages), col_width), jnp.bfloat16),
            pltpu.VMEM((slots, block, col_width), jnp.float32),
            pltpu.SemaphoreType.DMA((slots,)),
        ],
        compiler_params=pltpu.CompilerParams(vmem_limit_bytes=VMEM_LIMIT),
        cost_estimate=cost(10**10, 3 * 10**7),
        name="outer",
    )(*messages)


def shifted(value, axis, by):
    devices = lax.axis_size(axis)
    return lax.ppermute(value, axis, [(i, (i + by) % devices) for i in range(devices)])


def sent_to(value, step, side, rows, cols):
    moves = [(r * cols + c, (r + step) % rows * cols + (c ^ side)) for r in range(rows) for c in range(cols)]
    return lax.ppermute(value, ("row", "col"), moves)


def on_device(cond_orbitals, occ_orbitals, cond_energy, occ_energy, occ_band, sphere_index):
    rows = lax.axis_size("row")
    cols = lax.axis_size("col")
    entries = 2 * sphere_index.shape[1]
    plan = (rows, cols, entries // rows, entries // cols)
    occ_second = shifted(occ_orbitals, "row", 1)
    levels = jnp.stack([cond_energy, occ_energy, occ_band.astype(jnp.float32)])
    own = transform(cond_orbitals, occ_orbitals, occ_second, sphere_index)
    arrived = [own] + [shifted(own, "col", 2 * k) for k in range(1, cols // 2)]
    targets = [(step, side) for step in range(rows) for side in range(2)]
    packed = pack(arrived, levels, targets, plan)
    messages = [packed[0]] + [sent_to(value, *target, rows, cols) for value, target in zip(packed[1:], targets[1:])]
    return outer(messages, plan)


def solution(mesh):
    placed = (P(("row", "col"), None, None), P(("row", "col"), None, None), P(), P(), P(), P())
    return jax.shard_map(
        on_device, mesh=mesh, in_specs=placed, out_specs=P("row", "col"), check_vma=False
    )
```

```python
import functools
import math

import jax
import jax.numpy as jnp
import ml_dtypes
import numpy as np
from jax import lax
from jax.experimental import pallas as pl
from jax.experimental.pallas import tpu as pltpu
from jax.sharding import PartitionSpec as P

GMAX = 18
STEPS = 2
RADIX = 6
SPAN = 2 * GMAX + 1
KX_ROWS = 40
LANES = 128
OMEGA_SQUARED = 0.0625
TILE = 512
VMEM_LIMIT = 40 * 2**20


def split(values, count):
    parts = []
    for _ in range(count):
        parts.append(values.astype(ml_dtypes.bfloat16))
        values = values - parts[-1].astype(np.float64)
    return parts


def table_rows(grid):
    width = (grid // RADIX) * grid
    x_first = 4 * width
    twiddle_first = x_first + 2 * KX_ROWS
    return width, x_first, twiddle_first


def packed_tables(grid):
    turn = 2.0 * np.pi / grid
    width, _, _ = table_rows(grid)
    y_lo = np.arange(width) // grid
    z = np.arange(width) % grid

    column = np.arange((2 * GMAX // RADIX + 1) * GMAX)
    q = column // GMAX - GMAX // RADIX
    kz = column % GMAX + 1
    phase = (RADIX * q[None, :] * y_lo[:, None] + kz[None, :] * z[:, None]) % grid
    last = np.zeros((2 * width, LANES))
    last[:width, : column.size] = np.cos(turn * phase)
    last[width:, : column.size] = -np.sin(turn * phase)
    pieces = split(last, 2)

    kx = np.arange(SPAN) - GMAX
    angle = turn * (kx[:, None] * np.arange(grid)[None, :] % grid)
    x_table = np.zeros((2 * KX_ROWS, grid))
    x_table[:SPAN] = np.cos(angle)
    x_table[KX_ROWS : KX_ROWS + SPAN] = -np.sin(angle)
    x_table = np.concatenate(split(x_table, 2), axis=1)
    pieces.append(np.pad(x_table, ((0, 0), (0, LANES - 2 * grid))))

    angle = turn * (np.arange(RADIX)[:, None] * y_lo[None, :] % grid)
    twiddle = np.zeros((16, width))
    twiddle[:RADIX] = np.cos(angle)
    twiddle[RADIX : 2 * RADIX] = -np.sin(angle)
    for part in split(twiddle, 3):
        pieces += [part[:, first : first + LANES] for first in range(0, width, LANES)]
    return np.concatenate(pieces, axis=0)


def dft_six(re, im):
    half = 0.5
    root = math.sqrt(3.0) / 2.0
    s_re = [re[h] + re[h + 3] for h in range(3)]
    s_im = [im[h] + im[h + 3] for h in range(3)]
    d_re = [re[h] - re[h + 3] for h in range(3)]
    d_im = [im[h] - im[h + 3] for h in range(3)]
    out = [None] * 6
    sum_re, sum_im = s_re[1] + s_re[2], s_im[1] + s_im[2]
    dif_re, dif_im = (s_re[1] - s_re[2]) * root, (s_im[1] - s_im[2]) * root
    out[0] = (s_re[0] + sum_re, s_im[0] + sum_im)
    mid_re, mid_im = s_re[0] - half * sum_re, s_im[0] - half * sum_im
    out[2] = (mid_re + dif_im, mid_im - dif_re)
    out[4] = (mid_re - dif_im, mid_im + dif_re)
    sum_re, sum_im = (d_re[1] + d_re[2]) * root, (d_im[1] + d_im[2]) * root
    dif_re, dif_im = d_re[1] - d_re[2], d_im[1] - d_im[2]
    out[3] = (d_re[0] - dif_re, d_im[0] - dif_im)
    mid_re, mid_im = d_re[0] + half * dif_re, d_im[0] + half * dif_im
    out[1] = (mid_re + sum_im, mid_im - sum_re)
    out[5] = (mid_re - sum_im, mid_im + sum_re)
    return out


def dot(a, b):
    return jnp.dot(a, b, preferred_element_type=jnp.float32)


def own_place():
    return lax.axis_index("row"), lax.axis_index("col")


def spectrum_of(grid, cond, occ, table_ref):
    norm = np.float32(grid ** (-1.5))
    width, x_first, twiddle_first = table_rows(grid)
    density = (cond.astype(jnp.float32) * occ.astype(jnp.float32)).astype(jnp.bfloat16)
    x_table = table_ref[x_first:twiddle_first, : 2 * grid]
    section = dot(x_table, jnp.concatenate([density, density], axis=0))
    re = [section[:KX_ROWS, h * width : (h + 1) * width] for h in range(RADIX)]
    im = [section[KX_ROWS:, h * width : (h + 1) * width] for h in range(RADIX)]
    chunks = width // LANES
    twiddle = 0.0
    for part in range(3):
        first = twiddle_first + 16 * chunks * part
        whole = [table_ref[first + 16 * i : first + 16 * (i + 1), :].astype(jnp.float32) for i in range(chunks)]
        twiddle = twiddle + jnp.concatenate(whole, axis=1)
    rows = []
    for residue, (d_re, d_im) in enumerate(dft_six(re, im)):
        if residue > 0:
            t_re = twiddle[residue : residue + 1, :]
            t_im = twiddle[RADIX + residue : RADIX + residue + 1, :]
            d_re, d_im = d_re * t_re - d_im * t_im, d_re * t_im + d_im * t_re
        rows.append(jnp.concatenate([d_re, d_im], axis=1))
    whole = jnp.concatenate(rows, axis=0)
    whole_hi = whole.astype(jnp.bfloat16)
    whole_lo = (whole - whole_hi.astype(jnp.float32)).astype(jnp.bfloat16)

    def rotation(first):
        cos_part = table_ref[first : first + width, :]
        sin_part = table_ref[first + width : first + 2 * width, :]
        upper = jnp.concatenate([cos_part, sin_part], axis=1)
        return jnp.concatenate([upper, jnp.concatenate([-sin_part, cos_part], axis=1)], axis=0)

    upper, lower = rotation(0), rotation(2 * width)
    spectrum = (dot(whole_hi, upper) + dot(whole_lo, upper) + dot(whole_hi, lower)) * norm
    parts = []
    for side in range(2):
        own = spectrum[:, side * LANES : (side + 1) * LANES]
        for group in range(RADIX // 2):
            first = 2 * group * KX_ROWS
            parts.append(jnp.concatenate([own[first : first + KX_ROWS], own[first + KX_ROWS : first + 2 * KX_ROWS]], axis=1))
    return jnp.concatenate(parts, axis=0).astype(jnp.bfloat16)


def pair_weights(sources, levels_ref):
    rows, cols = lax.axis_size("row"), lax.axis_size("col")
    r, _ = own_place()
    devices = rows * cols
    pairs = STEPS * len(sources)
    line = lax.broadcasted_iota(jnp.int32, (pairs, 1), 0)
    band = jnp.zeros((pairs, 1), jnp.int32)
    slot = jnp.zeros((pairs, 1), jnp.int32)
    for j, source in enumerate(sources):
        place = r * cols + source
        for step in range(STEPS):
            here = line == STEPS * j + step
            band = jnp.where(here, place, band)
            slot = jnp.where(here, lax.rem(place - step * cols + devices, devices), slot)
    lane = lax.broadcasted_iota(jnp.int32, (pairs, levels_ref.shape[1]), 1)

    def at(which, chosen):
        return jnp.sum(jnp.where(lane == chosen, levels_ref[which : which + 1, :], 0.0), axis=1, keepdims=True)

    gap = at(0, band) - at(1, at(2, slot).astype(jnp.int32))
    return -4.0 * gap / (gap * gap + OMEGA_SQUARED) / (devices * STEPS)


def first_kernel(grid, orbitals_ref, table_ref, sphere_ref, cube_ref, places_ref, table_out):
    half = grid // 2
    sx, sy, kz = sphere_ref[0:1, :], sphere_ref[1:2, :], sphere_ref[2:3, :]
    kx = jnp.where(sx >= half, sx - grid, sx) + GMAX
    ky = jnp.where(sy >= half, sy - grid, sy) + GMAX
    q = (ky * 43) >> 8
    residue = ky - q * RADIX
    places_ref[0:1, :] = (residue & 1) * LANES + q * GMAX + kz - 1
    places_ref[1:2, :] = (residue >> 1) * KX_ROWS + kx
    table_out[...] = table_ref[...]
    cube_ref[...] = spectrum_of(grid, orbitals_ref[0], orbitals_ref[1], table_ref)


def pick(cube_ref, places_ref, coef_ref):
    groups = RADIX // 2 * KX_ROWS // 8
    half_count = places_ref.shape[1]
    counted = lax.broadcasted_iota(jnp.int32, (2 * LANES, TILE), 0).astype(jnp.float32).astype(jnp.bfloat16)
    line = lax.broadcasted_iota(jnp.int32, (8, TILE), 0)
    for first in range(0, half_count, TILE):
        here = slice(first, first + TILE)
        lane = places_ref[0:1, here].astype(jnp.float32).astype(jnp.bfloat16)
        row = places_ref[1:2, here]
        one_hot = jnp.where(counted == lane, jnp.bfloat16(1), jnp.bfloat16(0))
        found = dot(cube_ref[...], one_hot)
        away = line - row
        values = [jnp.zeros((8, TILE), jnp.float32)] * 4
        for group in range(groups):
            chosen = away == -8 * group
            for which in range(4):
                start = (which * groups + group) * 8
                values[which] = jnp.where(chosen, found[start : start + 8], values[which])
        for which in range(4):
            pair, side = divmod(which, 2)
            value = jnp.sum(values[which], axis=0, keepdims=True)
            coef_ref[pair : pair + 1, side * half_count + first : side * half_count + first + TILE] = value.astype(jnp.bfloat16)


def second_kernel(grid, orbitals_ref, occ_ref, first_ref, places_ref, table_ref, coef_ref, later_ref, cube_ref):
    later_ref[...] = jnp.zeros_like(later_ref)
    picks = RADIX * KX_ROWS
    cube_ref[:picks, :] = first_ref[...]
    cube_ref[picks:, :] = spectrum_of(grid, orbitals_ref[0], occ_ref[0], table_ref)
    pick(cube_ref, places_ref, coef_ref)


def cost(flops, data):
    return pl.CostEstimate(flops=flops, bytes_accessed=data, transcendentals=0)


def in_vmem(count):
    return [pl.BlockSpec(memory_space=pltpu.VMEM)] * count


def transform(cond_orbitals, occ_orbitals, occ_second, sphere_index, band_shape):
    grid = cond_orbitals.shape[1]
    half_count = sphere_index.shape[1]
    table = jnp.asarray(packed_tables(grid))
    orbitals = jnp.concatenate([cond_orbitals, occ_orbitals], axis=0)
    picks = RADIX * KX_ROWS
    params = dict(
        compiler_params=pltpu.CompilerParams(vmem_limit_bytes=VMEM_LIMIT),
        cost_estimate=cost(2 * 10**9, 2 * 10**6),
    )
    handed = pl.pallas_call(
        functools.partial(first_kernel, grid),
        out_shape=[
            jax.ShapeDtypeStruct((picks, 2 * LANES), jnp.bfloat16),
            jax.ShapeDtypeStruct((2, half_count), jnp.int32),
            jax.ShapeDtypeStruct(table.shape, table.dtype),
        ],
        in_specs=in_vmem(3),
        out_specs=in_vmem(3),
        name="first_pair",
        **params,
    )(orbitals, table, sphere_index)
    return pl.pallas_call(
        functools.partial(second_kernel, grid),
        out_shape=[
            jax.ShapeDtypeStruct((STEPS, 2 * half_count), jnp.bfloat16),
            jax.ShapeDtypeStruct((1, *band_shape), jnp.int32),
        ],
        in_specs=in_vmem(5),
        out_specs=in_vmem(2),
        scratch_shapes=[pltpu.VMEM((STEPS * picks, 2 * LANES), jnp.bfloat16)],
        name="second_pair",
        **params,
    )(orbitals, occ_second, *handed)


def pack_kernel(plan, turns, targets, levels_ref, *refs):
    rows, cols, row_width, col_width = plan
    arrived, outs, mixed_ref = refs[: cols // 2], refs[cols // 2 : -1], refs[-1]
    r, c = own_place()
    for j, ref in enumerate(arrived):
        mixed_ref[STEPS * j : STEPS * (j + 1), :] = ref[...].astype(jnp.float32)
    weight = pair_weights([c ^ turn for turn in turns], levels_ref)
    columns = []
    for side in range(2):
        start = pl.multiple_of((c ^ side) * col_width, LANES)
        columns.append((weight * mixed_ref[:, pl.ds(start, col_width)]).astype(jnp.bfloat16))
    for (step, side), out_ref in zip(targets, outs):
        start = pl.multiple_of(lax.rem(r + step, rows) * row_width, LANES)
        out_ref[:, :row_width] = mixed_ref[:, pl.ds(start, row_width)].astype(jnp.bfloat16)
        out_ref[:, row_width:] = columns[side]


def pack(arrived, levels, turns, targets, plan):
    rows, cols, row_width, col_width = plan
    pairs = STEPS * len(arrived)
    return pl.pallas_call(
        functools.partial(pack_kernel, plan, turns, targets),
        out_shape=[jax.ShapeDtypeStruct((pairs, row_width + col_width), jnp.bfloat16)] * len(targets),
        in_specs=in_vmem(1 + len(arrived)),
        out_specs=in_vmem(len(targets)),
        scratch_shapes=[pltpu.VMEM((pairs, arrived[0].shape[1]), jnp.float32)],
        compiler_params=pltpu.CompilerParams(vmem_limit_bytes=VMEM_LIMIT),
        cost_estimate=cost(10**9, 10**6),
        name="pack",
    )(levels, *arrived)


def outer_kernel(row_width, block, slots, *refs):
    messages, (out_ref, left_ref, right_ref, held_ref, sems) = refs[:-5], refs[-5:]
    depth = messages[0].shape[0]
    merge = max(1, 16 // depth)
    for j in range(0, len(messages), merge):
        whole = jnp.concatenate([ref[...].astype(jnp.float32) for ref in messages[j : j + merge]], axis=0).astype(jnp.bfloat16)
        left_ref[depth * j : depth * (j + merge), :] = whole[:, :row_width]
        right_ref[depth * j : depth * (j + merge), :] = whole[:, row_width:]
    count = row_width // block

    def copy_out(i, slot):
        rows = pl.ds(pl.multiple_of(i * block, block), block)
        return pltpu.make_async_copy(held_ref.at[slot], out_ref.at[rows], sems.at[slot])

    def step(i, carry):
        slot = lax.rem(i, slots)

        @pl.when(i >= slots)
        def _():
            copy_out(i - slots, slot).wait()

        here = pl.ds(pl.multiple_of(i * block, block), block)
        held_ref[slot] = lax.dot_general(
            left_ref[:, here], right_ref[...], (((0,), (0,)), ((), ())), preferred_element_type=jnp.float32
        )
        copy_out(i, slot).start()
        return carry

    lax.fori_loop(0, count, step, 0)
    for i in range(max(0, count - slots), count):
        copy_out(i, i % slots).wait()


def outer(messages, plan):
    rows, cols, row_width, col_width = plan
    depth = messages[0].shape[0]
    block = min(256, row_width)
    slots = min(4, row_width // block)
    return pl.pallas_call(
        functools.partial(outer_kernel, row_width, block, slots),
        out_shape=jax.ShapeDtypeStruct((row_width, col_width), jnp.float32),
        in_specs=in_vmem(len(messages)),
        out_specs=pl.BlockSpec(memory_space=pltpu.HBM),
        scratch_shapes=[
            pltpu.VMEM((depth * len(messages), row_width), jnp.bfloat16),
            pltpu.VMEM((depth * len(messages), col_width), jnp.bfloat16),
            pltpu.VMEM((slots, block, col_width), jnp.float32),
            pltpu.SemaphoreType.DMA((slots,)),
        ],
        compiler_params=pltpu.CompilerParams(vmem_limit_bytes=VMEM_LIMIT),
        cost_estimate=cost(10**10, 3 * 10**7),
        name="outer",
    )(*messages)


def shifted(value, axis, by):
    devices = lax.axis_size(axis)
    return lax.ppermute(value, axis, [(i, (i + by) % devices) for i in range(devices)])


def turned(value, axis, turn):
    devices = lax.axis_size(axis)
    return lax.ppermute(value, axis, [(i, i ^ turn) for i in range(devices)])


def far_first(turn):
    return (-turn.bit_length(), turn)


def sent_to(value, step, side, rows, cols):
    moves = [(r * cols + c, (r + step) % rows * cols + (c ^ side)) for r in range(rows) for c in range(cols)]
    return lax.ppermute(value, ("row", "col"), moves)


def on_device(cond_orbitals, occ_orbitals, cond_energy, occ_energy, occ_band, sphere_index):
    rows = lax.axis_size("row")
    cols = lax.axis_size("col")
    entries = 2 * sphere_index.shape[1]
    plan = (rows, cols, entries // rows, entries // cols)
    occ_second = shifted(occ_orbitals, "row", 1)
    own, later = transform(cond_orbitals, occ_orbitals, occ_second, sphere_index, occ_band.shape)
    levels = jnp.stack([cond_energy, occ_energy, (occ_band + later[0]).astype(jnp.float32)])
    turns = [0] + sorted(range(2, cols, 2), key=far_first)
    arrived = [own] + [turned(own, "col", turn) for turn in turns[1:]]
    targets = [(step, side) for step in range(rows) for side in range(2)]
    packed = pack(arrived, levels, turns, targets, plan)
    messages = [packed[0]] + [sent_to(value, *target, rows, cols) for value, target in zip(packed[1:], targets[1:])]
    return outer(messages, plan)


def solution(mesh):
    placed = (P(("row", "col"), None, None), P(("row", "col"), None, None), P(), P(), P(), P())
    return jax.shard_map(
        on_device, mesh=mesh, in_specs=placed, out_specs=P("row", "col"), check_vma=False
    )
```

```python
import functools
import math

import jax
import jax.numpy as jnp
import ml_dtypes
import numpy as np
from jax import lax
from jax.experimental import pallas as pl
from jax.experimental.pallas import tpu as pltpu
from jax.sharding import PartitionSpec as P

GMAX = 18
STEPS = 2
RADIX = 6
SPAN = 2 * GMAX + 1
KX_ROWS = 40
LANES = 128
OMEGA_SQUARED = 0.0625
TILE = 512
VMEM_LIMIT = 40 * 2**20


def split(values, count):
    parts = []
    for _ in range(count):
        parts.append(values.astype(ml_dtypes.bfloat16))
        values = values - parts[-1].astype(np.float64)
    return parts


def table_rows(grid):
    width = (grid // RADIX) * grid
    x_first = 4 * width
    twiddle_first = x_first + 2 * KX_ROWS
    return width, x_first, twiddle_first


def packed_tables(grid):
    turn = 2.0 * np.pi / grid
    width, _, _ = table_rows(grid)
    y_lo = np.arange(width) // grid
    z = np.arange(width) % grid

    column = np.arange((2 * GMAX // RADIX + 1) * GMAX)
    q = column // GMAX - GMAX // RADIX
    kz = column % GMAX + 1
    phase = (RADIX * q[None, :] * y_lo[:, None] + kz[None, :] * z[:, None]) % grid
    last = np.zeros((2 * width, LANES))
    last[:width, : column.size] = np.cos(turn * phase)
    last[width:, : column.size] = -np.sin(turn * phase)
    pieces = split(last, 2)

    kx = np.arange(SPAN) - GMAX
    angle = turn * (kx[:, None] * np.arange(grid)[None, :] % grid)
    x_table = np.zeros((2 * KX_ROWS, grid))
    x_table[:SPAN] = np.cos(angle)
    x_table[KX_ROWS : KX_ROWS + SPAN] = -np.sin(angle)
    x_table = np.concatenate(split(x_table, 2), axis=1)
    pieces.append(np.pad(x_table, ((0, 0), (0, LANES - 2 * grid))))

    angle = turn * (np.arange(RADIX)[:, None] * y_lo[None, :] % grid)
    twiddle = np.zeros((16, width))
    twiddle[:RADIX] = np.cos(angle)
    twiddle[RADIX : 2 * RADIX] = -np.sin(angle)
    for part in split(twiddle, 3):
        pieces += [part[:, first : first + LANES] for first in range(0, width, LANES)]
    return np.concatenate(pieces, axis=0)


def dft_six(re, im):
    half = 0.5
    root = math.sqrt(3.0) / 2.0
    s_re = [re[h] + re[h + 3] for h in range(3)]
    s_im = [im[h] + im[h + 3] for h in range(3)]
    d_re = [re[h] - re[h + 3] for h in range(3)]
    d_im = [im[h] - im[h + 3] for h in range(3)]
    out = [None] * 6
    sum_re, sum_im = s_re[1] + s_re[2], s_im[1] + s_im[2]
    dif_re, dif_im = (s_re[1] - s_re[2]) * root, (s_im[1] - s_im[2]) * root
    out[0] = (s_re[0] + sum_re, s_im[0] + sum_im)
    mid_re, mid_im = s_re[0] - half * sum_re, s_im[0] - half * sum_im
    out[2] = (mid_re + dif_im, mid_im - dif_re)
    out[4] = (mid_re - dif_im, mid_im + dif_re)
    sum_re, sum_im = (d_re[1] + d_re[2]) * root, (d_im[1] + d_im[2]) * root
    dif_re, dif_im = d_re[1] - d_re[2], d_im[1] - d_im[2]
    out[3] = (d_re[0] - dif_re, d_im[0] - dif_im)
    mid_re, mid_im = d_re[0] + half * dif_re, d_im[0] + half * dif_im
    out[1] = (mid_re + sum_im, mid_im - sum_re)
    out[5] = (mid_re - sum_im, mid_im + sum_re)
    return out


def dot(a, b):
    return jnp.dot(a, b, preferred_element_type=jnp.float32)


def own_place():
    return lax.axis_index("row"), lax.axis_index("col")


def spectrum_of(grid, cond, occ, table_ref):
    norm = np.float32(grid ** (-1.5))
    width, x_first, twiddle_first = table_rows(grid)
    density = (cond.astype(jnp.float32) * occ.astype(jnp.float32)).astype(jnp.bfloat16)
    x_table = table_ref[x_first:twiddle_first, : 2 * grid]
    section = dot(x_table, jnp.concatenate([density, density], axis=0))
    re = [section[:KX_ROWS, h * width : (h + 1) * width] for h in range(RADIX)]
    im = [section[KX_ROWS:, h * width : (h + 1) * width] for h in range(RADIX)]
    chunks = width // LANES
    twiddle = 0.0
    for part in range(3):
        first = twiddle_first + 16 * chunks * part
        whole = [table_ref[first + 16 * i : first + 16 * (i + 1), :].astype(jnp.float32) for i in range(chunks)]
        twiddle = twiddle + jnp.concatenate(whole, axis=1)
    rows = []
    for residue, (d_re, d_im) in enumerate(dft_six(re, im)):
        if residue > 0:
            t_re = twiddle[residue : residue + 1, :]
            t_im = twiddle[RADIX + residue : RADIX + residue + 1, :]
            d_re, d_im = d_re * t_re - d_im * t_im, d_re * t_im + d_im * t_re
        rows.append(jnp.concatenate([d_re, d_im], axis=1))
    whole = jnp.concatenate(rows, axis=0)
    whole_hi = whole.astype(jnp.bfloat16)
    whole_lo = (whole - whole_hi.astype(jnp.float32)).astype(jnp.bfloat16)

    def rotation(first):
        cos_part = table_ref[first : first + width, :]
        sin_part = table_ref[first + width : first + 2 * width, :]
        upper = jnp.concatenate([cos_part, sin_part], axis=1)
        return jnp.concatenate([upper, jnp.concatenate([-sin_part, cos_part], axis=1)], axis=0)

    upper, lower = rotation(0), rotation(2 * width)
    spectrum = (dot(whole_hi, upper) + dot(whole_lo, upper) + dot(whole_hi, lower)) * norm
    parts = []
    for side in range(2):
        own = spectrum[:, side * LANES : (side + 1) * LANES]
        for group in range(RADIX // 2):
            first = 2 * group * KX_ROWS
            parts.append(jnp.concatenate([own[first : first + KX_ROWS], own[first + KX_ROWS : first + 2 * KX_ROWS]], axis=1))
    return jnp.concatenate(parts, axis=0).astype(jnp.bfloat16)


def pair_weights(sources, levels_ref):
    rows, cols = lax.axis_size("row"), lax.axis_size("col")
    r, _ = own_place()
    devices = rows * cols
    pairs = STEPS * len(sources)
    line = lax.broadcasted_iota(jnp.int32, (pairs, 1), 0)
    band = jnp.zeros((pairs, 1), jnp.int32)
    slot = jnp.zeros((pairs, 1), jnp.int32)
    for j, source in enumerate(sources):
        place = r * cols + source
        for step in range(STEPS):
            here = line == STEPS * j + step
            band = jnp.where(here, place, band)
            slot = jnp.where(here, lax.rem(place - step * cols + devices, devices), slot)
    lane = lax.broadcasted_iota(jnp.int32, (pairs, levels_ref.shape[1]), 1)

    def at(which, chosen):
        return jnp.sum(jnp.where(lane == chosen, levels_ref[which : which + 1, :], 0.0), axis=1, keepdims=True)

    gap = at(0, band) - at(1, at(2, slot).astype(jnp.int32))
    return -4.0 * gap / (gap * gap + OMEGA_SQUARED) / (devices * STEPS)


def first_kernel(grid, orbitals_ref, table_ref, sphere_ref, cube_ref, places_ref, table_out):
    half = grid // 2
    sx, sy, kz = sphere_ref[0:1, :], sphere_ref[1:2, :], sphere_ref[2:3, :]
    kx = jnp.where(sx >= half, sx - grid, sx) + GMAX
    ky = jnp.where(sy >= half, sy - grid, sy) + GMAX
    q = (ky * 43) >> 8
    residue = ky - q * RADIX
    places_ref[0:1, :] = (residue & 1) * LANES + q * GMAX + kz - 1
    places_ref[1:2, :] = (residue >> 1) * KX_ROWS + kx
    table_out[...] = table_ref[...]
    cube_ref[...] = spectrum_of(grid, orbitals_ref[0], orbitals_ref[1], table_ref)


def pick(cube_ref, places_ref, coef_ref):
    groups = RADIX // 2 * KX_ROWS // 8
    half_count = places_ref.shape[1]
    counted = lax.broadcasted_iota(jnp.int32, (2 * LANES, TILE), 0).astype(jnp.float32).astype(jnp.bfloat16)
    line = lax.broadcasted_iota(jnp.int32, (8, TILE), 0)
    for first in range(0, half_count, TILE):
        here = slice(first, first + TILE)
        lane = places_ref[0:1, here].astype(jnp.float32).astype(jnp.bfloat16)
        row = places_ref[1:2, here]
        one_hot = jnp.where(counted == lane, jnp.bfloat16(1), jnp.bfloat16(0))
        found = dot(cube_ref[...], one_hot)
        away = line - row
        values = [jnp.zeros((8, TILE), jnp.float32)] * 4
        for group in range(groups):
            chosen = away == -8 * group
            for which in range(4):
                start = (which * groups + group) * 8
                values[which] = jnp.where(chosen, found[start : start + 8], values[which])
        for which in range(4):
            pair, side = divmod(which, 2)
            value = jnp.sum(values[which], axis=0, keepdims=True)
            coef_ref[pair : pair + 1, side * half_count + first : side * half_count + first + TILE] = value.astype(jnp.bfloat16)


def second_kernel(grid, orbitals_ref, occ_ref, first_ref, places_ref, table_ref, coef_ref, later_ref, cube_ref):
    later_ref[...] = jnp.zeros_like(later_ref)
    picks = RADIX * KX_ROWS
    cube_ref[:picks, :] = first_ref[...]
    cube_ref[picks:, :] = spectrum_of(grid, orbitals_ref[0], occ_ref[0], table_ref)
    pick(cube_ref, places_ref, coef_ref)


def cost(flops, data):
    return pl.CostEstimate(flops=flops, bytes_accessed=data, transcendentals=0)


def in_vmem(count):
    return [pl.BlockSpec(memory_space=pltpu.VMEM)] * count


def transform(cond_orbitals, occ_orbitals, occ_second, sphere_index, band_shape):
    grid = cond_orbitals.shape[1]
    half_count = sphere_index.shape[1]
    table = jnp.asarray(packed_tables(grid))
    orbitals = jnp.concatenate([cond_orbitals, occ_orbitals], axis=0)
    picks = RADIX * KX_ROWS
    params = dict(
        compiler_params=pltpu.CompilerParams(vmem_limit_bytes=VMEM_LIMIT),
        cost_estimate=cost(2 * 10**9, 2 * 10**6),
    )
    handed = pl.pallas_call(
        functools.partial(first_kernel, grid),
        out_shape=[
            jax.ShapeDtypeStruct((picks, 2 * LANES), jnp.bfloat16),
            jax.ShapeDtypeStruct((2, half_count), jnp.int32),
            jax.ShapeDtypeStruct(table.shape, table.dtype),
        ],
        in_specs=in_vmem(3),
        out_specs=in_vmem(3),
        name="first_pair",
        **params,
    )(orbitals, table, sphere_index)
    return pl.pallas_call(
        functools.partial(second_kernel, grid),
        out_shape=[
            jax.ShapeDtypeStruct((STEPS, 2 * half_count), jnp.bfloat16),
            jax.ShapeDtypeStruct((1, *band_shape), jnp.int32),
        ],
        in_specs=in_vmem(5),
        out_specs=in_vmem(2),
        scratch_shapes=[pltpu.VMEM((STEPS * picks, 2 * LANES), jnp.bfloat16)],
        name="second_pair",
        **params,
    )(orbitals, occ_second, *handed)


def pack_kernel(plan, turns, targets, levels_ref, *refs):
    rows, cols, row_width, col_width = plan
    arrived, outs, mixed_ref = refs[: cols // 2], refs[cols // 2 : -1], refs[-1]
    r, c = own_place()
    for j, ref in enumerate(arrived):
        mixed_ref[STEPS * j : STEPS * (j + 1), :] = ref[...].astype(jnp.float32)
    weight = pair_weights([c ^ turn for turn in turns], levels_ref)
    columns = []
    for side in range(2):
        start = pl.multiple_of((c ^ side) * col_width, LANES)
        columns.append((weight * mixed_ref[:, pl.ds(start, col_width)]).astype(jnp.bfloat16))
    for (turn, side), out_ref in zip(targets, outs):
        start = pl.multiple_of((r ^ turn) // 2 * (2 * row_width), LANES)
        out_ref[:, : 2 * row_width] = mixed_ref[:, pl.ds(start, 2 * row_width)].astype(jnp.bfloat16)
        out_ref[:, 2 * row_width :] = columns[side]


def pack(arrived, levels, turns, targets, plan):
    rows, cols, row_width, col_width = plan
    pairs = STEPS * len(arrived)
    return pl.pallas_call(
        functools.partial(pack_kernel, plan, turns, targets),
        out_shape=[jax.ShapeDtypeStruct((pairs, 2 * row_width + col_width), jnp.bfloat16)] * len(targets),
        in_specs=in_vmem(1 + len(arrived)),
        out_specs=in_vmem(len(targets)),
        scratch_shapes=[pltpu.VMEM((pairs, arrived[0].shape[1]), jnp.float32)],
        compiler_params=pltpu.CompilerParams(vmem_limit_bytes=VMEM_LIMIT),
        cost_estimate=cost(10**9, 10**6),
        name="pack",
    )(levels, *arrived)


def stacked(refs, lanes):
    return jnp.concatenate([ref[:, lanes].astype(jnp.float32) for ref in refs], axis=0).astype(jnp.bfloat16)


def outer_kernel(row_width, block, slots, *refs):
    messages, (out_ref, left_ref, right_ref, held_ref, sems) = refs[:-5], refs[-5:]
    depth = messages[0].shape[0]
    merge = max(1, 16 // depth)
    r, _ = own_place()
    own_rows = pl.ds(pl.multiple_of((r & 1) * row_width, LANES), row_width)
    columns = slice(2 * row_width, None)
    for j in range(0, len(messages), merge):
        here = slice(depth * j, depth * (j + merge))
        left_ref[here, :] = stacked(messages[j : j + merge], own_rows)
        right_ref[here, :] = stacked(messages[j : j + merge], columns)
    count = row_width // block

    def copy_out(i, slot):
        rows = pl.ds(pl.multiple_of(i * block, block), block)
        return pltpu.make_async_copy(held_ref.at[slot], out_ref.at[rows], sems.at[slot])

    def step(i, carry):
        slot = lax.rem(i, slots)

        @pl.when(i >= slots)
        def _():
            copy_out(i - slots, slot).wait()

        here = pl.ds(pl.multiple_of(i * block, block), block)
        held_ref[slot] = lax.dot_general(
            left_ref[:, here], right_ref[...], (((0,), (0,)), ((), ())), preferred_element_type=jnp.float32
        )
        copy_out(i, slot).start()
        return carry

    lax.fori_loop(0, count, step, 0)
    for i in range(max(0, count - slots), count):
        copy_out(i, i % slots).wait()


def outer(messages, plan):
    rows, cols, row_width, col_width = plan
    depth = messages[0].shape[0]
    block = min(256, row_width)
    slots = min(4, row_width // block)
    return pl.pallas_call(
        functools.partial(outer_kernel, row_width, block, slots),
        out_shape=jax.ShapeDtypeStruct((row_width, col_width), jnp.float32),
        in_specs=in_vmem(len(messages)),
        out_specs=pl.BlockSpec(memory_space=pltpu.HBM),
        scratch_shapes=[
            pltpu.VMEM((depth * len(messages), row_width), jnp.bfloat16),
            pltpu.VMEM((depth * len(messages), col_width), jnp.bfloat16),
            pltpu.VMEM((slots, block, col_width), jnp.float32),
            pltpu.SemaphoreType.DMA((slots,)),
        ],
        compiler_params=pltpu.CompilerParams(vmem_limit_bytes=VMEM_LIMIT),
        cost_estimate=cost(10**10, 3 * 10**7),
        name="outer",
    )(*messages)


def shifted(value, axis, by):
    devices = lax.axis_size(axis)
    return lax.ppermute(value, axis, [(i, (i + by) % devices) for i in range(devices)])


def turned(value, axis, turn):
    devices = lax.axis_size(axis)
    return lax.ppermute(value, axis, [(i, i ^ turn) for i in range(devices)])


def sent_across(value, turn, side, rows, cols):
    moves = [(r * cols + c, (r ^ turn) * cols + (c ^ side)) for r in range(rows) for c in range(cols)]
    return lax.ppermute(value, ("row", "col"), moves)


def on_device(cond_orbitals, occ_orbitals, cond_energy, occ_energy, occ_band, sphere_index):
    rows = lax.axis_size("row")
    cols = lax.axis_size("col")
    entries = 2 * sphere_index.shape[1]
    plan = (rows, cols, entries // rows, entries // cols)
    occ_second = shifted(occ_orbitals, "row", 1)
    own, later = transform(cond_orbitals, occ_orbitals, occ_second, sphere_index, occ_band.shape)
    levels = jnp.stack([cond_energy, occ_energy, (occ_band + later[0]).astype(jnp.float32)])
    turns = [0, 2, *range(cols - 2, 2, -2)]
    arrived = [own] + [turned(own, "col", turn) for turn in turns[1:]]
    targets = [(turn, side) for turn in range(0, rows, 2) for side in range(2)]
    packed = list(pack(arrived, levels, turns, targets, plan))
    straight = packed[:1] + [sent_across(value, *target, rows, cols) for value, target in zip(packed[1:], targets[1:])]
    return outer(straight + [turned(value, "row", 1) for value in straight], plan)


def solution(mesh):
    placed = (P(("row", "col"), None, None), P(("row", "col"), None, None), P(), P(), P(), P())
    return jax.shard_map(
        on_device, mesh=mesh, in_specs=placed, out_specs=P("row", "col"), check_vma=False
    )
```

```python
import functools
import math

import jax
import jax.numpy as jnp
import ml_dtypes
import numpy as np
from jax import lax
from jax.experimental import pallas as pl
from jax.experimental.pallas import tpu as pltpu
from jax.sharding import PartitionSpec as P

GMAX = 18
STEPS = 2
RADIX = 6
SPAN = 2 * GMAX + 1
KX_ROWS = 40
LANES = 128
OMEGA_SQUARED = 0.0625
TILE = 512
VMEM_LIMIT = 40 * 2**20


def split(values, count):
    parts = []
    for _ in range(count):
        parts.append(values.astype(ml_dtypes.bfloat16))
        values = values - parts[-1].astype(np.float64)
    return parts


def table_rows(grid):
    width = (grid // RADIX) * grid
    x_first = 4 * width
    twiddle_first = x_first + 2 * KX_ROWS
    return width, x_first, twiddle_first


def packed_tables(grid):
    turn = 2.0 * np.pi / grid
    width, _, _ = table_rows(grid)
    y_lo = np.arange(width) // grid
    z = np.arange(width) % grid

    column = np.arange((2 * GMAX // RADIX + 1) * GMAX)
    q = column // GMAX - GMAX // RADIX
    kz = column % GMAX + 1
    phase = (RADIX * q[None, :] * y_lo[:, None] + kz[None, :] * z[:, None]) % grid
    last = np.zeros((2 * width, LANES))
    last[:width, : column.size] = np.cos(turn * phase)
    last[width:, : column.size] = -np.sin(turn * phase)
    pieces = split(last, 2)

    kx = np.arange(SPAN) - GMAX
    angle = turn * (kx[:, None] * np.arange(grid)[None, :] % grid)
    x_table = np.zeros((2 * KX_ROWS, grid))
    x_table[:SPAN] = np.cos(angle)
    x_table[KX_ROWS : KX_ROWS + SPAN] = -np.sin(angle)
    x_table = np.concatenate(split(x_table, 2), axis=1)
    pieces.append(np.pad(x_table, ((0, 0), (0, LANES - 2 * grid))))

    angle = turn * (np.arange(RADIX)[:, None] * y_lo[None, :] % grid)
    twiddle = np.zeros((16, width))
    twiddle[:RADIX] = np.cos(angle)
    twiddle[RADIX : 2 * RADIX] = -np.sin(angle)
    for part in split(twiddle, 3):
        pieces += [part[:, first : first + LANES] for first in range(0, width, LANES)]
    return np.concatenate(pieces, axis=0)


def dft_six(re, im):
    half = 0.5
    root = math.sqrt(3.0) / 2.0
    s_re = [re[h] + re[h + 3] for h in range(3)]
    s_im = [im[h] + im[h + 3] for h in range(3)]
    d_re = [re[h] - re[h + 3] for h in range(3)]
    d_im = [im[h] - im[h + 3] for h in range(3)]
    out = [None] * 6
    sum_re, sum_im = s_re[1] + s_re[2], s_im[1] + s_im[2]
    dif_re, dif_im = (s_re[1] - s_re[2]) * root, (s_im[1] - s_im[2]) * root
    out[0] = (s_re[0] + sum_re, s_im[0] + sum_im)
    mid_re, mid_im = s_re[0] - half * sum_re, s_im[0] - half * sum_im
    out[2] = (mid_re + dif_im, mid_im - dif_re)
    out[4] = (mid_re - dif_im, mid_im + dif_re)
    sum_re, sum_im = (d_re[1] + d_re[2]) * root, (d_im[1] + d_im[2]) * root
    dif_re, dif_im = d_re[1] - d_re[2], d_im[1] - d_im[2]
    out[3] = (d_re[0] - dif_re, d_im[0] - dif_im)
    mid_re, mid_im = d_re[0] + half * dif_re, d_im[0] + half * dif_im
    out[1] = (mid_re + sum_im, mid_im - sum_re)
    out[5] = (mid_re - sum_im, mid_im + sum_re)
    return out


def dot(a, b):
    return jnp.dot(a, b, preferred_element_type=jnp.float32)


def own_place():
    return lax.axis_index("row"), lax.axis_index("col")


def spectrum_of(grid, cond, occ, table_ref):
    norm = np.float32(grid ** (-1.5))
    width, x_first, twiddle_first = table_rows(grid)
    density = (cond.astype(jnp.float32) * occ.astype(jnp.float32)).astype(jnp.bfloat16)
    x_table = table_ref[x_first:twiddle_first, : 2 * grid]
    section = dot(x_table, jnp.concatenate([density, density], axis=0))
    re = [section[:KX_ROWS, h * width : (h + 1) * width] for h in range(RADIX)]
    im = [section[KX_ROWS:, h * width : (h + 1) * width] for h in range(RADIX)]
    chunks = width // LANES
    twiddle = 0.0
    for part in range(3):
        first = twiddle_first + 16 * chunks * part
        whole = [table_ref[first + 16 * i : first + 16 * (i + 1), :].astype(jnp.float32) for i in range(chunks)]
        twiddle = twiddle + jnp.concatenate(whole, axis=1)
    rows = []
    for residue, (d_re, d_im) in enumerate(dft_six(re, im)):
        if residue > 0:
            t_re = twiddle[residue : residue + 1, :]
            t_im = twiddle[RADIX + residue : RADIX + residue + 1, :]
            d_re, d_im = d_re * t_re - d_im * t_im, d_re * t_im + d_im * t_re
        rows.append(jnp.concatenate([d_re, d_im], axis=1))
    whole = jnp.concatenate(rows, axis=0)
    whole_hi = whole.astype(jnp.bfloat16)
    whole_lo = (whole - whole_hi.astype(jnp.float32)).astype(jnp.bfloat16)

    def rotation(first):
        cos_part = table_ref[first : first + width, :]
        sin_part = table_ref[first + width : first + 2 * width, :]
        upper = jnp.concatenate([cos_part, sin_part], axis=1)
        return jnp.concatenate([upper, jnp.concatenate([-sin_part, cos_part], axis=1)], axis=0)

    upper, lower = rotation(0), rotation(2 * width)
    spectrum = (dot(whole_hi, upper) + dot(whole_lo, upper) + dot(whole_hi, lower)) * norm
    parts = []
    for side in range(2):
        own = spectrum[:, side * LANES : (side + 1) * LANES]
        for group in range(RADIX // 2):
            first = 2 * group * KX_ROWS
            parts.append(jnp.concatenate([own[first : first + KX_ROWS], own[first + KX_ROWS : first + 2 * KX_ROWS]], axis=1))
    return jnp.concatenate(parts, axis=0).astype(jnp.bfloat16)


def pair_weights(sources, levels_ref):
    rows, cols = lax.axis_size("row"), lax.axis_size("col")
    r, _ = own_place()
    devices = rows * cols
    pairs = STEPS * len(sources)
    line = lax.broadcasted_iota(jnp.int32, (pairs, 1), 0)
    band = jnp.zeros((pairs, 1), jnp.int32)
    slot = jnp.zeros((pairs, 1), jnp.int32)
    for j, source in enumerate(sources):
        place = r * cols + source
        for step in range(STEPS):
            here = line == STEPS * j + step
            band = jnp.where(here, place, band)
            slot = jnp.where(here, lax.rem(place - step * cols + devices, devices), slot)
    lane = lax.broadcasted_iota(jnp.int32, (pairs, levels_ref.shape[1]), 1)

    def at(which, chosen):
        return jnp.sum(jnp.where(lane == chosen, levels_ref[which : which + 1, :], 0.0), axis=1, keepdims=True)

    gap = at(0, band) - at(1, at(2, slot).astype(jnp.int32))
    return -4.0 * gap / (gap * gap + OMEGA_SQUARED) / (devices * STEPS)


def first_kernel(grid, orbitals_ref, table_ref, sphere_ref, cube_ref, places_ref, table_out):
    half = grid // 2
    sx, sy, kz = sphere_ref[0:1, :], sphere_ref[1:2, :], sphere_ref[2:3, :]
    kx = jnp.where(sx >= half, sx - grid, sx) + GMAX
    ky = jnp.where(sy >= half, sy - grid, sy) + GMAX
    q = (ky * 43) >> 8
    residue = ky - q * RADIX
    places_ref[0:1, :] = (residue & 1) * LANES + q * GMAX + kz - 1
    places_ref[1:2, :] = (residue >> 1) * KX_ROWS + kx
    table_out[...] = table_ref[...]
    cube_ref[...] = spectrum_of(grid, orbitals_ref[0], orbitals_ref[1], table_ref)


def pick(cube_ref, places_ref, coef_ref):
    groups = RADIX // 2 * KX_ROWS // 8
    half_count = places_ref.shape[1]
    counted = lax.broadcasted_iota(jnp.int32, (2 * LANES, TILE), 0).astype(jnp.float32).astype(jnp.bfloat16)
    line = lax.broadcasted_iota(jnp.int32, (8, TILE), 0)
    for first in range(0, half_count, TILE):
        here = slice(first, first + TILE)
        lane = places_ref[0:1, here].astype(jnp.float32).astype(jnp.bfloat16)
        row = places_ref[1:2, here]
        one_hot = jnp.where(counted == lane, jnp.bfloat16(1), jnp.bfloat16(0))
        found = dot(cube_ref[...], one_hot)
        away = line - row
        values = [jnp.zeros((8, TILE), jnp.float32)] * 4
        for group in range(groups):
            chosen = away == -8 * group
            for which in range(4):
                start = (which * groups + group) * 8
                values[which] = jnp.where(chosen, found[start : start + 8], values[which])
        for which in range(4):
            pair, side = divmod(which, 2)
            value = jnp.sum(values[which], axis=0, keepdims=True)
            coef_ref[pair : pair + 1, side * half_count + first : side * half_count + first + TILE] = value.astype(jnp.bfloat16)


def second_kernel(grid, orbitals_ref, occ_ref, first_ref, places_ref, table_ref, coef_ref, later_ref, cube_ref):
    later_ref[...] = jnp.zeros_like(later_ref)
    picks = RADIX * KX_ROWS
    cube_ref[:picks, :] = first_ref[...]
    cube_ref[picks:, :] = spectrum_of(grid, orbitals_ref[0], occ_ref[0], table_ref)
    pick(cube_ref, places_ref, coef_ref)


def cost(flops, data):
    return pl.CostEstimate(flops=flops, bytes_accessed=data, transcendentals=0)


def in_vmem(count):
    return [pl.BlockSpec(memory_space=pltpu.VMEM)] * count


def transform(cond_orbitals, occ_orbitals, occ_second, sphere_index, band_shape):
    grid = cond_orbitals.shape[1]
    half_count = sphere_index.shape[1]
    table = jnp.asarray(packed_tables(grid))
    orbitals = jnp.concatenate([cond_orbitals, occ_orbitals], axis=0)
    picks = RADIX * KX_ROWS
    params = dict(
        compiler_params=pltpu.CompilerParams(vmem_limit_bytes=VMEM_LIMIT),
        cost_estimate=cost(2 * 10**9, 2 * 10**6),
    )
    handed = pl.pallas_call(
        functools.partial(first_kernel, grid),
        out_shape=[
            jax.ShapeDtypeStruct((picks, 2 * LANES), jnp.bfloat16),
            jax.ShapeDtypeStruct((2, half_count), jnp.int32),
            jax.ShapeDtypeStruct(table.shape, table.dtype),
        ],
        in_specs=in_vmem(3),
        out_specs=in_vmem(3),
        name="first_pair",
        **params,
    )(orbitals, table, sphere_index)
    return pl.pallas_call(
        functools.partial(second_kernel, grid),
        out_shape=[
            jax.ShapeDtypeStruct((STEPS, 2 * half_count), jnp.bfloat16),
            jax.ShapeDtypeStruct((1, *band_shape), jnp.int32),
        ],
        in_specs=in_vmem(5),
        out_specs=in_vmem(2),
        scratch_shapes=[pltpu.VMEM((STEPS * picks, 2 * LANES), jnp.bfloat16)],
        name="second_pair",
        **params,
    )(orbitals, occ_second, *handed)


def pack_kernel(plan, turns, targets, levels_ref, *refs):
    rows, cols, row_width, col_width = plan
    arrived, outs, mixed_ref = refs[: len(turns)], refs[len(turns) : -1], refs[-1]
    r, c = own_place()
    for j, ref in enumerate(arrived):
        mixed_ref[STEPS * j : STEPS * (j + 1), :] = ref[...].astype(jnp.float32)
    weight = pair_weights([c ^ turn for turn in turns], levels_ref)
    columns = []
    for side in range(2):
        start = pl.multiple_of((c ^ side) * col_width, LANES)
        columns.append((weight * mixed_ref[:, pl.ds(start, col_width)]).astype(jnp.bfloat16))
    for (turn, side), out_ref in zip(targets, outs):
        start = pl.multiple_of((r ^ turn) // 2 * (2 * row_width), LANES)
        out_ref[:, : 2 * row_width] = mixed_ref[:, pl.ds(start, 2 * row_width)].astype(jnp.bfloat16)
        out_ref[:, 2 * row_width :] = columns[side]


def pack(arrived, levels, turns, targets, plan):
    rows, cols, row_width, col_width = plan
    pairs = STEPS * len(arrived)
    return pl.pallas_call(
        functools.partial(pack_kernel, plan, turns, targets),
        out_shape=[jax.ShapeDtypeStruct((pairs, 2 * row_width + col_width), jnp.bfloat16)] * len(targets),
        in_specs=in_vmem(1 + len(arrived)),
        out_specs=in_vmem(len(targets)),
        scratch_shapes=[pltpu.VMEM((pairs, arrived[0].shape[1]), jnp.float32)],
        compiler_params=pltpu.CompilerParams(vmem_limit_bytes=VMEM_LIMIT),
        cost_estimate=cost(10**9, 10**6),
        name="pack",
    )(levels, *arrived)


def stacked(refs, lanes):
    return jnp.concatenate([ref[:, lanes].astype(jnp.float32) for ref in refs], axis=0).astype(jnp.bfloat16)


def outer_kernel(row_width, block, slots, *refs):
    messages, (out_ref, left_ref, right_ref, held_ref, sems) = refs[:-5], refs[-5:]
    depth = messages[0].shape[0]
    merge = max(1, 16 // depth)
    r, _ = own_place()
    own_rows = pl.ds(pl.multiple_of((r & 1) * row_width, LANES), row_width)
    columns = slice(2 * row_width, None)
    for j in range(0, len(messages), merge):
        here = slice(depth * j, depth * (j + merge))
        left_ref[here, :] = stacked(messages[j : j + merge], own_rows)
        right_ref[here, :] = stacked(messages[j : j + merge], columns)
    count = row_width // block

    def copy_out(i, slot):
        rows = pl.ds(pl.multiple_of(i * block, block), block)
        return pltpu.make_async_copy(held_ref.at[slot], out_ref.at[rows], sems.at[slot])

    def step(i, carry):
        slot = lax.rem(i, slots)

        @pl.when(i >= slots)
        def _():
            copy_out(i - slots, slot).wait()

        here = pl.ds(pl.multiple_of(i * block, block), block)
        held_ref[slot] = lax.dot_general(
            left_ref[:, here], right_ref[...], (((0,), (0,)), ((), ())), preferred_element_type=jnp.float32
        )
        copy_out(i, slot).start()
        return carry

    lax.fori_loop(0, count, step, 0)
    for i in range(max(0, count - slots), count):
        copy_out(i, i % slots).wait()


def outer(messages, plan):
    rows, cols, row_width, col_width = plan
    depth = messages[0].shape[0]
    block = min(256, row_width)
    slots = min(4, row_width // block)
    return pl.pallas_call(
        functools.partial(outer_kernel, row_width, block, slots),
        out_shape=jax.ShapeDtypeStruct((row_width, col_width), jnp.float32),
        in_specs=in_vmem(len(messages)),
        out_specs=pl.BlockSpec(memory_space=pltpu.HBM),
        scratch_shapes=[
            pltpu.VMEM((depth * len(messages), row_width), jnp.bfloat16),
            pltpu.VMEM((depth * len(messages), col_width), jnp.bfloat16),
            pltpu.VMEM((slots, block, col_width), jnp.float32),
            pltpu.SemaphoreType.DMA((slots,)),
        ],
        compiler_params=pltpu.CompilerParams(vmem_limit_bytes=VMEM_LIMIT),
        cost_estimate=cost(10**10, 3 * 10**7),
        name="outer",
    )(*messages)


def shifted(value, axis, by):
    devices = lax.axis_size(axis)
    return lax.ppermute(value, axis, [(i, (i + by) % devices) for i in range(devices)])


def turned(value, axis, turn):
    devices = lax.axis_size(axis)
    return lax.ppermute(value, axis, [(i, i ^ turn) for i in range(devices)])


def sent_across(value, turn, side, rows, cols):
    moves = [(r * cols + c, (r ^ turn) * cols + (c ^ side)) for r in range(rows) for c in range(cols)]
    return lax.ppermute(value, ("row", "col"), moves)


def on_device(cond_orbitals, occ_orbitals, cond_energy, occ_energy, occ_band, sphere_index):
    rows = lax.axis_size("row")
    cols = lax.axis_size("col")
    entries = 2 * sphere_index.shape[1]
    plan = (rows, cols, entries // rows, entries // cols)
    occ_second = shifted(occ_orbitals, "row", 1)
    own, later = transform(cond_orbitals, occ_orbitals, occ_second, sphere_index, occ_band.shape)
    levels = jnp.stack([cond_energy, occ_energy, (occ_band + later[0]).astype(jnp.float32)])
    arrived = {turn: turned(own, "col", turn) if turn else own for turn in range(0, cols, 2)}
    targets = [(turn, side) for turn in range(0, rows, 2) for side in range(2)]
    messages = []
    for turns in (range(0, cols // 2, 2), range(cols // 2, cols, 2)):
        packed = list(pack([arrived[turn] for turn in turns], levels, turns, targets, plan))
        straight = packed[:1] + [sent_across(value, *target, rows, cols) for value, target in zip(packed[1:], targets[1:])]
        messages += straight + [turned(value, "row", 1) for value in straight]
    return outer(messages, plan)


def solution(mesh):
    placed = (P(("row", "col"), None, None), P(("row", "col"), None, None), P(), P(), P(), P())
    return jax.shard_map(
        on_device, mesh=mesh, in_specs=placed, out_specs=P("row", "col"), check_vma=False
    )
```

```python
import functools
import math

import jax
import jax.numpy as jnp
import ml_dtypes
import numpy as np
from jax import lax
from jax.experimental import pallas as pl
from jax.experimental.pallas import tpu as pltpu
from jax.sharding import PartitionSpec as P

GMAX = 18
STEPS = 2
RADIX = 6
SPAN = 2 * GMAX + 1
KX_ROWS = 40
LANES = 128
OMEGA_SQUARED = 0.0625
TILE = 512
VMEM_LIMIT = 40 * 2**20


def split(values, count):
    parts = []
    for _ in range(count):
        parts.append(values.astype(ml_dtypes.bfloat16))
        values = values - parts[-1].astype(np.float64)
    return parts


def table_rows(grid):
    width = (grid // RADIX) * grid
    x_first = 4 * width
    twiddle_first = x_first + 2 * KX_ROWS
    return width, x_first, twiddle_first


def packed_tables(grid):
    turn = 2.0 * np.pi / grid
    width, _, _ = table_rows(grid)
    y_lo = np.arange(width) // grid
    z = np.arange(width) % grid

    column = np.arange((2 * GMAX // RADIX + 1) * GMAX)
    q = column // GMAX - GMAX // RADIX
    kz = column % GMAX + 1
    phase = (RADIX * q[None, :] * y_lo[:, None] + kz[None, :] * z[:, None]) % grid
    last = np.zeros((2 * width, LANES))
    last[:width, : column.size] = np.cos(turn * phase)
    last[width:, : column.size] = -np.sin(turn * phase)
    pieces = split(last, 2)

    kx = np.arange(SPAN) - GMAX
    angle = turn * (kx[:, None] * np.arange(grid)[None, :] % grid)
    x_table = np.zeros((2 * KX_ROWS, grid))
    x_table[:SPAN] = np.cos(angle)
    x_table[KX_ROWS : KX_ROWS + SPAN] = -np.sin(angle)
    x_table = np.concatenate(split(x_table, 2), axis=1)
    pieces.append(np.pad(x_table, ((0, 0), (0, LANES - 2 * grid))))

    angle = turn * (np.arange(RADIX)[:, None] * y_lo[None, :] % grid)
    twiddle = np.zeros((16, width))
    twiddle[:RADIX] = np.cos(angle)
    twiddle[RADIX : 2 * RADIX] = -np.sin(angle)
    for part in split(twiddle, 3):
        pieces += [part[:, first : first + LANES] for first in range(0, width, LANES)]
    return np.concatenate(pieces, axis=0)


def dft_six(re, im):
    half = 0.5
    root = math.sqrt(3.0) / 2.0
    s_re = [re[h] + re[h + 3] for h in range(3)]
    s_im = [im[h] + im[h + 3] for h in range(3)]
    d_re = [re[h] - re[h + 3] for h in range(3)]
    d_im = [im[h] - im[h + 3] for h in range(3)]
    out = [None] * 6
    sum_re, sum_im = s_re[1] + s_re[2], s_im[1] + s_im[2]
    dif_re, dif_im = (s_re[1] - s_re[2]) * root, (s_im[1] - s_im[2]) * root
    out[0] = (s_re[0] + sum_re, s_im[0] + sum_im)
    mid_re, mid_im = s_re[0] - half * sum_re, s_im[0] - half * sum_im
    out[2] = (mid_re + dif_im, mid_im - dif_re)
    out[4] = (mid_re - dif_im, mid_im + dif_re)
    sum_re, sum_im = (d_re[1] + d_re[2]) * root, (d_im[1] + d_im[2]) * root
    dif_re, dif_im = d_re[1] - d_re[2], d_im[1] - d_im[2]
    out[3] = (d_re[0] - dif_re, d_im[0] - dif_im)
    mid_re, mid_im = d_re[0] + half * dif_re, d_im[0] + half * dif_im
    out[1] = (mid_re + sum_im, mid_im - sum_re)
    out[5] = (mid_re - sum_im, mid_im + sum_re)
    return out


def dot(a, b):
    return jnp.dot(a, b, preferred_element_type=jnp.float32)


def own_place():
    return lax.axis_index("row"), lax.axis_index("col")


def spectrum_of(grid, cond, occ, table_ref):
    norm = np.float32(grid ** (-1.5))
    width, x_first, twiddle_first = table_rows(grid)
    density = (cond.astype(jnp.float32) * occ.astype(jnp.float32)).astype(jnp.bfloat16)
    x_table = table_ref[x_first:twiddle_first, : 2 * grid]
    section = dot(x_table, jnp.concatenate([density, density], axis=0))
    re = [section[:KX_ROWS, h * width : (h + 1) * width] for h in range(RADIX)]
    im = [section[KX_ROWS:, h * width : (h + 1) * width] for h in range(RADIX)]
    chunks = width // LANES
    twiddle = 0.0
    for part in range(3):
        first = twiddle_first + 16 * chunks * part
        whole = [table_ref[first + 16 * i : first + 16 * (i + 1), :].astype(jnp.float32) for i in range(chunks)]
        twiddle = twiddle + jnp.concatenate(whole, axis=1)
    rows = []
    for residue, (d_re, d_im) in enumerate(dft_six(re, im)):
        if residue > 0:
            t_re = twiddle[residue : residue + 1, :]
            t_im = twiddle[RADIX + residue : RADIX + residue + 1, :]
            d_re, d_im = d_re * t_re - d_im * t_im, d_re * t_im + d_im * t_re
        rows.append(jnp.concatenate([d_re, d_im], axis=1))
    whole = jnp.concatenate(rows, axis=0)
    whole_hi = whole.astype(jnp.bfloat16)
    whole_lo = (whole - whole_hi.astype(jnp.float32)).astype(jnp.bfloat16)

    def rotation(first):
        cos_part = table_ref[first : first + width, :]
        sin_part = table_ref[first + width : first + 2 * width, :]
        upper = jnp.concatenate([cos_part, sin_part], axis=1)
        return jnp.concatenate([upper, jnp.concatenate([-sin_part, cos_part], axis=1)], axis=0)

    upper, lower = rotation(0), rotation(2 * width)
    spectrum = (dot(whole_hi, upper) + dot(whole_lo, upper) + dot(whole_hi, lower)) * norm
    parts = []
    for side in range(2):
        own = spectrum[:, side * LANES : (side + 1) * LANES]
        for group in range(RADIX // 2):
            first = 2 * group * KX_ROWS
            parts.append(jnp.concatenate([own[first : first + KX_ROWS], own[first + KX_ROWS : first + 2 * KX_ROWS]], axis=1))
    return jnp.concatenate(parts, axis=0).astype(jnp.bfloat16)


def pair_weights(sources, levels_ref):
    rows, cols = lax.axis_size("row"), lax.axis_size("col")
    r, _ = own_place()
    devices = rows * cols
    pairs = STEPS * len(sources)
    line = lax.broadcasted_iota(jnp.int32, (pairs, 1), 0)
    band = jnp.zeros((pairs, 1), jnp.int32)
    slot = jnp.zeros((pairs, 1), jnp.int32)
    for j, source in enumerate(sources):
        place = r * cols + source
        for step in range(STEPS):
            here = line == STEPS * j + step
            band = jnp.where(here, place, band)
            slot = jnp.where(here, lax.rem(place - step * cols + devices, devices), slot)
    lane = lax.broadcasted_iota(jnp.int32, (pairs, levels_ref.shape[1]), 1)

    def at(which, chosen):
        return jnp.sum(jnp.where(lane == chosen, levels_ref[which : which + 1, :], 0.0), axis=1, keepdims=True)

    gap = at(0, band) - at(1, at(2, slot).astype(jnp.int32))
    return -4.0 * gap / (gap * gap + OMEGA_SQUARED) / (devices * STEPS)


def first_kernel(grid, orbitals_ref, table_ref, sphere_ref, cube_ref, places_ref, table_out):
    half = grid // 2
    sx, sy, kz = sphere_ref[0:1, :], sphere_ref[1:2, :], sphere_ref[2:3, :]
    kx = jnp.where(sx >= half, sx - grid, sx) + GMAX
    ky = jnp.where(sy >= half, sy - grid, sy) + GMAX
    q = (ky * 43) >> 8
    residue = ky - q * RADIX
    places_ref[0:1, :] = (residue & 1) * LANES + q * GMAX + kz - 1
    places_ref[1:2, :] = (residue >> 1) * KX_ROWS + kx
    table_out[...] = table_ref[...]
    cube_ref[...] = spectrum_of(grid, orbitals_ref[0], orbitals_ref[1], table_ref)


def pick(cube_ref, places_ref, coef_ref):
    groups = RADIX // 2 * KX_ROWS // 8
    half_count = places_ref.shape[1]
    counted = lax.broadcasted_iota(jnp.int32, (2 * LANES, TILE), 0).astype(jnp.float32).astype(jnp.bfloat16)
    line = lax.broadcasted_iota(jnp.int32, (8, TILE), 0)
    for first in range(0, half_count, TILE):
        here = slice(first, first + TILE)
        lane = places_ref[0:1, here].astype(jnp.float32).astype(jnp.bfloat16)
        row = places_ref[1:2, here]
        one_hot = jnp.where(counted == lane, jnp.bfloat16(1), jnp.bfloat16(0))
        found = dot(cube_ref[...], one_hot)
        away = line - row
        values = [jnp.zeros((8, TILE), jnp.float32)] * 4
        for group in range(groups):
            chosen = away == -8 * group
            for which in range(4):
                start = (which * groups + group) * 8
                values[which] = jnp.where(chosen, found[start : start + 8], values[which])
        for which in range(4):
            pair, side = divmod(which, 2)
            value = jnp.sum(values[which], axis=0, keepdims=True)
            coef_ref[pair : pair + 1, side * half_count + first : side * half_count + first + TILE] = value.astype(jnp.bfloat16)


def second_kernel(grid, orbitals_ref, occ_ref, first_ref, places_ref, table_ref, coef_ref, later_ref, cube_ref):
    later_ref[...] = jnp.zeros_like(later_ref)
    picks = RADIX * KX_ROWS
    cube_ref[:picks, :] = first_ref[...]
    cube_ref[picks:, :] = spectrum_of(grid, orbitals_ref[0], occ_ref[0], table_ref)
    pick(cube_ref, places_ref, coef_ref)


def cost(flops, data):
    return pl.CostEstimate(flops=flops, bytes_accessed=data, transcendentals=0)


def in_vmem(count):
    return [pl.BlockSpec(memory_space=pltpu.VMEM)] * count


def transform(cond_orbitals, occ_orbitals, occ_second, sphere_index, band_shape):
    grid = cond_orbitals.shape[1]
    half_count = sphere_index.shape[1]
    table = jnp.asarray(packed_tables(grid))
    orbitals = jnp.concatenate([cond_orbitals, occ_orbitals], axis=0)
    picks = RADIX * KX_ROWS
    params = dict(
        compiler_params=pltpu.CompilerParams(vmem_limit_bytes=VMEM_LIMIT),
        cost_estimate=cost(2 * 10**9, 2 * 10**6),
    )
    handed = pl.pallas_call(
        functools.partial(first_kernel, grid),
        out_shape=[
            jax.ShapeDtypeStruct((picks, 2 * LANES), jnp.bfloat16),
            jax.ShapeDtypeStruct((2, half_count), jnp.int32),
            jax.ShapeDtypeStruct(table.shape, table.dtype),
        ],
        in_specs=in_vmem(3),
        out_specs=in_vmem(3),
        name="first_pair",
        **params,
    )(orbitals, table, sphere_index)
    return pl.pallas_call(
        functools.partial(second_kernel, grid),
        out_shape=[
            jax.ShapeDtypeStruct((STEPS, 2 * half_count), jnp.bfloat16),
            jax.ShapeDtypeStruct((1, *band_shape), jnp.int32),
        ],
        in_specs=in_vmem(5),
        out_specs=in_vmem(2),
        scratch_shapes=[pltpu.VMEM((STEPS * picks, 2 * LANES), jnp.bfloat16)],
        name="second_pair",
        **params,
    )(orbitals, occ_second, *handed)


def pack_kernel(plan, turns, targets, merged, levels_ref, *refs):
    rows, cols, row_width, col_width = plan
    count = len(refs) - len(targets) - 1 - merged
    arrived, outs, mixed_ref = refs[:count], refs[count:-1], refs[-1]
    r, c = own_place()
    first = 0
    for ref in arrived:
        mixed_ref[first : first + ref.shape[0], :] = ref[...].astype(jnp.float32)
        first += ref.shape[0]
    if merged:
        outs[-1][...] = mixed_ref[...].astype(jnp.bfloat16)
    weight = pair_weights([c ^ turn for turn in turns], levels_ref)
    columns = []
    for side in range(2):
        start = pl.multiple_of((c ^ side) * col_width, LANES)
        columns.append((weight * mixed_ref[:, pl.ds(start, col_width)]).astype(jnp.bfloat16))
    for (turn, side), out_ref in zip(targets, outs):
        start = pl.multiple_of((r ^ turn) // 2 * (2 * row_width), LANES)
        out_ref[:, : 2 * row_width] = mixed_ref[:, pl.ds(start, 2 * row_width)].astype(jnp.bfloat16)
        out_ref[:, 2 * row_width :] = columns[side]


def pack(arrived, levels, turns, targets, merged, plan):
    rows, cols, row_width, col_width = plan
    pairs = STEPS * len(turns)
    entries = arrived[0].shape[1]
    shapes = [(pairs, 2 * row_width + col_width)] * len(targets) + [(pairs, entries)] * merged
    return pl.pallas_call(
        functools.partial(pack_kernel, plan, turns, targets, merged),
        out_shape=[jax.ShapeDtypeStruct(shape, jnp.bfloat16) for shape in shapes],
        in_specs=in_vmem(1 + len(arrived)),
        out_specs=in_vmem(len(shapes)),
        scratch_shapes=[pltpu.VMEM((pairs, entries), jnp.float32)],
        compiler_params=pltpu.CompilerParams(vmem_limit_bytes=VMEM_LIMIT),
        cost_estimate=cost(10**9, 10**6),
        name="pack",
    )(levels, *arrived)


def stacked(refs, lanes):
    return jnp.concatenate([ref[:, lanes].astype(jnp.float32) for ref in refs], axis=0).astype(jnp.bfloat16)


def outer_kernel(row_width, block, slots, *refs):
    messages, (out_ref, left_ref, right_ref, held_ref, sems) = refs[:-5], refs[-5:]
    depth = messages[0].shape[0]
    merge = max(1, 16 // depth)
    r, _ = own_place()
    own_rows = pl.ds(pl.multiple_of((r & 1) * row_width, LANES), row_width)
    columns = slice(2 * row_width, None)
    for j in range(0, len(messages), merge):
        here = slice(depth * j, depth * (j + merge))
        left_ref[here, :] = stacked(messages[j : j + merge], own_rows)
        right_ref[here, :] = stacked(messages[j : j + merge], columns)
    count = row_width // block

    def copy_out(i, slot):
        rows = pl.ds(pl.multiple_of(i * block, block), block)
        return pltpu.make_async_copy(held_ref.at[slot], out_ref.at[rows], sems.at[slot])

    def step(i, carry):
        slot = lax.rem(i, slots)

        @pl.when(i >= slots)
        def _():
            copy_out(i - slots, slot).wait()

        here = pl.ds(pl.multiple_of(i * block, block), block)
        held_ref[slot] = lax.dot_general(
            left_ref[:, here], right_ref[...], (((0,), (0,)), ((), ())), preferred_element_type=jnp.float32
        )
        copy_out(i, slot).start()
        return carry

    lax.fori_loop(0, count, step, 0)
    for i in range(max(0, count - slots), count):
        copy_out(i, i % slots).wait()


def outer(messages, plan):
    rows, cols, row_width, col_width = plan
    depth = messages[0].shape[0]
    block = min(256, row_width)
    slots = min(4, row_width // block)
    return pl.pallas_call(
        functools.partial(outer_kernel, row_width, block, slots),
        out_shape=jax.ShapeDtypeStruct((row_width, col_width), jnp.float32),
        in_specs=in_vmem(len(messages)),
        out_specs=pl.BlockSpec(memory_space=pltpu.HBM),
        scratch_shapes=[
            pltpu.VMEM((depth * len(messages), row_width), jnp.bfloat16),
            pltpu.VMEM((depth * len(messages), col_width), jnp.bfloat16),
            pltpu.VMEM((slots, block, col_width), jnp.float32),
            pltpu.SemaphoreType.DMA((slots,)),
        ],
        compiler_params=pltpu.CompilerParams(vmem_limit_bytes=VMEM_LIMIT),
        cost_estimate=cost(10**10, 3 * 10**7),
        name="outer",
    )(*messages)


def shifted(value, axis, by):
    devices = lax.axis_size(axis)
    return lax.ppermute(value, axis, [(i, (i + by) % devices) for i in range(devices)])


def turned(value, axis, turn):
    devices = lax.axis_size(axis)
    return lax.ppermute(value, axis, [(i, i ^ turn) for i in range(devices)])


def sent_across(value, turn, side, rows, cols):
    moves = [(r * cols + c, (r ^ turn) * cols + (c ^ side)) for r in range(rows) for c in range(cols)]
    return lax.ppermute(value, ("row", "col"), moves)


def on_device(cond_orbitals, occ_orbitals, cond_energy, occ_energy, occ_band, sphere_index):
    rows = lax.axis_size("row")
    cols = lax.axis_size("col")
    entries = 2 * sphere_index.shape[1]
    plan = (rows, cols, entries // rows, entries // cols)
    occ_second = shifted(occ_orbitals, "row", 1)
    own, later = transform(cond_orbitals, occ_orbitals, occ_second, sphere_index, occ_band.shape)
    levels = jnp.stack([cond_energy, occ_energy, (occ_band + later[0]).astype(jnp.float32)])
    targets = [(turn, side) for turn in range(0, rows, 2) for side in range(2)]

    def sent(packed):
        straight = [packed[0]] + [sent_across(value, *target, rows, cols) for value, target in zip(packed[1:], targets[1:])]
        return straight + [turned(value, "row", 1) for value in straight]

    held, turns, bit = [own], [0], cols // 2
    while bit > 2:
        if len(held) > 1:
            held = [jnp.concatenate(held, axis=0)]
        held.append(turned(held[0], "col", bit))
        turns += [turn + bit for turn in turns]
        bit //= 2
    *packed, merged = pack(held, levels, turns, targets, 1, plan)
    messages = sent(packed)
    far = turned(merged, "col", bit)
    messages += sent(pack([far], levels, [turn + bit for turn in turns], targets, 0, plan))
    return outer(messages, plan)


def solution(mesh):
    placed = (P(("row", "col"), None, None), P(("row", "col"), None, None), P(), P(), P(), P())
    return jax.shard_map(
        on_device, mesh=mesh, in_specs=placed, out_specs=P("row", "col"), check_vma=False
    )
```

```python
import functools
import math

import jax
import jax.numpy as jnp
import ml_dtypes
import numpy as np
from jax import lax
from jax.experimental import pallas as pl
from jax.experimental.pallas import tpu as pltpu
from jax.sharding import PartitionSpec as P

GMAX = 18
STEPS = 2
RADIX = 6
SPAN = 2 * GMAX + 1
KX_ROWS = 40
LANES = 128
OMEGA_SQUARED = 0.0625
TILE = 512
VMEM_LIMIT = 40 * 2**20


def split(values, count):
    parts = []
    for _ in range(count):
        parts.append(values.astype(ml_dtypes.bfloat16))
        values = values - parts[-1].astype(np.float64)
    return parts


def table_rows(grid):
    width = (grid // RADIX) * grid
    x_first = 4 * width
    twiddle_first = x_first + 2 * KX_ROWS
    return width, x_first, twiddle_first


def packed_tables(grid):
    turn = 2.0 * np.pi / grid
    width, _, _ = table_rows(grid)
    y_lo = np.arange(width) // grid
    z = np.arange(width) % grid

    column = np.arange((2 * GMAX // RADIX + 1) * GMAX)
    q = column // GMAX - GMAX // RADIX
    kz = column % GMAX + 1
    phase = (RADIX * q[None, :] * y_lo[:, None] + kz[None, :] * z[:, None]) % grid
    last = np.zeros((2 * width, LANES))
    last[:width, : column.size] = np.cos(turn * phase)
    last[width:, : column.size] = -np.sin(turn * phase)
    pieces = split(last, 2)

    kx = np.arange(SPAN) - GMAX
    angle = turn * (kx[:, None] * np.arange(grid)[None, :] % grid)
    x_table = np.zeros((2 * KX_ROWS, grid))
    x_table[:SPAN] = np.cos(angle)
    x_table[KX_ROWS : KX_ROWS + SPAN] = -np.sin(angle)
    x_table = np.concatenate(split(x_table, 2), axis=1)
    pieces.append(np.pad(x_table, ((0, 0), (0, LANES - 2 * grid))))

    angle = turn * (np.arange(RADIX)[:, None] * y_lo[None, :] % grid)
    twiddle = np.zeros((16, width))
    twiddle[:RADIX] = np.cos(angle)
    twiddle[RADIX : 2 * RADIX] = -np.sin(angle)
    for part in split(twiddle, 3):
        pieces += [part[:, first : first + LANES] for first in range(0, width, LANES)]
    return np.concatenate(pieces, axis=0)


def dft_six(re, im):
    half = 0.5
    root = math.sqrt(3.0) / 2.0
    s_re = [re[h] + re[h + 3] for h in range(3)]
    s_im = [im[h] + im[h + 3] for h in range(3)]
    d_re = [re[h] - re[h + 3] for h in range(3)]
    d_im = [im[h] - im[h + 3] for h in range(3)]
    out = [None] * 6
    sum_re, sum_im = s_re[1] + s_re[2], s_im[1] + s_im[2]
    dif_re, dif_im = (s_re[1] - s_re[2]) * root, (s_im[1] - s_im[2]) * root
    out[0] = (s_re[0] + sum_re, s_im[0] + sum_im)
    mid_re, mid_im = s_re[0] - half * sum_re, s_im[0] - half * sum_im
    out[2] = (mid_re + dif_im, mid_im - dif_re)
    out[4] = (mid_re - dif_im, mid_im + dif_re)
    sum_re, sum_im = (d_re[1] + d_re[2]) * root, (d_im[1] + d_im[2]) * root
    dif_re, dif_im = d_re[1] - d_re[2], d_im[1] - d_im[2]
    out[3] = (d_re[0] - dif_re, d_im[0] - dif_im)
    mid_re, mid_im = d_re[0] + half * dif_re, d_im[0] + half * dif_im
    out[1] = (mid_re + sum_im, mid_im - sum_re)
    out[5] = (mid_re - sum_im, mid_im + sum_re)
    return out


def dot(a, b):
    return jnp.dot(a, b, preferred_element_type=jnp.float32)


def own_place():
    return lax.axis_index("row"), lax.axis_index("col")


def spectrum_of(grid, cond, occ, table_ref):
    norm = np.float32(grid ** (-1.5))
    width, x_first, twiddle_first = table_rows(grid)
    density = (cond.astype(jnp.float32) * occ.astype(jnp.float32)).astype(jnp.bfloat16)
    x_table = table_ref[x_first:twiddle_first, : 2 * grid]
    section = dot(x_table, jnp.concatenate([density, density], axis=0))
    re = [section[:KX_ROWS, h * width : (h + 1) * width] for h in range(RADIX)]
    im = [section[KX_ROWS:, h * width : (h + 1) * width] for h in range(RADIX)]
    chunks = width // LANES
    twiddle = 0.0
    for part in range(3):
        first = twiddle_first + 16 * chunks * part
        whole = [table_ref[first + 16 * i : first + 16 * (i + 1), :].astype(jnp.float32) for i in range(chunks)]
        twiddle = twiddle + jnp.concatenate(whole, axis=1)
    rows = []
    for residue, (d_re, d_im) in enumerate(dft_six(re, im)):
        if residue > 0:
            t_re = twiddle[residue : residue + 1, :]
            t_im = twiddle[RADIX + residue : RADIX + residue + 1, :]
            d_re, d_im = d_re * t_re - d_im * t_im, d_re * t_im + d_im * t_re
        rows.append(jnp.concatenate([d_re, d_im], axis=1))
    whole = jnp.concatenate(rows, axis=0)
    whole_hi = whole.astype(jnp.bfloat16)
    whole_lo = (whole - whole_hi.astype(jnp.float32)).astype(jnp.bfloat16)

    def rotation(first):
        cos_part = table_ref[first : first + width, :]
        sin_part = table_ref[first + width : first + 2 * width, :]
        upper = jnp.concatenate([cos_part, sin_part], axis=1)
        return jnp.concatenate([upper, jnp.concatenate([-sin_part, cos_part], axis=1)], axis=0)

    upper, lower = rotation(0), rotation(2 * width)
    spectrum = (dot(whole_hi, upper) + dot(whole_lo, upper) + dot(whole_hi, lower)) * norm
    parts = []
    for side in range(2):
        own = spectrum[:, side * LANES : (side + 1) * LANES]
        for group in range(RADIX // 2):
            first = 2 * group * KX_ROWS
            parts.append(jnp.concatenate([own[first : first + KX_ROWS], own[first + KX_ROWS : first + 2 * KX_ROWS]], axis=1))
    return jnp.concatenate(parts, axis=0).astype(jnp.bfloat16)


def pair_weights(sources, levels_ref):
    rows, cols = lax.axis_size("row"), lax.axis_size("col")
    r, _ = own_place()
    devices = rows * cols
    pairs = STEPS * len(sources)
    line = lax.broadcasted_iota(jnp.int32, (pairs, 1), 0)
    band = jnp.zeros((pairs, 1), jnp.int32)
    slot = jnp.zeros((pairs, 1), jnp.int32)
    for j, source in enumerate(sources):
        place = r * cols + source
        for step in range(STEPS):
            here = line == STEPS * j + step
            band = jnp.where(here, place, band)
            slot = jnp.where(here, lax.rem(place - step * cols + devices, devices), slot)
    lane = lax.broadcasted_iota(jnp.int32, (pairs, levels_ref.shape[1]), 1)

    def at(which, chosen):
        return jnp.sum(jnp.where(lane == chosen, levels_ref[which : which + 1, :], 0.0), axis=1, keepdims=True)

    gap = at(0, band) - at(1, at(2, slot).astype(jnp.int32))
    return -4.0 * gap / (gap * gap + OMEGA_SQUARED) / (devices * STEPS)


def first_kernel(grid, orbitals_ref, table_ref, sphere_ref, cube_ref, places_ref, table_out):
    half = grid // 2
    sx, sy, kz = sphere_ref[0:1, :], sphere_ref[1:2, :], sphere_ref[2:3, :]
    kx = jnp.where(sx >= half, sx - grid, sx) + GMAX
    ky = jnp.where(sy >= half, sy - grid, sy) + GMAX
    q = (ky * 43) >> 8
    residue = ky - q * RADIX
    places_ref[0:1, :] = (residue & 1) * LANES + q * GMAX + kz - 1
    places_ref[1:2, :] = (residue >> 1) * KX_ROWS + kx
    table_out[...] = table_ref[...]
    cube_ref[...] = spectrum_of(grid, orbitals_ref[0], orbitals_ref[1], table_ref)


def pick(cube_ref, places_ref, coef_ref):
    groups = RADIX // 2 * KX_ROWS // 8
    half_count = places_ref.shape[1]
    counted = lax.broadcasted_iota(jnp.int32, (2 * LANES, TILE), 0).astype(jnp.float32).astype(jnp.bfloat16)
    line = lax.broadcasted_iota(jnp.int32, (8, TILE), 0)
    for first in range(0, half_count, TILE):
        here = slice(first, first + TILE)
        lane = places_ref[0:1, here].astype(jnp.float32).astype(jnp.bfloat16)
        row = places_ref[1:2, here]
        one_hot = jnp.where(counted == lane, jnp.bfloat16(1), jnp.bfloat16(0))
        found = dot(cube_ref[...], one_hot)
        away = line - row
        values = [jnp.zeros((8, TILE), jnp.float32)] * 4
        for group in range(groups):
            chosen = away == -8 * group
            for which in range(4):
                start = (which * groups + group) * 8
                values[which] = jnp.where(chosen, found[start : start + 8], values[which])
        for which in range(4):
            pair, side = divmod(which, 2)
            value = jnp.sum(values[which], axis=0, keepdims=True)
            coef_ref[pair : pair + 1, side * half_count + first : side * half_count + first + TILE] = value.astype(jnp.bfloat16)


def second_kernel(grid, orbitals_ref, occ_ref, first_ref, places_ref, table_ref, coef_ref, later_ref, cube_ref):
    later_ref[...] = jnp.zeros_like(later_ref)
    picks = RADIX * KX_ROWS
    cube_ref[:picks, :] = first_ref[...]
    cube_ref[picks:, :] = spectrum_of(grid, orbitals_ref[0], occ_ref[0], table_ref)
    pick(cube_ref, places_ref, coef_ref)


def cost(flops, data):
    return pl.CostEstimate(flops=flops, bytes_accessed=data, transcendentals=0)


def in_vmem(count):
    return [pl.BlockSpec(memory_space=pltpu.VMEM)] * count


def transform(cond_orbitals, occ_orbitals, occ_second, sphere_index, band_shape):
    grid = cond_orbitals.shape[1]
    half_count = sphere_index.shape[1]
    table = jnp.asarray(packed_tables(grid))
    orbitals = jnp.concatenate([cond_orbitals, occ_orbitals], axis=0)
    picks = RADIX * KX_ROWS
    params = dict(
        compiler_params=pltpu.CompilerParams(vmem_limit_bytes=VMEM_LIMIT),
        cost_estimate=cost(2 * 10**9, 2 * 10**6),
    )
    handed = pl.pallas_call(
        functools.partial(first_kernel, grid),
        out_shape=[
            jax.ShapeDtypeStruct((picks, 2 * LANES), jnp.bfloat16),
            jax.ShapeDtypeStruct((2, half_count), jnp.int32),
            jax.ShapeDtypeStruct(table.shape, table.dtype),
        ],
        in_specs=in_vmem(3),
        out_specs=in_vmem(3),
        name="first_pair",
        **params,
    )(orbitals, table, sphere_index)
    return pl.pallas_call(
        functools.partial(second_kernel, grid),
        out_shape=[
            jax.ShapeDtypeStruct((STEPS, 2 * half_count), jnp.bfloat16),
            jax.ShapeDtypeStruct((1, *band_shape), jnp.int32),
        ],
        in_specs=in_vmem(5),
        out_specs=in_vmem(2),
        scratch_shapes=[pltpu.VMEM((STEPS * picks, 2 * LANES), jnp.bfloat16)],
        name="second_pair",
        **params,
    )(orbitals, occ_second, *handed)


def pack_kernel(plan, turns, targets, merged, levels_ref, *refs):
    rows, cols, row_width, col_width = plan
    count = len(refs) - len(targets) - 1 - merged
    arrived, outs, mixed_ref = refs[:count], refs[count:-1], refs[-1]
    r, c = own_place()
    first = 0
    for ref in arrived:
        mixed_ref[first : first + ref.shape[0], :] = ref[...].astype(jnp.float32)
        first += ref.shape[0]
    if merged:
        outs[-1][...] = mixed_ref[...].astype(jnp.bfloat16)
    weight = pair_weights([c ^ turn for turn in turns], levels_ref)
    columns = []
    for side in range(2):
        start = pl.multiple_of((c ^ side) * col_width, LANES)
        columns.append((weight * mixed_ref[:, pl.ds(start, col_width)]).astype(jnp.bfloat16))
    for (turn, side), out_ref in zip(targets, outs):
        start = pl.multiple_of((r ^ turn) // 2 * (2 * row_width), LANES)
        out_ref[:, : 2 * row_width] = mixed_ref[:, pl.ds(start, 2 * row_width)].astype(jnp.bfloat16)
        out_ref[:, 2 * row_width :] = columns[side]


def pack(arrived, levels, turns, targets, merged, plan):
    rows, cols, row_width, col_width = plan
    pairs = STEPS * len(turns)
    entries = arrived[0].shape[1]
    shapes = [(pairs, 2 * row_width + col_width)] * len(targets) + [(pairs, entries)] * merged
    return pl.pallas_call(
        functools.partial(pack_kernel, plan, turns, targets, merged),
        out_shape=[jax.ShapeDtypeStruct(shape, jnp.bfloat16) for shape in shapes],
        in_specs=in_vmem(1 + len(arrived)),
        out_specs=in_vmem(len(shapes)),
        scratch_shapes=[pltpu.VMEM((pairs, entries), jnp.float32)],
        compiler_params=pltpu.CompilerParams(vmem_limit_bytes=VMEM_LIMIT),
        cost_estimate=cost(10**9, 10**6),
        name="pack",
    )(levels, *arrived)


def stacked(refs, lanes):
    return jnp.concatenate([ref[:, lanes].astype(jnp.float32) for ref in refs], axis=0).astype(jnp.bfloat16)


def join_kernel(row_width, *refs):
    messages, outs = refs[:-2], refs[-2:]
    depth = messages[0].shape[0]
    merge = max(1, 16 // depth)
    r, _ = own_place()
    for j in range(0, len(messages), merge):
        here = slice(depth * j, depth * (j + merge))
        columns = stacked(messages[j : j + merge], slice(2 * row_width, None))
        for side, out_ref in enumerate(outs):
            lanes = pl.ds(pl.multiple_of((r & 1 ^ side) * row_width, LANES), row_width)
            out_ref[here, :row_width] = stacked(messages[j : j + merge], lanes)
            out_ref[here, row_width:] = columns


def join(messages, plan):
    rows, cols, row_width, col_width = plan
    depth = messages[0].shape[0]
    return pl.pallas_call(
        functools.partial(join_kernel, row_width),
        out_shape=[jax.ShapeDtypeStruct((depth * len(messages), row_width + col_width), jnp.bfloat16)] * 2,
        in_specs=in_vmem(len(messages)),
        out_specs=in_vmem(2),
        compiler_params=pltpu.CompilerParams(vmem_limit_bytes=VMEM_LIMIT),
        cost_estimate=cost(10**9, 10**6),
        name="join",
    )(*messages)


def outer_kernel(row_width, block, slots, *refs):
    messages, (out_ref, left_ref, right_ref, held_ref, sems) = refs[:-5], refs[-5:]
    depth = messages[0].shape[0]
    for j, ref in enumerate(messages):
        left_ref[depth * j : depth * (j + 1), :] = ref[:, :row_width]
        right_ref[depth * j : depth * (j + 1), :] = ref[:, row_width:]
    count = row_width // block

    def copy_out(i, slot):
        rows = pl.ds(pl.multiple_of(i * block, block), block)
        return pltpu.make_async_copy(held_ref.at[slot], out_ref.at[rows], sems.at[slot])

    def step(i, carry):
        slot = lax.rem(i, slots)

        @pl.when(i >= slots)
        def _():
            copy_out(i - slots, slot).wait()

        here = pl.ds(pl.multiple_of(i * block, block), block)
        held_ref[slot] = lax.dot_general(
            left_ref[:, here], right_ref[...], (((0,), (0,)), ((), ())), preferred_element_type=jnp.float32
        )
        copy_out(i, slot).start()
        return carry

    lax.fori_loop(0, count, step, 0)
    for i in range(max(0, count - slots), count):
        copy_out(i, i % slots).wait()


def outer(messages, plan):
    rows, cols, row_width, col_width = plan
    depth = messages[0].shape[0]
    block = min(256, row_width)
    slots = min(4, row_width // block)
    return pl.pallas_call(
        functools.partial(outer_kernel, row_width, block, slots),
        out_shape=jax.ShapeDtypeStruct((row_width, col_width), jnp.float32),
        in_specs=in_vmem(len(messages)),
        out_specs=pl.BlockSpec(memory_space=pltpu.HBM),
        scratch_shapes=[
            pltpu.VMEM((depth * len(messages), row_width), jnp.bfloat16),
            pltpu.VMEM((depth * len(messages), col_width), jnp.bfloat16),
            pltpu.VMEM((slots, block, col_width), jnp.float32),
            pltpu.SemaphoreType.DMA((slots,)),
        ],
        compiler_params=pltpu.CompilerParams(vmem_limit_bytes=VMEM_LIMIT),
        cost_estimate=cost(10**10, 3 * 10**7),
        name="outer",
    )(*messages)


def shifted(value, axis, by):
    devices = lax.axis_size(axis)
    return lax.ppermute(value, axis, [(i, (i + by) % devices) for i in range(devices)])


def turned(value, axis, turn):
    devices = lax.axis_size(axis)
    return lax.ppermute(value, axis, [(i, i ^ turn) for i in range(devices)])


def sent_across(value, turn, side, rows, cols):
    moves = [(r * cols + c, (r ^ turn) * cols + (c ^ side)) for r in range(rows) for c in range(cols)]
    return lax.ppermute(value, ("row", "col"), moves)


def on_device(cond_orbitals, occ_orbitals, cond_energy, occ_energy, occ_band, sphere_index):
    rows = lax.axis_size("row")
    cols = lax.axis_size("col")
    entries = 2 * sphere_index.shape[1]
    plan = (rows, cols, entries // rows, entries // cols)
    occ_second = shifted(occ_orbitals, "row", 1)
    own, later = transform(cond_orbitals, occ_orbitals, occ_second, sphere_index, occ_band.shape)
    levels = jnp.stack([cond_energy, occ_energy, (occ_band + later[0]).astype(jnp.float32)])
    targets = [(turn, side) for turn in range(0, rows, 2) for side in range(2)]

    def sent(packed):
        return [packed[0]] + [sent_across(value, *target, rows, cols) for value, target in zip(packed[1:], targets[1:])]

    held, turns, bit = [own], [0], cols // 2
    while bit > 2:
        if len(held) > 1:
            held = [jnp.concatenate(held, axis=0)]
        held.append(turned(held[0], "col", bit))
        turns += [turn + bit for turn in turns]
        bit //= 2
    *packed, merged = pack(held, levels, turns, targets, 1, plan)
    messages = sent(packed)
    far = turned(merged, "col", bit)
    messages += sent(pack([far], levels, [turn + bit for turn in turns], targets, 0, plan))
    kept, passed = join(messages, plan)
    return outer([kept, turned(passed, "row", 1)], plan)


def solution(mesh):
    placed = (P(("row", "col"), None, None), P(("row", "col"), None, None), P(), P(), P(), P())
    return jax.shard_map(
        on_device, mesh=mesh, in_specs=placed, out_specs=P("row", "col"), check_vma=False
    )
```

```python
import functools
import math

import jax
import jax.numpy as jnp
import ml_dtypes
import numpy as np
from jax import lax
from jax.experimental import pallas as pl
from jax.experimental.pallas import tpu as pltpu
from jax.sharding import PartitionSpec as P

GMAX = 18
STEPS = 2
RADIX = 6
SPAN = 2 * GMAX + 1
KX_ROWS = 40
LANES = 128
OMEGA_SQUARED = 0.0625
TILE = 512
VMEM_LIMIT = 40 * 2**20


def split(values, count):
    parts = []
    for _ in range(count):
        parts.append(values.astype(ml_dtypes.bfloat16))
        values = values - parts[-1].astype(np.float64)
    return parts


def table_rows(grid):
    width = (grid // RADIX) * grid
    x_first = 4 * width
    twiddle_first = x_first + 2 * KX_ROWS
    return width, x_first, twiddle_first


def packed_tables(grid):
    turn = 2.0 * np.pi / grid
    width, _, _ = table_rows(grid)
    y_lo = np.arange(width) // grid
    z = np.arange(width) % grid

    column = np.arange((2 * GMAX // RADIX + 1) * GMAX)
    q = column // GMAX - GMAX // RADIX
    kz = column % GMAX + 1
    phase = (RADIX * q[None, :] * y_lo[:, None] + kz[None, :] * z[:, None]) % grid
    last = np.zeros((2 * width, LANES))
    last[:width, : column.size] = np.cos(turn * phase)
    last[width:, : column.size] = -np.sin(turn * phase)
    pieces = split(last, 2)

    kx = np.arange(SPAN) - GMAX
    angle = turn * (kx[:, None] * np.arange(grid)[None, :] % grid)
    x_table = np.zeros((2 * KX_ROWS, grid))
    x_table[:SPAN] = np.cos(angle)
    x_table[KX_ROWS : KX_ROWS + SPAN] = -np.sin(angle)
    x_table = np.concatenate(split(x_table, 2), axis=1)
    pieces.append(np.pad(x_table, ((0, 0), (0, LANES - 2 * grid))))

    angle = turn * (np.arange(RADIX)[:, None] * y_lo[None, :] % grid)
    twiddle = np.zeros((16, width))
    twiddle[:RADIX] = np.cos(angle)
    twiddle[RADIX : 2 * RADIX] = -np.sin(angle)
    for part in split(twiddle, 3):
        pieces += [part[:, first : first + LANES] for first in range(0, width, LANES)]
    return np.concatenate(pieces, axis=0)


def dft_six(re, im):
    half = 0.5
    root = math.sqrt(3.0) / 2.0
    s_re = [re[h] + re[h + 3] for h in range(3)]
    s_im = [im[h] + im[h + 3] for h in range(3)]
    d_re = [re[h] - re[h + 3] for h in range(3)]
    d_im = [im[h] - im[h + 3] for h in range(3)]
    out = [None] * 6
    sum_re, sum_im = s_re[1] + s_re[2], s_im[1] + s_im[2]
    dif_re, dif_im = (s_re[1] - s_re[2]) * root, (s_im[1] - s_im[2]) * root
    out[0] = (s_re[0] + sum_re, s_im[0] + sum_im)
    mid_re, mid_im = s_re[0] - half * sum_re, s_im[0] - half * sum_im
    out[2] = (mid_re + dif_im, mid_im - dif_re)
    out[4] = (mid_re - dif_im, mid_im + dif_re)
    sum_re, sum_im = (d_re[1] + d_re[2]) * root, (d_im[1] + d_im[2]) * root
    dif_re, dif_im = d_re[1] - d_re[2], d_im[1] - d_im[2]
    out[3] = (d_re[0] - dif_re, d_im[0] - dif_im)
    mid_re, mid_im = d_re[0] + half * dif_re, d_im[0] + half * dif_im
    out[1] = (mid_re + sum_im, mid_im - sum_re)
    out[5] = (mid_re - sum_im, mid_im + sum_re)
    return out


def dot(a, b):
    return jnp.dot(a, b, preferred_element_type=jnp.float32)


def own_place():
    return lax.axis_index("row"), lax.axis_index("col")


def spectrum_of(grid, cond, occ, table_ref):
    norm = np.float32(grid ** (-1.5))
    width, x_first, twiddle_first = table_rows(grid)
    density = (cond.astype(jnp.float32) * occ.astype(jnp.float32)).astype(jnp.bfloat16)
    x_table = table_ref[x_first:twiddle_first, : 2 * grid]
    section = dot(x_table, jnp.concatenate([density, density], axis=0))
    re = [section[:KX_ROWS, h * width : (h + 1) * width] for h in range(RADIX)]
    im = [section[KX_ROWS:, h * width : (h + 1) * width] for h in range(RADIX)]
    chunks = width // LANES
    twiddle = 0.0
    for part in range(3):
        first = twiddle_first + 16 * chunks * part
        whole = [table_ref[first + 16 * i : first + 16 * (i + 1), :].astype(jnp.float32) for i in range(chunks)]
        twiddle = twiddle + jnp.concatenate(whole, axis=1)
    rows = []
    for residue, (d_re, d_im) in enumerate(dft_six(re, im)):
        if residue > 0:
            t_re = twiddle[residue : residue + 1, :]
            t_im = twiddle[RADIX + residue : RADIX + residue + 1, :]
            d_re, d_im = d_re * t_re - d_im * t_im, d_re * t_im + d_im * t_re
        rows.append(jnp.concatenate([d_re, d_im], axis=1))
    whole = jnp.concatenate(rows, axis=0)
    whole_hi = whole.astype(jnp.bfloat16)
    whole_lo = (whole - whole_hi.astype(jnp.float32)).astype(jnp.bfloat16)

    def rotation(first):
        cos_part = table_ref[first : first + width, :]
        sin_part = table_ref[first + width : first + 2 * width, :]
        upper = jnp.concatenate([cos_part, sin_part], axis=1)
        return jnp.concatenate([upper, jnp.concatenate([-sin_part, cos_part], axis=1)], axis=0)

    upper, lower = rotation(0), rotation(2 * width)
    spectrum = (dot(whole_hi, upper) + dot(whole_lo, upper) + dot(whole_hi, lower)) * norm
    parts = []
    for side in range(2):
        own = spectrum[:, side * LANES : (side + 1) * LANES]
        for group in range(RADIX // 2):
            first = 2 * group * KX_ROWS
            parts.append(jnp.concatenate([own[first : first + KX_ROWS], own[first + KX_ROWS : first + 2 * KX_ROWS]], axis=1))
    return jnp.concatenate(parts, axis=0).astype(jnp.bfloat16)


def pair_weights(sources, levels_ref):
    rows, cols = lax.axis_size("row"), lax.axis_size("col")
    r, _ = own_place()
    devices = rows * cols
    pairs = STEPS * len(sources)
    line = lax.broadcasted_iota(jnp.int32, (pairs, 1), 0)
    band = jnp.zeros((pairs, 1), jnp.int32)
    slot = jnp.zeros((pairs, 1), jnp.int32)
    for j, source in enumerate(sources):
        place = r * cols + source
        for step in range(STEPS):
            here = line == STEPS * j + step
            band = jnp.where(here, place, band)
            slot = jnp.where(here, lax.rem(place - step * cols + devices, devices), slot)
    lane = lax.broadcasted_iota(jnp.int32, (pairs, levels_ref.shape[1]), 1)

    def at(which, chosen):
        return jnp.sum(jnp.where(lane == chosen, levels_ref[which : which + 1, :], 0.0), axis=1, keepdims=True)

    gap = at(0, band) - at(1, at(2, slot).astype(jnp.int32))
    return -4.0 * gap / (gap * gap + OMEGA_SQUARED) / (devices * STEPS)


def first_kernel(grid, orbitals_ref, table_ref, sphere_ref, cube_ref, places_ref, table_out):
    half = grid // 2
    sx, sy, kz = sphere_ref[0:1, :], sphere_ref[1:2, :], sphere_ref[2:3, :]
    kx = jnp.where(sx >= half, sx - grid, sx) + GMAX
    ky = jnp.where(sy >= half, sy - grid, sy) + GMAX
    q = (ky * 43) >> 8
    residue = ky - q * RADIX
    places_ref[0:1, :] = (residue & 1) * LANES + q * GMAX + kz - 1
    places_ref[1:2, :] = (residue >> 1) * KX_ROWS + kx
    table_out[...] = table_ref[...]
    cube_ref[...] = spectrum_of(grid, orbitals_ref[0], orbitals_ref[1], table_ref)


def pick(cube_ref, places_ref, coef_ref):
    groups = RADIX // 2 * KX_ROWS // 8
    half_count = places_ref.shape[1]
    counted = lax.broadcasted_iota(jnp.int32, (2 * LANES, TILE), 0).astype(jnp.float32).astype(jnp.bfloat16)
    line = lax.broadcasted_iota(jnp.int32, (8, TILE), 0)
    for first in range(0, half_count, TILE):
        here = slice(first, first + TILE)
        lane = places_ref[0:1, here].astype(jnp.float32).astype(jnp.bfloat16)
        row = places_ref[1:2, here]
        one_hot = jnp.where(counted == lane, jnp.bfloat16(1), jnp.bfloat16(0))
        found = dot(cube_ref[...], one_hot)
        away = line - row
        values = [jnp.zeros((8, TILE), jnp.float32)] * 4
        for group in range(groups):
            chosen = away == -8 * group
            for which in range(4):
                start = (which * groups + group) * 8
                values[which] = jnp.where(chosen, found[start : start + 8], values[which])
        for which in range(4):
            pair, side = divmod(which, 2)
            value = jnp.sum(values[which], axis=0, keepdims=True)
            coef_ref[pair : pair + 1, side * half_count + first : side * half_count + first + TILE] = value.astype(jnp.bfloat16)


def second_kernel(grid, orbitals_ref, occ_ref, first_ref, places_ref, table_ref, coef_ref, later_ref, cube_ref):
    later_ref[...] = jnp.zeros_like(later_ref)
    picks = RADIX * KX_ROWS
    cube_ref[:picks, :] = first_ref[...]
    cube_ref[picks:, :] = spectrum_of(grid, orbitals_ref[0], occ_ref[0], table_ref)
    pick(cube_ref, places_ref, coef_ref)


def cost(flops, data):
    return pl.CostEstimate(flops=flops, bytes_accessed=data, transcendentals=0)


def in_vmem(count):
    return [pl.BlockSpec(memory_space=pltpu.VMEM)] * count


def transform(cond_orbitals, occ_orbitals, occ_second, sphere_index, band_shape):
    grid = cond_orbitals.shape[1]
    half_count = sphere_index.shape[1]
    table = jnp.asarray(packed_tables(grid))
    orbitals = jnp.concatenate([cond_orbitals, occ_orbitals], axis=0)
    picks = RADIX * KX_ROWS
    params = dict(
        compiler_params=pltpu.CompilerParams(vmem_limit_bytes=VMEM_LIMIT),
        cost_estimate=cost(2 * 10**9, 2 * 10**6),
    )
    handed = pl.pallas_call(
        functools.partial(first_kernel, grid),
        out_shape=[
            jax.ShapeDtypeStruct((picks, 2 * LANES), jnp.bfloat16),
            jax.ShapeDtypeStruct((2, half_count), jnp.int32),
            jax.ShapeDtypeStruct(table.shape, table.dtype),
        ],
        in_specs=in_vmem(3),
        out_specs=in_vmem(3),
        name="first_pair",
        **params,
    )(orbitals, table, sphere_index)
    return pl.pallas_call(
        functools.partial(second_kernel, grid),
        out_shape=[
            jax.ShapeDtypeStruct((STEPS, 2 * half_count), jnp.bfloat16),
            jax.ShapeDtypeStruct((1, *band_shape), jnp.int32),
        ],
        in_specs=in_vmem(5),
        out_specs=in_vmem(2),
        scratch_shapes=[pltpu.VMEM((STEPS * picks, 2 * LANES), jnp.bfloat16)],
        name="second_pair",
        **params,
    )(orbitals, occ_second, *handed)


def pack_kernel(plan, turns, targets, merged, levels_ref, *refs):
    rows, cols, row_width, col_width = plan
    count = len(refs) - len(targets) - 1 - merged
    arrived, outs, mixed_ref = refs[:count], refs[count:-1], refs[-1]
    r, c = own_place()
    first = 0
    for ref in arrived:
        mixed_ref[first : first + ref.shape[0], :] = ref[...].astype(jnp.float32)
        first += ref.shape[0]
    if merged:
        outs[-1][...] = mixed_ref[...].astype(jnp.bfloat16)
    weight = pair_weights([c ^ turn for turn in turns], levels_ref)
    columns = []
    for side in range(2):
        start = pl.multiple_of((c ^ side) * col_width, LANES)
        columns.append((weight * mixed_ref[:, pl.ds(start, col_width)]).astype(jnp.bfloat16))
    for (turn, side), out_ref in zip(targets, outs):
        start = pl.multiple_of((r ^ turn) // 2 * (2 * row_width), LANES)
        out_ref[:, : 2 * row_width] = mixed_ref[:, pl.ds(start, 2 * row_width)].astype(jnp.bfloat16)
        out_ref[:, 2 * row_width :] = columns[side]


def pack(arrived, levels, turns, targets, merged, plan):
    rows, cols, row_width, col_width = plan
    pairs = STEPS * len(turns)
    entries = arrived[0].shape[1]
    shapes = [(pairs, 2 * row_width + col_width)] * len(targets) + [(pairs, entries)] * merged
    return pl.pallas_call(
        functools.partial(pack_kernel, plan, turns, targets, merged),
        out_shape=[jax.ShapeDtypeStruct(shape, jnp.bfloat16) for shape in shapes],
        in_specs=in_vmem(1 + len(arrived)),
        out_specs=in_vmem(len(shapes)),
        scratch_shapes=[pltpu.VMEM((pairs, entries), jnp.float32)],
        compiler_params=pltpu.CompilerParams(vmem_limit_bytes=VMEM_LIMIT),
        cost_estimate=cost(10**9, 10**6),
        name="pack",
    )(levels, *arrived)


def stacked(refs, lanes):
    return jnp.concatenate([ref[:, lanes].astype(jnp.float32) for ref in refs], axis=0).astype(jnp.bfloat16)


def join_kernel(row_width, *refs):
    messages, outs = refs[:-2], refs[-2:]
    depth = messages[0].shape[0]
    merge = max(1, 16 // depth)
    r, _ = own_place()
    for j in range(0, len(messages), merge):
        here = slice(depth * j, depth * (j + merge))
        columns = stacked(messages[j : j + merge], slice(2 * row_width, None))
        for side, out_ref in enumerate(outs):
            lanes = pl.ds(pl.multiple_of((r & 1 ^ side) * row_width, LANES), row_width)
            out_ref[here, :row_width] = stacked(messages[j : j + merge], lanes)
            out_ref[here, row_width:] = columns


def join(messages, plan):
    rows, cols, row_width, col_width = plan
    depth = messages[0].shape[0]
    return pl.pallas_call(
        functools.partial(join_kernel, row_width),
        out_shape=[jax.ShapeDtypeStruct((depth * len(messages), row_width + col_width), jnp.bfloat16)] * 2,
        in_specs=in_vmem(len(messages)),
        out_specs=in_vmem(2),
        compiler_params=pltpu.CompilerParams(vmem_limit_bytes=VMEM_LIMIT),
        cost_estimate=cost(10**9, 10**6),
        name="join",
    )(*messages)


def outer_kernel(row_width, block, slots, *refs):
    messages, (out_ref, right_ref, held_ref, sems) = refs[:-4], refs[-4:]
    depth = messages[0].shape[0]
    for j, ref in enumerate(messages):
        right_ref[depth * j : depth * (j + 1), :] = ref[:, row_width:]
    count = row_width // block

    def copy_out(i, slot):
        rows = pl.ds(pl.multiple_of(i * block, block), block)
        return pltpu.make_async_copy(held_ref.at[slot], out_ref.at[rows], sems.at[slot])

    def step(i, carry):
        slot = lax.rem(i, slots)

        @pl.when(i >= slots)
        def _():
            copy_out(i - slots, slot).wait()

        here = pl.ds(pl.multiple_of(i * block, block), block)
        left = jnp.concatenate([ref[:, here] for ref in messages], axis=0)
        held_ref[slot] = lax.dot_general(left, right_ref[...], (((0,), (0,)), ((), ())), preferred_element_type=jnp.float32)
        copy_out(i, slot).start()
        return carry

    lax.fori_loop(0, count, step, 0)
    for i in range(max(0, count - slots), count):
        copy_out(i, i % slots).wait()


def outer(messages, plan):
    rows, cols, row_width, col_width = plan
    depth = messages[0].shape[0]
    block = min(256, row_width)
    slots = min(4, row_width // block)
    return pl.pallas_call(
        functools.partial(outer_kernel, row_width, block, slots),
        out_shape=jax.ShapeDtypeStruct((row_width, col_width), jnp.float32),
        in_specs=in_vmem(len(messages)),
        out_specs=pl.BlockSpec(memory_space=pltpu.HBM),
        scratch_shapes=[
            pltpu.VMEM((depth * len(messages), col_width), jnp.bfloat16),
            pltpu.VMEM((slots, block, col_width), jnp.float32),
            pltpu.SemaphoreType.DMA((slots,)),
        ],
        compiler_params=pltpu.CompilerParams(vmem_limit_bytes=VMEM_LIMIT),
        cost_estimate=cost(10**10, 3 * 10**7),
        name="outer",
    )(*messages)


def shifted(value, axis, by):
    devices = lax.axis_size(axis)
    return lax.ppermute(value, axis, [(i, (i + by) % devices) for i in range(devices)])


def turned(value, axis, turn):
    devices = lax.axis_size(axis)
    return lax.ppermute(value, axis, [(i, i ^ turn) for i in range(devices)])


def sent_across(value, turn, side, rows, cols):
    moves = [(r * cols + c, (r ^ turn) * cols + (c ^ side)) for r in range(rows) for c in range(cols)]
    return lax.ppermute(value, ("row", "col"), moves)


def on_device(cond_orbitals, occ_orbitals, cond_energy, occ_energy, occ_band, sphere_index):
    rows = lax.axis_size("row")
    cols = lax.axis_size("col")
    entries = 2 * sphere_index.shape[1]
    plan = (rows, cols, entries // rows, entries // cols)
    occ_second = shifted(occ_orbitals, "row", 1)
    own, later = transform(cond_orbitals, occ_orbitals, occ_second, sphere_index, occ_band.shape)
    levels = jnp.stack([cond_energy, occ_energy, (occ_band + later[0]).astype(jnp.float32)])
    targets = [(0, 0)] + [(turn, side) for side in (1, 0) for turn in range(rows - 2, -2, -2) if turn or side]
    targets.append(targets.pop(rows // 2))

    def sent(packed):
        return [packed[0]] + [sent_across(value, *target, rows, cols) for value, target in zip(packed[1:], targets[1:])]

    held, turns, bit = [own], [0], cols // 2
    while bit > 2:
        if len(held) > 1:
            held = [jnp.concatenate(held, axis=0)]
        held.append(turned(held[0], "col", bit))
        turns += [turn + bit for turn in turns]
        bit //= 2
    *packed, merged = pack(held, levels, turns, targets, 1, plan)
    messages = sent(packed)
    far = turned(merged, "col", bit)
    messages += sent(pack([far], levels, [turn + bit for turn in turns], targets, 0, plan))
    kept, passed = join(messages, plan)
    return outer([kept, turned(passed, "row", 1)], plan)


def solution(mesh):
    placed = (P(("row", "col"), None, None), P(("row", "col"), None, None), P(), P(), P(), P())
    return jax.shard_map(
        on_device, mesh=mesh, in_specs=placed, out_specs=P("row", "col"), check_vma=False
    )
```

```python
import functools
import math

import jax
import jax.numpy as jnp
import ml_dtypes
import numpy as np
from jax import lax
from jax.experimental import pallas as pl
from jax.experimental.pallas import tpu as pltpu
from jax.sharding import PartitionSpec as P

GMAX = 18
STEPS = 2
RADIX = 6
SPAN = 2 * GMAX + 1
KX_ROWS = 40
LANES = 128
OMEGA_SQUARED = 0.0625
TILE = 512
VMEM_LIMIT = 40 * 2**20


def split(values, count):
    parts = []
    for _ in range(count):
        parts.append(values.astype(ml_dtypes.bfloat16))
        values = values - parts[-1].astype(np.float64)
    return parts


def table_rows(grid):
    width = (grid // RADIX) * grid
    x_first = 4 * width
    twiddle_first = x_first + 2 * KX_ROWS
    return width, x_first, twiddle_first


def packed_tables(grid):
    turn = 2.0 * np.pi / grid
    width, _, _ = table_rows(grid)
    y_lo = np.arange(width) // grid
    z = np.arange(width) % grid

    column = np.arange((2 * GMAX // RADIX + 1) * GMAX)
    q = column // GMAX - GMAX // RADIX
    kz = column % GMAX + 1
    phase = (RADIX * q[None, :] * y_lo[:, None] + kz[None, :] * z[:, None]) % grid
    last = np.zeros((2 * width, LANES))
    last[:width, : column.size] = np.cos(turn * phase)
    last[width:, : column.size] = -np.sin(turn * phase)
    pieces = split(last, 2)

    kx = np.arange(SPAN) - GMAX
    angle = turn * (kx[:, None] * np.arange(grid)[None, :] % grid)
    x_table = np.zeros((2 * KX_ROWS, grid))
    x_table[:SPAN] = np.cos(angle)
    x_table[KX_ROWS : KX_ROWS + SPAN] = -np.sin(angle)
    x_table = np.concatenate(split(x_table, 2), axis=1)
    pieces.append(np.pad(x_table, ((0, 0), (0, LANES - 2 * grid))))

    angle = turn * (np.arange(RADIX)[:, None] * y_lo[None, :] % grid)
    twiddle = np.zeros((16, width))
    twiddle[:RADIX] = np.cos(angle)
    twiddle[RADIX : 2 * RADIX] = -np.sin(angle)
    for part in split(twiddle, 3):
        pieces += [part[:, first : first + LANES] for first in range(0, width, LANES)]
    return np.concatenate(pieces, axis=0)


def dft_six(re, im):
    half = 0.5
    root = math.sqrt(3.0) / 2.0
    s_re = [re[h] + re[h + 3] for h in range(3)]
    s_im = [im[h] + im[h + 3] for h in range(3)]
    d_re = [re[h] - re[h + 3] for h in range(3)]
    d_im = [im[h] - im[h + 3] for h in range(3)]
    out = [None] * 6
    sum_re, sum_im = s_re[1] + s_re[2], s_im[1] + s_im[2]
    dif_re, dif_im = (s_re[1] - s_re[2]) * root, (s_im[1] - s_im[2]) * root
    out[0] = (s_re[0] + sum_re, s_im[0] + sum_im)
    mid_re, mid_im = s_re[0] - half * sum_re, s_im[0] - half * sum_im
    out[2] = (mid_re + dif_im, mid_im - dif_re)
    out[4] = (mid_re - dif_im, mid_im + dif_re)
    sum_re, sum_im = (d_re[1] + d_re[2]) * root, (d_im[1] + d_im[2]) * root
    dif_re, dif_im = d_re[1] - d_re[2], d_im[1] - d_im[2]
    out[3] = (d_re[0] - dif_re, d_im[0] - dif_im)
    mid_re, mid_im = d_re[0] + half * dif_re, d_im[0] + half * dif_im
    out[1] = (mid_re + sum_im, mid_im - sum_re)
    out[5] = (mid_re - sum_im, mid_im + sum_re)
    return out


def dot(a, b):
    return jnp.dot(a, b, preferred_element_type=jnp.float32)


def own_place():
    return lax.axis_index("row"), lax.axis_index("col")


def spectrum_of(grid, cond, occ, table_ref):
    norm = np.float32(grid ** (-1.5))
    width, x_first, twiddle_first = table_rows(grid)
    density = (cond.astype(jnp.float32) * occ.astype(jnp.float32)).astype(jnp.bfloat16)
    x_table = table_ref[x_first:twiddle_first, : 2 * grid]
    section = dot(x_table, jnp.concatenate([density, density], axis=0))
    re = [section[:KX_ROWS, h * width : (h + 1) * width] for h in range(RADIX)]
    im = [section[KX_ROWS:, h * width : (h + 1) * width] for h in range(RADIX)]
    chunks = width // LANES
    twiddle = 0.0
    for part in range(3):
        first = twiddle_first + 16 * chunks * part
        whole = [table_ref[first + 16 * i : first + 16 * (i + 1), :].astype(jnp.float32) for i in range(chunks)]
        twiddle = twiddle + jnp.concatenate(whole, axis=1)
    rows = []
    for residue, (d_re, d_im) in enumerate(dft_six(re, im)):
        if residue > 0:
            t_re = twiddle[residue : residue + 1, :]
            t_im = twiddle[RADIX + residue : RADIX + residue + 1, :]
            d_re, d_im = d_re * t_re - d_im * t_im, d_re * t_im + d_im * t_re
        rows.append(jnp.concatenate([d_re, d_im], axis=1))
    whole = jnp.concatenate(rows, axis=0)
    whole_hi = whole.astype(jnp.bfloat16)
    whole_lo = (whole - whole_hi.astype(jnp.float32)).astype(jnp.bfloat16)

    def rotation(first):
        cos_part = table_ref[first : first + width, :]
        sin_part = table_ref[first + width : first + 2 * width, :]
        upper = jnp.concatenate([cos_part, sin_part], axis=1)
        return jnp.concatenate([upper, jnp.concatenate([-sin_part, cos_part], axis=1)], axis=0)

    upper, lower = rotation(0), rotation(2 * width)
    spectrum = (dot(whole_hi, upper) + dot(whole_lo, upper) + dot(whole_hi, lower)) * norm
    parts = []
    for side in range(2):
        own = spectrum[:, side * LANES : (side + 1) * LANES]
        for group in range(RADIX // 2):
            first = 2 * group * KX_ROWS
            parts.append(jnp.concatenate([own[first : first + KX_ROWS], own[first + KX_ROWS : first + 2 * KX_ROWS]], axis=1))
    return jnp.concatenate(parts, axis=0).astype(jnp.bfloat16)


def pair_weights(sources, levels_ref):
    rows, cols = lax.axis_size("row"), lax.axis_size("col")
    devices = rows * cols
    pairs = STEPS * len(sources)
    line = lax.broadcasted_iota(jnp.int32, (pairs, 1), 0)
    band = jnp.zeros((pairs, 1), jnp.int32)
    slot = jnp.zeros((pairs, 1), jnp.int32)
    for j, place in enumerate(sources):
        for step in range(STEPS):
            here = line == STEPS * j + step
            band = jnp.where(here, place, band)
            slot = jnp.where(here, lax.rem(place - step * cols + devices, devices), slot)
    lane = lax.broadcasted_iota(jnp.int32, (pairs, levels_ref.shape[1]), 1)

    def at(which, chosen):
        return jnp.sum(jnp.where(lane == chosen, levels_ref[which : which + 1, :], 0.0), axis=1, keepdims=True)

    gap = at(0, band) - at(1, at(2, slot).astype(jnp.int32))
    return -4.0 * gap / (gap * gap + OMEGA_SQUARED) / (devices * STEPS)


def first_kernel(grid, orbitals_ref, table_ref, sphere_ref, cube_ref, places_ref, table_out):
    half = grid // 2
    sx, sy, kz = sphere_ref[0:1, :], sphere_ref[1:2, :], sphere_ref[2:3, :]
    kx = jnp.where(sx >= half, sx - grid, sx) + GMAX
    ky = jnp.where(sy >= half, sy - grid, sy) + GMAX
    q = (ky * 43) >> 8
    residue = ky - q * RADIX
    places_ref[0:1, :] = (residue & 1) * LANES + q * GMAX + kz - 1
    places_ref[1:2, :] = (residue >> 1) * KX_ROWS + kx
    table_out[...] = table_ref[...]
    cube_ref[...] = spectrum_of(grid, orbitals_ref[0], orbitals_ref[1], table_ref)


def pick(cube_ref, places_ref, coef_ref):
    groups = RADIX // 2 * KX_ROWS // 8
    half_count = places_ref.shape[1]
    counted = lax.broadcasted_iota(jnp.int32, (2 * LANES, TILE), 0).astype(jnp.float32).astype(jnp.bfloat16)
    line = lax.broadcasted_iota(jnp.int32, (8, TILE), 0)
    for first in range(0, half_count, TILE):
        here = slice(first, first + TILE)
        lane = places_ref[0:1, here].astype(jnp.float32).astype(jnp.bfloat16)
        row = places_ref[1:2, here]
        one_hot = jnp.where(counted == lane, jnp.bfloat16(1), jnp.bfloat16(0))
        found = dot(cube_ref[...], one_hot)
        away = line - row
        values = [jnp.zeros((8, TILE), jnp.float32)] * 4
        for group in range(groups):
            chosen = away == -8 * group
            for which in range(4):
                start = (which * groups + group) * 8
                values[which] = jnp.where(chosen, found[start : start + 8], values[which])
        for which in range(4):
            pair, side = divmod(which, 2)
            value = jnp.sum(values[which], axis=0, keepdims=True)
            coef_ref[pair : pair + 1, side * half_count + first : side * half_count + first + TILE] = value.astype(jnp.bfloat16)


def fill_message(plan, target, coefficients_ref, out_ref):
    rows, cols, row_width, col_width = plan
    r, c = own_place()
    turn, side = target
    start = pl.multiple_of((r ^ turn) // 2 * (2 * row_width), LANES)
    out_ref[:, : 2 * row_width] = coefficients_ref[:, pl.ds(start, 2 * row_width)].astype(jnp.bfloat16)
    start = pl.multiple_of((c ^ side) * col_width, LANES)
    out_ref[:, 2 * row_width :] = coefficients_ref[:, pl.ds(start, col_width)].astype(jnp.bfloat16)


def second_kernel(grid, plan, targets, orbitals_ref, occ_ref, first_ref, places_ref, table_ref, coef_ref, later_ref, *refs):
    outs, cube_ref = refs[:-1], refs[-1]
    later_ref[...] = jnp.zeros_like(later_ref)
    picks = RADIX * KX_ROWS
    cube_ref[:picks, :] = first_ref[...]
    cube_ref[picks:, :] = spectrum_of(grid, orbitals_ref[0], occ_ref[0], table_ref)
    pick(cube_ref, places_ref, coef_ref)
    for target, out_ref in zip(targets, outs):
        fill_message(plan, target, coef_ref, out_ref)


def cost(flops, data):
    return pl.CostEstimate(flops=flops, bytes_accessed=data, transcendentals=0)


def in_vmem(count):
    return [pl.BlockSpec(memory_space=pltpu.VMEM)] * count


def transform(cond_orbitals, occ_orbitals, occ_second, sphere_index, band_shape, targets, plan):
    grid = cond_orbitals.shape[1]
    half_count = sphere_index.shape[1]
    table = jnp.asarray(packed_tables(grid))
    orbitals = jnp.concatenate([cond_orbitals, occ_orbitals], axis=0)
    picks = RADIX * KX_ROWS
    params = dict(
        compiler_params=pltpu.CompilerParams(vmem_limit_bytes=VMEM_LIMIT),
        cost_estimate=cost(2 * 10**9, 2 * 10**6),
    )
    handed = pl.pallas_call(
        functools.partial(first_kernel, grid),
        out_shape=[
            jax.ShapeDtypeStruct((picks, 2 * LANES), jnp.bfloat16),
            jax.ShapeDtypeStruct((2, half_count), jnp.int32),
            jax.ShapeDtypeStruct(table.shape, table.dtype),
        ],
        in_specs=in_vmem(3),
        out_specs=in_vmem(3),
        name="first_pair",
        **params,
    )(orbitals, table, sphere_index)
    return pl.pallas_call(
        functools.partial(second_kernel, grid, plan, targets),
        out_shape=[
            jax.ShapeDtypeStruct((STEPS, 2 * half_count), jnp.bfloat16),
            jax.ShapeDtypeStruct((1, *band_shape), jnp.int32),
            *[message_shape(STEPS, plan)] * len(targets),
        ],
        in_specs=in_vmem(5),
        out_specs=in_vmem(2 + len(targets)),
        scratch_shapes=[pltpu.VMEM((STEPS * picks, 2 * LANES), jnp.bfloat16)],
        name="second_pair",
        **params,
    )(orbitals, occ_second, *handed)


def message_shape(pairs, plan):
    rows, cols, row_width, col_width = plan
    return jax.ShapeDtypeStruct((pairs, 2 * row_width + col_width), jnp.bfloat16)


def pack_kernel(plan, targets, count, *refs):
    arrived, outs, mixed_ref = refs[:count], refs[-1 - len(targets) : -1], refs[-1]
    first = 0
    for ref in arrived:
        mixed_ref[first : first + ref.shape[0], :] = ref[...].astype(jnp.float32)
        first += ref.shape[0]
    for target, out_ref in zip(targets, outs):
        fill_message(plan, target, mixed_ref, out_ref)


def pack(arrived, behind, targets, plan):
    pairs = sum(value.shape[0] for value in arrived)
    return pl.pallas_call(
        functools.partial(pack_kernel, plan, targets, len(arrived)),
        out_shape=[message_shape(pairs, plan)] * len(targets),
        in_specs=in_vmem(len(arrived) + len(behind)),
        out_specs=in_vmem(len(targets)),
        scratch_shapes=[pltpu.VMEM((pairs, arrived[0].shape[1]), jnp.float32)],
        compiler_params=pltpu.CompilerParams(vmem_limit_bytes=VMEM_LIMIT),
        cost_estimate=cost(10**9, 10**6),
        name="pack",
    )(*arrived, *behind)


def stacked(refs, lanes):
    return jnp.concatenate([ref[:, lanes].astype(jnp.float32) for ref in refs], axis=0).astype(jnp.bfloat16)


def join_kernel(plan, turns, levels_ref, *refs):
    rows, cols, row_width, col_width = plan
    messages, outs = refs[:-2], refs[-2:]
    r, c = own_place()
    weights = pair_weights([(r ^ row_turn) * cols + (c ^ col_turn) for part in turns for row_turn, col_turn in part], levels_ref)
    first, group = 0, []
    for ref in messages:
        group.append(ref)
        depth = sum(part.shape[0] for part in group)
        if depth % 16 and ref is not messages[-1]:
            continue
        here = slice(first, first + depth)
        columns = stacked(group, slice(2 * row_width, None)).astype(jnp.float32)
        columns = (weights[here] * columns).astype(jnp.bfloat16)
        for side, out_ref in enumerate(outs):
            lanes = pl.ds(pl.multiple_of((r & 1 ^ side) * row_width, LANES), row_width)
            out_ref[here, :row_width] = stacked(group, lanes)
            out_ref[here, row_width:] = columns
        first, group = first + depth, []


def join(messages, turns, levels, plan):
    rows, cols, row_width, col_width = plan
    depth = sum(message.shape[0] for message in messages)
    return pl.pallas_call(
        functools.partial(join_kernel, plan, turns),
        out_shape=[jax.ShapeDtypeStruct((depth, row_width + col_width), jnp.bfloat16)] * 2,
        in_specs=in_vmem(1 + len(messages)),
        out_specs=in_vmem(2),
        compiler_params=pltpu.CompilerParams(vmem_limit_bytes=VMEM_LIMIT),
        cost_estimate=cost(10**9, 10**6),
        name="join",
    )(levels, *messages)


def outer_kernel(row_width, block, slots, *refs):
    messages, (out_ref, right_ref, held_ref, sems) = refs[:-4], refs[-4:]
    depth = messages[0].shape[0]
    for j, ref in enumerate(messages):
        right_ref[depth * j : depth * (j + 1), :] = ref[:, row_width:]
    count = row_width // block

    def copy_out(i, slot):
        rows = pl.ds(pl.multiple_of(i * block, block), block)
        return pltpu.make_async_copy(held_ref.at[slot], out_ref.at[rows], sems.at[slot])

    def step(i, carry):
        slot = lax.rem(i, slots)

        @pl.when(i >= slots)
        def _():
            copy_out(i - slots, slot).wait()

        here = pl.ds(pl.multiple_of(i * block, block), block)
        left = jnp.concatenate([ref[:, here] for ref in messages], axis=0)
        held_ref[slot] = lax.dot_general(left, right_ref[...], (((0,), (0,)), ((), ())), preferred_element_type=jnp.float32)
        copy_out(i, slot).start()
        return carry

    lax.fori_loop(0, count, step, 0)
    for i in range(max(0, count - slots), count):
        copy_out(i, i % slots).wait()


def outer(messages, plan):
    rows, cols, row_width, col_width = plan
    depth = messages[0].shape[0]
    block = min(256, row_width)
    slots = min(4, row_width // block)
    return pl.pallas_call(
        functools.partial(outer_kernel, row_width, block, slots),
        out_shape=jax.ShapeDtypeStruct((row_width, col_width), jnp.float32),
        in_specs=in_vmem(len(messages)),
        out_specs=pl.BlockSpec(memory_space=pltpu.HBM),
        scratch_shapes=[
            pltpu.VMEM((depth * len(messages), col_width), jnp.bfloat16),
            pltpu.VMEM((slots, block, col_width), jnp.float32),
            pltpu.SemaphoreType.DMA((slots,)),
        ],
        compiler_params=pltpu.CompilerParams(vmem_limit_bytes=VMEM_LIMIT),
        cost_estimate=cost(10**10, 3 * 10**7),
        name="outer",
    )(*messages)


def shifted(value, axis, by):
    devices = lax.axis_size(axis)
    return lax.ppermute(value, axis, [(i, (i + by) % devices) for i in range(devices)])


def turned(value, axis, turn):
    devices = lax.axis_size(axis)
    return lax.ppermute(value, axis, [(i, i ^ turn) for i in range(devices)])


def sent_across(value, turn, side, rows, cols):
    moves = [(r * cols + c, (r ^ turn) * cols + (c ^ side)) for r in range(rows) for c in range(cols)]
    return lax.ppermute(value, ("row", "col"), moves)


def on_device(cond_orbitals, occ_orbitals, cond_energy, occ_energy, occ_band, sphere_index):
    rows = lax.axis_size("row")
    cols = lax.axis_size("col")
    entries = 2 * sphere_index.shape[1]
    plan = (rows, cols, entries // rows, entries // cols)
    occ_second = shifted(occ_orbitals, "row", 1)
    targets = [(0, 0)] + [(turn, side) for side in (1, 0) for turn in range(rows - 2, -2, -2) if turn or side]
    targets.append(targets.pop(rows // 2))

    def sent(packed):
        return [packed[0]] + [sent_across(value, *target, rows, cols) for value, target in zip(packed[1:], targets[1:])]

    own, later, *packed = transform(cond_orbitals, occ_orbitals, occ_second, sphere_index, occ_band.shape, targets, plan)
    levels = jnp.stack([cond_energy, occ_energy, (occ_band + later[0]).astype(jnp.float32)])
    others, other_turns, bit = [], [], cols // 2
    while bit > 2:
        held = jnp.concatenate([own, *others], axis=0) if others else own
        others.append(turned(held, "col", bit))
        other_turns += [turn + bit for turn in [0, *other_turns]]
        bit //= 2
    beside = turned(own, "col", bit)
    relayed = turned(jnp.concatenate(others, axis=0) if len(others) > 1 else others[0], "col", bit)
    first = sent(packed)
    middle = sent(pack([*others, beside], first[1:], targets, plan))
    last = sent(pack([relayed], [], targets, plan))

    def turns_of(target, turns):
        return [(target[0], target[1] ^ turn) for turn in turns]

    turns = [turns_of(target, [*other_turns, bit]) for target in targets]
    turns += [turns_of(target, [0, *[turn + bit for turn in other_turns]]) for target in targets]
    messages = middle + [message for pair in zip(first, last) for message in pair]
    kept, passed = join(messages, turns, levels, plan)
    return outer([kept, turned(passed, "row", 1)], plan)


def solution(mesh):
    placed = (P(("row", "col"), None, None), P(("row", "col"), None, None), P(), P(), P(), P())
    return jax.shard_map(
        on_device, mesh=mesh, in_specs=placed, out_specs=P("row", "col"), check_vma=False
    )
```

```python
import functools
import math

import jax
import jax.numpy as jnp
import numpy as np
from jax import lax
from jax.experimental import pallas as pl
from jax.experimental.pallas import tpu as pltpu
from jax.sharding import PartitionSpec as P

GMAX = 18
STEPS = 2
RADIX = 6
SPAN = 2 * GMAX + 1
KX_ROWS = 40
LANES = 128
OMEGA_SQUARED = 0.0625
TILE = 512
VMEM_LIMIT = 40 * 2**20


COSINE_TERMS = 10


def table_rows(grid):
    width = (grid // RADIX) * grid
    x_first = 4 * width
    return width, x_first, x_first + 2 * KX_ROWS


def cosine(phase, grid):
    phase = phase - (phase * 43691 >> 21) * 48
    angle = (phase - grid // 2).astype(jnp.float32) * np.float32(2.0 * math.pi / grid)
    square = angle * angle
    value = jnp.zeros_like(angle)
    for term in reversed(range(COSINE_TERMS)):
        value = value * square - np.float32((-1.0) ** term / math.factorial(2 * term))
    return value


def in_two(values):
    upper = values.astype(jnp.bfloat16)
    return upper, (values - upper.astype(jnp.float32)).astype(jnp.bfloat16)


def write_tables(grid, table_ref, twiddle_ref):
    width, x_first, x_end = table_rows(grid)
    quarter = grid // 4

    def counted(shape, dimension):
        return lax.broadcasted_iota(jnp.int32, shape, dimension)

    row, lane = counted((2 * KX_ROWS, LANES), 0), counted((2 * KX_ROWS, LANES), 1)
    below = (row >= KX_ROWS).astype(jnp.int32)
    place = jnp.where(lane >= grid, lane - grid, lane)
    place = jnp.where(place >= grid, 0, place)
    frequency = row - KX_ROWS * below + (grid - GMAX)
    upper, lower = in_two(cosine(frequency * place + quarter * below, grid))
    mixed = jnp.where(lane < grid, upper.astype(jnp.float32), lower.astype(jnp.float32))
    table_ref[x_first:x_end, :] = mixed.astype(jnp.bfloat16)

    row, lane = counted((16, width), 0), counted((16, width), 1)
    below = (row >= RADIX).astype(jnp.int32)
    residue = jnp.where(row >= 2 * RADIX, 0, row - RADIX * below)
    twiddle_ref[...] = cosine(residue * (lane * 43691 >> 21) + quarter * below, grid)

    lane = counted((1, LANES), 1)
    q = lane * 57 >> 10
    kz = lane - q * GMAX + 1
    y_phase = RADIX * (q + (grid // RADIX - GMAX // RADIX)) * counted((grid // RADIX, LANES), 0)
    z_phase = kz * counted((grid, LANES), 0)
    cos_y, sin_y = cosine(y_phase, grid), cosine(y_phase + 3 * quarter, grid)
    cos_z, sin_z = cosine(z_phase, grid), cosine(z_phase + 3 * quarter, grid)
    for y in range(grid // RADIX):
        cos_here, sin_here = cos_y[y : y + 1], sin_y[y : y + 1]
        whole = (cos_here * cos_z - sin_here * sin_z, -(sin_here * cos_z + cos_here * sin_z))
        for part, values in enumerate(whole):
            for level, piece in enumerate(in_two(values)):
                first = (2 * level + part) * width + y * grid
                table_ref[first : first + grid, :] = piece


def dft_six(re, im):
    half = 0.5
    root = math.sqrt(3.0) / 2.0
    s_re = [re[h] + re[h + 3] for h in range(3)]
    s_im = [im[h] + im[h + 3] for h in range(3)]
    d_re = [re[h] - re[h + 3] for h in range(3)]
    d_im = [im[h] - im[h + 3] for h in range(3)]
    out = [None] * 6
    sum_re, sum_im = s_re[1] + s_re[2], s_im[1] + s_im[2]
    dif_re, dif_im = (s_re[1] - s_re[2]) * root, (s_im[1] - s_im[2]) * root
    out[0] = (s_re[0] + sum_re, s_im[0] + sum_im)
    mid_re, mid_im = s_re[0] - half * sum_re, s_im[0] - half * sum_im
    out[2] = (mid_re + dif_im, mid_im - dif_re)
    out[4] = (mid_re - dif_im, mid_im + dif_re)
    sum_re, sum_im = (d_re[1] + d_re[2]) * root, (d_im[1] + d_im[2]) * root
    dif_re, dif_im = d_re[1] - d_re[2], d_im[1] - d_im[2]
    out[3] = (d_re[0] - dif_re, d_im[0] - dif_im)
    mid_re, mid_im = d_re[0] + half * dif_re, d_im[0] + half * dif_im
    out[1] = (mid_re + sum_im, mid_im - sum_re)
    out[5] = (mid_re - sum_im, mid_im + sum_re)
    return out


def dot(a, b):
    return jnp.dot(a, b, preferred_element_type=jnp.float32)


def own_place():
    return lax.axis_index("row"), lax.axis_index("col")


def spectrum_of(grid, cond, occ, table_ref, twiddle_ref):
    norm = np.float32(grid ** (-1.5))
    width, x_first, x_end = table_rows(grid)
    density = (cond.astype(jnp.float32) * occ.astype(jnp.float32)).astype(jnp.bfloat16)
    x_table = table_ref[x_first:x_end, : 2 * grid]
    section = dot(x_table, jnp.concatenate([density, density], axis=0))
    re = [section[:KX_ROWS, h * width : (h + 1) * width] for h in range(RADIX)]
    im = [section[KX_ROWS:, h * width : (h + 1) * width] for h in range(RADIX)]
    rows = []
    for residue, (d_re, d_im) in enumerate(dft_six(re, im)):
        if residue > 0:
            t_re = twiddle_ref[residue : residue + 1, :]
            t_im = twiddle_ref[RADIX + residue : RADIX + residue + 1, :]
            d_re, d_im = d_re * t_re - d_im * t_im, d_re * t_im + d_im * t_re
        rows.append(jnp.concatenate([d_re, d_im], axis=1))
    whole = jnp.concatenate(rows, axis=0)
    whole_hi = whole.astype(jnp.bfloat16)
    whole_lo = (whole - whole_hi.astype(jnp.float32)).astype(jnp.bfloat16)

    def rotation(first):
        cos_part = table_ref[first : first + width, :]
        sin_part = table_ref[first + width : first + 2 * width, :]
        upper = jnp.concatenate([cos_part, sin_part], axis=1)
        return jnp.concatenate([upper, jnp.concatenate([-sin_part, cos_part], axis=1)], axis=0)

    upper, lower = rotation(0), rotation(2 * width)
    spectrum = (dot(whole_hi, upper) + dot(whole_lo, upper) + dot(whole_hi, lower)) * norm
    parts = []
    for side in range(2):
        own = spectrum[:, side * LANES : (side + 1) * LANES]
        for group in range(RADIX // 2):
            first = 2 * group * KX_ROWS
            parts.append(jnp.concatenate([own[first : first + KX_ROWS], own[first + KX_ROWS : first + 2 * KX_ROWS]], axis=1))
    return jnp.concatenate(parts, axis=0).astype(jnp.bfloat16)


def pair_weights(sources, levels_ref):
    rows, cols = lax.axis_size("row"), lax.axis_size("col")
    r, _ = own_place()
    devices = rows * cols
    pairs = STEPS * len(sources)
    line = lax.broadcasted_iota(jnp.int32, (pairs, 1), 0)
    band = jnp.zeros((pairs, 1), jnp.int32)
    slot = jnp.zeros((pairs, 1), jnp.int32)
    for j, source in enumerate(sources):
        place = r * cols + source
        for step in range(STEPS):
            here = line == STEPS * j + step
            band = jnp.where(here, place, band)
            slot = jnp.where(here, lax.rem(place - step * cols + devices, devices), slot)
    lane = lax.broadcasted_iota(jnp.int32, (pairs, levels_ref.shape[1]), 1)

    def at(which, chosen):
        return jnp.sum(jnp.where(lane == chosen, levels_ref[which : which + 1, :], 0.0), axis=1, keepdims=True)

    gap = at(0, band) - at(1, at(2, slot).astype(jnp.int32))
    return -4.0 * gap / (gap * gap + OMEGA_SQUARED) / (devices * STEPS)


def first_kernel(grid, orbitals_ref, sphere_ref, cube_ref, places_ref, table_ref, twiddle_ref):
    half = grid // 2
    sx, sy, kz = sphere_ref[0:1, :], sphere_ref[1:2, :], sphere_ref[2:3, :]
    kx = jnp.where(sx >= half, sx - grid, sx) + GMAX
    ky = jnp.where(sy >= half, sy - grid, sy) + GMAX
    q = (ky * 43) >> 8
    residue = ky - q * RADIX
    places_ref[0:1, :] = (residue & 1) * LANES + q * GMAX + kz - 1
    places_ref[1:2, :] = (residue >> 1) * KX_ROWS + kx
    write_tables(grid, table_ref, twiddle_ref)
    cube_ref[...] = spectrum_of(grid, orbitals_ref[0], orbitals_ref[1], table_ref, twiddle_ref)


def pick(cube_ref, places_ref, coef_ref):
    groups = RADIX // 2 * KX_ROWS // 8
    half_count = places_ref.shape[1]
    counted = lax.broadcasted_iota(jnp.int32, (2 * LANES, TILE), 0).astype(jnp.float32).astype(jnp.bfloat16)
    line = lax.broadcasted_iota(jnp.int32, (8, TILE), 0)
    for first in range(0, half_count, TILE):
        here = slice(first, first + TILE)
        lane = places_ref[0:1, here].astype(jnp.float32).astype(jnp.bfloat16)
        row = places_ref[1:2, here]
        one_hot = jnp.where(counted == lane, jnp.bfloat16(1), jnp.bfloat16(0))
        found = dot(cube_ref[...], one_hot)
        away = line - row
        values = [jnp.zeros((8, TILE), jnp.float32)] * 4
        for group in range(groups):
            chosen = away == -8 * group
            for which in range(4):
                start = (which * groups + group) * 8
                values[which] = jnp.where(chosen, found[start : start + 8], values[which])
        for which in range(4):
            pair, side = divmod(which, 2)
            value = jnp.sum(values[which], axis=0, keepdims=True)
            coef_ref[pair : pair + 1, side * half_count + first : side * half_count + first + TILE] = value.astype(jnp.bfloat16)


def second_kernel(grid, orbitals_ref, occ_ref, first_ref, places_ref, table_ref, twiddle_ref, coef_ref, later_ref, cube_ref):
    later_ref[...] = jnp.zeros_like(later_ref)
    picks = RADIX * KX_ROWS
    cube_ref[:picks, :] = first_ref[...]
    cube_ref[picks:, :] = spectrum_of(grid, orbitals_ref[0], occ_ref[0], table_ref, twiddle_ref)
    pick(cube_ref, places_ref, coef_ref)


def cost(flops, data):
    return pl.CostEstimate(flops=flops, bytes_accessed=data, transcendentals=0)


def in_vmem(count):
    return [pl.BlockSpec(memory_space=pltpu.VMEM)] * count


def transform(cond_orbitals, occ_orbitals, occ_second, sphere_index, band_shape):
    grid = cond_orbitals.shape[1]
    half_count = sphere_index.shape[1]
    width, _, table_count = table_rows(grid)
    orbitals = jnp.concatenate([cond_orbitals, occ_orbitals], axis=0)
    picks = RADIX * KX_ROWS
    params = dict(
        compiler_params=pltpu.CompilerParams(vmem_limit_bytes=VMEM_LIMIT),
        cost_estimate=cost(2 * 10**9, 2 * 10**6),
    )
    handed = pl.pallas_call(
        functools.partial(first_kernel, grid),
        out_shape=[
            jax.ShapeDtypeStruct((picks, 2 * LANES), jnp.bfloat16),
            jax.ShapeDtypeStruct((2, half_count), jnp.int32),
            jax.ShapeDtypeStruct((table_count, LANES), jnp.bfloat16),
            jax.ShapeDtypeStruct((16, width), jnp.float32),
        ],
        in_specs=in_vmem(2),
        out_specs=in_vmem(4),
        name="first_pair",
        **params,
    )(orbitals, sphere_index)
    return pl.pallas_call(
        functools.partial(second_kernel, grid),
        out_shape=[
            jax.ShapeDtypeStruct((STEPS, 2 * half_count), jnp.bfloat16),
            jax.ShapeDtypeStruct((1, *band_shape), jnp.int32),
        ],
        in_specs=in_vmem(6),
        out_specs=in_vmem(2),
        scratch_shapes=[pltpu.VMEM((STEPS * picks, 2 * LANES), jnp.bfloat16)],
        name="second_pair",
        **params,
    )(orbitals, occ_second, *handed)


def pack_kernel(plan, turns, targets, merged, levels_ref, *refs):
    rows, cols, row_width, col_width = plan
    count = len(refs) - len(targets) - 1 - merged
    arrived, outs, mixed_ref = refs[:count], refs[count:-1], refs[-1]
    r, c = own_place()
    first = 0
    for ref in arrived:
        mixed_ref[first : first + ref.shape[0], :] = ref[...].astype(jnp.float32)
        first += ref.shape[0]
    if merged:
        outs[-1][...] = mixed_ref[...].astype(jnp.bfloat16)
    weight = pair_weights([c ^ turn for turn in turns], levels_ref)
    columns = []
    for side in range(2):
        start = pl.multiple_of((c ^ side) * col_width, LANES)
        columns.append((weight * mixed_ref[:, pl.ds(start, col_width)]).astype(jnp.bfloat16))
    for (turn, side), out_ref in zip(targets, outs):
        start = pl.multiple_of((r ^ turn) // 2 * (2 * row_width), LANES)
        out_ref[:, : 2 * row_width] = mixed_ref[:, pl.ds(start, 2 * row_width)].astype(jnp.bfloat16)
        out_ref[:, 2 * row_width :] = columns[side]


def pack(arrived, levels, turns, targets, merged, plan):
    rows, cols, row_width, col_width = plan
    pairs = STEPS * len(turns)
    entries = arrived[0].shape[1]
    shapes = [(pairs, 2 * row_width + col_width)] * len(targets) + [(pairs, entries)] * merged
    return pl.pallas_call(
        functools.partial(pack_kernel, plan, turns, targets, merged),
        out_shape=[jax.ShapeDtypeStruct(shape, jnp.bfloat16) for shape in shapes],
        in_specs=in_vmem(1 + len(arrived)),
        out_specs=in_vmem(len(shapes)),
        scratch_shapes=[pltpu.VMEM((pairs, entries), jnp.float32)],
        compiler_params=pltpu.CompilerParams(vmem_limit_bytes=VMEM_LIMIT),
        cost_estimate=cost(10**9, 10**6),
        name="pack",
    )(levels, *arrived)


def stacked(refs, lanes):
    return jnp.concatenate([ref[:, lanes].astype(jnp.float32) for ref in refs], axis=0).astype(jnp.bfloat16)


def join_kernel(row_width, *refs):
    messages, outs = refs[:-2], refs[-2:]
    depth = messages[0].shape[0]
    merge = max(1, 16 // depth)
    r, _ = own_place()
    for j in range(0, len(messages), merge):
        here = slice(depth * j, depth * (j + merge))
        columns = stacked(messages[j : j + merge], slice(2 * row_width, None))
        for side, out_ref in enumerate(outs):
            lanes = pl.ds(pl.multiple_of((r & 1 ^ side) * row_width, LANES), row_width)
            out_ref[here, :row_width] = stacked(messages[j : j + merge], lanes)
            out_ref[here, row_width:] = columns


def join(messages, plan):
    rows, cols, row_width, col_width = plan
    depth = messages[0].shape[0]
    return pl.pallas_call(
        functools.partial(join_kernel, row_width),
        out_shape=[jax.ShapeDtypeStruct((depth * len(messages), row_width + col_width), jnp.bfloat16)] * 2,
        in_specs=in_vmem(len(messages)),
        out_specs=in_vmem(2),
        compiler_params=pltpu.CompilerParams(vmem_limit_bytes=VMEM_LIMIT),
        cost_estimate=cost(10**9, 10**6),
        name="join",
    )(*messages)


def outer_kernel(row_width, block, slots, *refs):
    messages, (out_ref, right_ref, held_ref, sems) = refs[:-4], refs[-4:]
    depth = messages[0].shape[0]
    for j, ref in enumerate(messages):
        right_ref[depth * j : depth * (j + 1), :] = ref[:, row_width:]
    count = row_width // block

    def copy_out(i, slot):
        rows = pl.ds(pl.multiple_of(i * block, block), block)
        return pltpu.make_async_copy(held_ref.at[slot], out_ref.at[rows], sems.at[slot])

    def step(i, carry):
        slot = lax.rem(i, slots)

        @pl.when(i >= slots)
        def _():
            copy_out(i - slots, slot).wait()

        here = pl.ds(pl.multiple_of(i * block, block), block)
        left = jnp.concatenate([ref[:, here] for ref in messages], axis=0)
        held_ref[slot] = lax.dot_general(left, right_ref[...], (((0,), (0,)), ((), ())), preferred_element_type=jnp.float32)
        copy_out(i, slot).start()
        return carry

    lax.fori_loop(0, count, step, 0)
    for i in range(max(0, count - slots), count):
        copy_out(i, i % slots).wait()


def outer(messages, plan):
    rows, cols, row_width, col_width = plan
    depth = messages[0].shape[0]
    block = min(256, row_width)
    slots = min(4, row_width // block)
    return pl.pallas_call(
        functools.partial(outer_kernel, row_width, block, slots),
        out_shape=jax.ShapeDtypeStruct((row_width, col_width), jnp.float32),
        in_specs=in_vmem(len(messages)),
        out_specs=pl.BlockSpec(memory_space=pltpu.HBM),
        scratch_shapes=[
            pltpu.VMEM((depth * len(messages), col_width), jnp.bfloat16),
            pltpu.VMEM((slots, block, col_width), jnp.float32),
            pltpu.SemaphoreType.DMA((slots,)),
        ],
        compiler_params=pltpu.CompilerParams(vmem_limit_bytes=VMEM_LIMIT),
        cost_estimate=cost(10**10, 3 * 10**7),
        name="outer",
    )(*messages)


def shifted(value, axis, by):
    devices = lax.axis_size(axis)
    return lax.ppermute(value, axis, [(i, (i + by) % devices) for i in range(devices)])


def turned(value, axis, turn):
    devices = lax.axis_size(axis)
    return lax.ppermute(value, axis, [(i, i ^ turn) for i in range(devices)])


def sent_across(value, turn, side, rows, cols):
    moves = [(r * cols + c, (r ^ turn) * cols + (c ^ side)) for r in range(rows) for c in range(cols)]
    return lax.ppermute(value, ("row", "col"), moves)


def on_device(cond_orbitals, occ_orbitals, cond_energy, occ_energy, occ_band, sphere_index):
    rows = lax.axis_size("row")
    cols = lax.axis_size("col")
    entries = 2 * sphere_index.shape[1]
    plan = (rows, cols, entries // rows, entries // cols)
    occ_second = shifted(occ_orbitals, "row", 1)
    own, later = transform(cond_orbitals, occ_orbitals, occ_second, sphere_index, occ_band.shape)
    levels = jnp.stack([cond_energy, occ_energy, (occ_band + later[0]).astype(jnp.float32)])
    targets = [(0, 0)] + [(turn, side) for side in (1, 0) for turn in range(rows - 2, -2, -2) if turn or side]
    targets.append(targets.pop(rows // 2))

    def sent(packed):
        return [packed[0]] + [sent_across(value, *target, rows, cols) for value, target in zip(packed[1:], targets[1:])]

    held, turns, bit = [own], [0], cols // 2
    while bit > 2:
        if len(held) > 1:
            held = [jnp.concatenate(held, axis=0)]
        held.append(turned(held[0], "col", bit))
        turns += [turn + bit for turn in turns]
        bit //= 2
    *packed, merged = pack(held, levels, turns, targets, 1, plan)
    messages = sent(packed)
    far = turned(merged, "col", bit)
    messages += sent(pack([far], levels, [turn + bit for turn in turns], targets, 0, plan))
    kept, passed = join(messages, plan)
    return outer([kept, turned(passed, "row", 1)], plan)


def solution(mesh):
    placed = (P(("row", "col"), None, None), P(("row", "col"), None, None), P(), P(), P(), P())
    return jax.shard_map(
        on_device, mesh=mesh, in_specs=placed, out_specs=P("row", "col"), check_vma=False
    )
```

```python
import functools
import math

import jax
import jax.numpy as jnp
import numpy as np
from jax import lax
from jax.experimental import pallas as pl
from jax.experimental.pallas import tpu as pltpu
from jax.sharding import PartitionSpec as P

GMAX = 18
STEPS = 2
RADIX = 6
SPAN = 2 * GMAX + 1
KX_ROWS = 40
LANES = 128
OMEGA_SQUARED = 0.0625
TILE = 512
VMEM_LIMIT = 40 * 2**20


COSINE_TERMS = 10


def table_rows(grid):
    width = (grid // RADIX) * grid
    x_first = 4 * width
    return width, x_first, x_first + 2 * KX_ROWS


def cosine(phase, grid):
    phase = phase - (phase * 43691 >> 21) * 48
    angle = (phase - grid // 2).astype(jnp.float32) * np.float32(2.0 * math.pi / grid)
    square = angle * angle
    value = jnp.zeros_like(angle)
    for term in reversed(range(COSINE_TERMS)):
        value = value * square - np.float32((-1.0) ** term / math.factorial(2 * term))
    return value


def in_two(values):
    upper = values.astype(jnp.bfloat16)
    return upper, (values - upper.astype(jnp.float32)).astype(jnp.bfloat16)


def write_tables(grid, table_ref, twiddle_ref):
    width, x_first, x_end = table_rows(grid)
    quarter = grid // 4

    def counted(shape, dimension):
        return lax.broadcasted_iota(jnp.int32, shape, dimension)

    row, lane = counted((2 * KX_ROWS, LANES), 0), counted((2 * KX_ROWS, LANES), 1)
    below = (row >= KX_ROWS).astype(jnp.int32)
    place = jnp.where(lane >= grid, lane - grid, lane)
    place = jnp.where(place >= grid, 0, place)
    frequency = row - KX_ROWS * below + (grid - GMAX)
    upper, lower = in_two(cosine(frequency * place + quarter * below, grid))
    mixed = jnp.where(lane < grid, upper.astype(jnp.float32), lower.astype(jnp.float32))
    table_ref[x_first:x_end, :] = mixed.astype(jnp.bfloat16)

    row, lane = counted((16, width), 0), counted((16, width), 1)
    below = (row >= RADIX).astype(jnp.int32)
    residue = jnp.where(row >= 2 * RADIX, 0, row - RADIX * below)
    twiddle_ref[...] = cosine(residue * (lane * 43691 >> 21) + quarter * below, grid)

    lane = counted((1, LANES), 1)
    q = lane * 57 >> 10
    kz = lane - q * GMAX + 1
    y_phase = RADIX * (q + (grid // RADIX - GMAX // RADIX)) * counted((grid // RADIX, LANES), 0)
    z_phase = kz * counted((grid, LANES), 0)
    cos_y, sin_y = cosine(y_phase, grid), cosine(y_phase + 3 * quarter, grid)
    cos_z, sin_z = cosine(z_phase, grid), cosine(z_phase + 3 * quarter, grid)
    for y in range(grid // RADIX):
        cos_here, sin_here = cos_y[y : y + 1], sin_y[y : y + 1]
        whole = (cos_here * cos_z - sin_here * sin_z, -(sin_here * cos_z + cos_here * sin_z))
        for part, values in enumerate(whole):
            for level, piece in enumerate(in_two(values)):
                first = (2 * level + part) * width + y * grid
                table_ref[first : first + grid, :] = piece


def dft_six(re, im):
    half = 0.5
    root = math.sqrt(3.0) / 2.0
    s_re = [re[h] + re[h + 3] for h in range(3)]
    s_im = [im[h] + im[h + 3] for h in range(3)]
    d_re = [re[h] - re[h + 3] for h in range(3)]
    d_im = [im[h] - im[h + 3] for h in range(3)]
    out = [None] * 6
    sum_re, sum_im = s_re[1] + s_re[2], s_im[1] + s_im[2]
    dif_re, dif_im = (s_re[1] - s_re[2]) * root, (s_im[1] - s_im[2]) * root
    out[0] = (s_re[0] + sum_re, s_im[0] + sum_im)
    mid_re, mid_im = s_re[0] - half * sum_re, s_im[0] - half * sum_im
    out[2] = (mid_re + dif_im, mid_im - dif_re)
    out[4] = (mid_re - dif_im, mid_im + dif_re)
    sum_re, sum_im = (d_re[1] + d_re[2]) * root, (d_im[1] + d_im[2]) * root
    dif_re, dif_im = d_re[1] - d_re[2], d_im[1] - d_im[2]
    out[3] = (d_re[0] - dif_re, d_im[0] - dif_im)
    mid_re, mid_im = d_re[0] + half * dif_re, d_im[0] + half * dif_im
    out[1] = (mid_re + sum_im, mid_im - sum_re)
    out[5] = (mid_re - sum_im, mid_im + sum_re)
    return out


def dot(a, b):
    return jnp.dot(a, b, preferred_element_type=jnp.float32)


def own_place():
    return lax.axis_index("row"), lax.axis_index("col")


def spectrum_of(grid, cond, occ, table_ref, twiddle_ref):
    norm = np.float32(grid ** (-1.5))
    width, x_first, x_end = table_rows(grid)
    density = (cond.astype(jnp.float32) * occ.astype(jnp.float32)).astype(jnp.bfloat16)
    x_table = table_ref[x_first:x_end, : 2 * grid]
    section = dot(x_table, jnp.concatenate([density, density], axis=0))
    re = [section[:KX_ROWS, h * width : (h + 1) * width] for h in range(RADIX)]
    im = [section[KX_ROWS:, h * width : (h + 1) * width] for h in range(RADIX)]
    rows = []
    for residue, (d_re, d_im) in enumerate(dft_six(re, im)):
        if residue > 0:
            t_re = twiddle_ref[residue : residue + 1, :]
            t_im = twiddle_ref[RADIX + residue : RADIX + residue + 1, :]
            d_re, d_im = d_re * t_re - d_im * t_im, d_re * t_im + d_im * t_re
        rows.append(jnp.concatenate([d_re, d_im], axis=1))
    whole = jnp.concatenate(rows, axis=0)
    whole_hi = whole.astype(jnp.bfloat16)
    whole_lo = (whole - whole_hi.astype(jnp.float32)).astype(jnp.bfloat16)

    def rotation(first):
        cos_part = table_ref[first : first + width, :]
        sin_part = table_ref[first + width : first + 2 * width, :]
        upper = jnp.concatenate([cos_part, sin_part], axis=1)
        return jnp.concatenate([upper, jnp.concatenate([-sin_part, cos_part], axis=1)], axis=0)

    upper, lower = rotation(0), rotation(2 * width)
    spectrum = (dot(whole_hi, upper) + dot(whole_lo, upper) + dot(whole_hi, lower)) * norm
    parts = []
    for side in range(2):
        own = spectrum[:, side * LANES : (side + 1) * LANES]
        for group in range(RADIX // 2):
            first = 2 * group * KX_ROWS
            parts.append(jnp.concatenate([own[first : first + KX_ROWS], own[first + KX_ROWS : first + 2 * KX_ROWS]], axis=1))
    return jnp.concatenate(parts, axis=0).astype(jnp.bfloat16)


def pair_weights(sources, levels_ref):
    rows, cols = lax.axis_size("row"), lax.axis_size("col")
    r, _ = own_place()
    devices = rows * cols
    pairs = STEPS * len(sources)
    line = lax.broadcasted_iota(jnp.int32, (pairs, 1), 0)
    band = jnp.zeros((pairs, 1), jnp.int32)
    slot = jnp.zeros((pairs, 1), jnp.int32)
    for j, source in enumerate(sources):
        place = r * cols + source
        for step in range(STEPS):
            here = line == STEPS * j + step
            band = jnp.where(here, place, band)
            slot = jnp.where(here, lax.rem(place - step * cols + devices, devices), slot)
    lane = lax.broadcasted_iota(jnp.int32, (pairs, levels_ref.shape[1]), 1)

    def at(which, chosen):
        return jnp.sum(jnp.where(lane == chosen, levels_ref[which : which + 1, :], 0.0), axis=1, keepdims=True)

    gap = at(0, band) - at(1, at(2, slot).astype(jnp.int32))
    return -4.0 * gap / (gap * gap + OMEGA_SQUARED) / (devices * STEPS)


def first_kernel(grid, orbitals_ref, sphere_ref, coef_ref, places_ref, table_ref, twiddle_ref, cube_ref):
    half = grid // 2
    sx, sy, kz = sphere_ref[0:1, :], sphere_ref[1:2, :], sphere_ref[2:3, :]
    kx = jnp.where(sx >= half, sx - grid, sx) + GMAX
    ky = jnp.where(sy >= half, sy - grid, sy) + GMAX
    q = (ky * 43) >> 8
    residue = ky - q * RADIX
    places_ref[0:1, :] = (residue & 1) * LANES + q * GMAX + kz - 1
    places_ref[1:2, :] = (residue >> 1) * KX_ROWS + kx
    write_tables(grid, table_ref, twiddle_ref)
    cube_ref[...] = spectrum_of(grid, orbitals_ref[0], orbitals_ref[1], table_ref, twiddle_ref)
    pick(cube_ref, places_ref, coef_ref, 0)


def pick(cube_ref, places_ref, coef_ref, pair):
    groups = RADIX // 2 * KX_ROWS // 8
    half_count = places_ref.shape[1]
    counted = lax.broadcasted_iota(jnp.int32, (2 * LANES, TILE), 0).astype(jnp.float32).astype(jnp.bfloat16)
    line = lax.broadcasted_iota(jnp.int32, (8, TILE), 0)
    for first in range(0, half_count, TILE):
        here = slice(first, first + TILE)
        lane = places_ref[0:1, here].astype(jnp.float32).astype(jnp.bfloat16)
        one_hot = jnp.where(counted == lane, jnp.bfloat16(1), jnp.bfloat16(0))
        found = dot(cube_ref[...], one_hot)
        away = line - places_ref[1:2, here]
        values = [jnp.zeros((8, TILE), jnp.float32)] * 2
        for group in range(groups):
            chosen = away == -8 * group
            for side in range(2):
                start = (side * groups + group) * 8
                values[side] = jnp.where(chosen, found[start : start + 8], values[side])
        for side in range(2):
            value = jnp.sum(values[side], axis=0, keepdims=True).astype(jnp.bfloat16)
            coef_ref[pair : pair + 1, side * half_count + first : side * half_count + first + TILE] = value


def second_kernel(grid, orbitals_ref, occ_ref, first_ref, places_ref, table_ref, twiddle_ref, coef_ref, later_ref, cube_ref):
    later_ref[...] = jnp.zeros_like(later_ref)
    coef_ref[0:1, :] = first_ref[...]
    cube_ref[...] = spectrum_of(grid, orbitals_ref[0], occ_ref[0], table_ref, twiddle_ref)
    pick(cube_ref, places_ref, coef_ref, 1)


def cost(flops, data):
    return pl.CostEstimate(flops=flops, bytes_accessed=data, transcendentals=0)


def in_vmem(count):
    return [pl.BlockSpec(memory_space=pltpu.VMEM)] * count


def transform(cond_orbitals, occ_orbitals, occ_second, sphere_index, band_shape):
    grid = cond_orbitals.shape[1]
    half_count = sphere_index.shape[1]
    width, _, table_count = table_rows(grid)
    orbitals = jnp.concatenate([cond_orbitals, occ_orbitals], axis=0)
    cube = pltpu.VMEM((RADIX * KX_ROWS, 2 * LANES), jnp.bfloat16)
    params = dict(
        scratch_shapes=[cube],
        compiler_params=pltpu.CompilerParams(vmem_limit_bytes=VMEM_LIMIT),
        cost_estimate=cost(2 * 10**9, 2 * 10**6),
    )
    handed = pl.pallas_call(
        functools.partial(first_kernel, grid),
        out_shape=[
            jax.ShapeDtypeStruct((1, 2 * half_count), jnp.bfloat16),
            jax.ShapeDtypeStruct((2, half_count), jnp.int32),
            jax.ShapeDtypeStruct((table_count, LANES), jnp.bfloat16),
            jax.ShapeDtypeStruct((16, width), jnp.float32),
        ],
        in_specs=in_vmem(2),
        out_specs=in_vmem(4),
        name="first_pair",
        **params,
    )(orbitals, sphere_index)
    return pl.pallas_call(
        functools.partial(second_kernel, grid),
        out_shape=[
            jax.ShapeDtypeStruct((STEPS, 2 * half_count), jnp.bfloat16),
            jax.ShapeDtypeStruct((1, *band_shape), jnp.int32),
        ],
        in_specs=in_vmem(6),
        out_specs=in_vmem(2),
        name="second_pair",
        **params,
    )(orbitals, occ_second, *handed)


def pack_kernel(plan, turns, targets, merged, levels_ref, *refs):
    rows, cols, row_width, col_width = plan
    count = len(refs) - len(targets) - 1 - merged
    arrived, outs, mixed_ref = refs[:count], refs[count:-1], refs[-1]
    r, c = own_place()
    first = 0
    for ref in arrived:
        mixed_ref[first : first + ref.shape[0], :] = ref[...].astype(jnp.float32)
        first += ref.shape[0]
    if merged:
        outs[-1][...] = mixed_ref[...].astype(jnp.bfloat16)
    weight = pair_weights([c ^ turn for turn in turns], levels_ref)
    columns = []
    for side in range(2):
        start = pl.multiple_of((c ^ side) * col_width, LANES)
        columns.append((weight * mixed_ref[:, pl.ds(start, col_width)]).astype(jnp.bfloat16))
    for (turn, side), out_ref in zip(targets, outs):
        start = pl.multiple_of((r ^ turn) // 2 * (2 * row_width), LANES)
        out_ref[:, : 2 * row_width] = mixed_ref[:, pl.ds(start, 2 * row_width)].astype(jnp.bfloat16)
        out_ref[:, 2 * row_width :] = columns[side]


def pack(arrived, levels, turns, targets, merged, plan):
    rows, cols, row_width, col_width = plan
    pairs = STEPS * len(turns)
    entries = arrived[0].shape[1]
    shapes = [(pairs, 2 * row_width + col_width)] * len(targets) + [(pairs, entries)] * merged
    return pl.pallas_call(
        functools.partial(pack_kernel, plan, turns, targets, merged),
        out_shape=[jax.ShapeDtypeStruct(shape, jnp.bfloat16) for shape in shapes],
        in_specs=in_vmem(1 + len(arrived)),
        out_specs=in_vmem(len(shapes)),
        scratch_shapes=[pltpu.VMEM((pairs, entries), jnp.float32)],
        compiler_params=pltpu.CompilerParams(vmem_limit_bytes=VMEM_LIMIT),
        cost_estimate=cost(10**9, 10**6),
        name="pack",
    )(levels, *arrived)


def stacked(refs, lanes):
    return jnp.concatenate([ref[:, lanes].astype(jnp.float32) for ref in refs], axis=0).astype(jnp.bfloat16)


def join_kernel(row_width, *refs):
    messages, outs = refs[:-2], refs[-2:]
    depth = messages[0].shape[0]
    merge = max(1, 16 // depth)
    r, _ = own_place()
    for j in range(0, len(messages), merge):
        here = slice(depth * j, depth * (j + merge))
        columns = stacked(messages[j : j + merge], slice(2 * row_width, None))
        for side, out_ref in enumerate(outs):
            lanes = pl.ds(pl.multiple_of((r & 1 ^ side) * row_width, LANES), row_width)
            out_ref[here, :row_width] = stacked(messages[j : j + merge], lanes)
            out_ref[here, row_width:] = columns


def join(messages, plan):
    rows, cols, row_width, col_width = plan
    depth = messages[0].shape[0]
    return pl.pallas_call(
        functools.partial(join_kernel, row_width),
        out_shape=[jax.ShapeDtypeStruct((depth * len(messages), row_width + col_width), jnp.bfloat16)] * 2,
        in_specs=in_vmem(len(messages)),
        out_specs=in_vmem(2),
        compiler_params=pltpu.CompilerParams(vmem_limit_bytes=VMEM_LIMIT),
        cost_estimate=cost(10**9, 10**6),
        name="join",
    )(*messages)


def outer_kernel(row_width, block, slots, *refs):
    messages, (out_ref, right_ref, held_ref, sems) = refs[:-4], refs[-4:]
    depth = messages[0].shape[0]
    for j, ref in enumerate(messages):
        right_ref[depth * j : depth * (j + 1), :] = ref[:, row_width:]
    count = row_width // block

    def copy_out(i, slot):
        rows = pl.ds(pl.multiple_of(i * block, block), block)
        return pltpu.make_async_copy(held_ref.at[slot], out_ref.at[rows], sems.at[slot])

    def step(i, carry):
        slot = lax.rem(i, slots)

        @pl.when(i >= slots)
        def _():
            copy_out(i - slots, slot).wait()

        here = pl.ds(pl.multiple_of(i * block, block), block)
        left = jnp.concatenate([ref[:, here] for ref in messages], axis=0)
        held_ref[slot] = lax.dot_general(left, right_ref[...], (((0,), (0,)), ((), ())), preferred_element_type=jnp.float32)
        copy_out(i, slot).start()
        return carry

    lax.fori_loop(0, count, step, 0)
    for i in range(max(0, count - slots), count):
        copy_out(i, i % slots).wait()


def outer(messages, plan):
    rows, cols, row_width, col_width = plan
    depth = messages[0].shape[0]
    block = min(256, row_width)
    slots = min(4, row_width // block)
    return pl.pallas_call(
        functools.partial(outer_kernel, row_width, block, slots),
        out_shape=jax.ShapeDtypeStruct((row_width, col_width), jnp.float32),
        in_specs=in_vmem(len(messages)),
        out_specs=pl.BlockSpec(memory_space=pltpu.HBM),
        scratch_shapes=[
            pltpu.VMEM((depth * len(messages), col_width), jnp.bfloat16),
            pltpu.VMEM((slots, block, col_width), jnp.float32),
            pltpu.SemaphoreType.DMA((slots,)),
        ],
        compiler_params=pltpu.CompilerParams(vmem_limit_bytes=VMEM_LIMIT),
        cost_estimate=cost(10**10, 3 * 10**7),
        name="outer",
    )(*messages)


def shifted(value, axis, by):
    devices = lax.axis_size(axis)
    return lax.ppermute(value, axis, [(i, (i + by) % devices) for i in range(devices)])


def turned(value, axis, turn):
    devices = lax.axis_size(axis)
    return lax.ppermute(value, axis, [(i, i ^ turn) for i in range(devices)])


def sent_across(value, turn, side, rows, cols):
    moves = [(r * cols + c, (r ^ turn) * cols + (c ^ side)) for r in range(rows) for c in range(cols)]
    return lax.ppermute(value, ("row", "col"), moves)


def on_device(cond_orbitals, occ_orbitals, cond_energy, occ_energy, occ_band, sphere_index):
    rows = lax.axis_size("row")
    cols = lax.axis_size("col")
    entries = 2 * sphere_index.shape[1]
    plan = (rows, cols, entries // rows, entries // cols)
    occ_second = shifted(occ_orbitals, "row", 1)
    own, later = transform(cond_orbitals, occ_orbitals, occ_second, sphere_index, occ_band.shape)
    levels = jnp.stack([cond_energy, occ_energy, (occ_band + later[0]).astype(jnp.float32)])
    targets = [(0, 0)] + [(turn, side) for side in (1, 0) for turn in range(rows - 2, -2, -2) if turn or side]
    targets.append(targets.pop(rows // 2))

    def sent(packed):
        return [packed[0]] + [sent_across(value, *target, rows, cols) for value, target in zip(packed[1:], targets[1:])]

    held, turns, bit = [own], [0], cols // 2
    while bit > 2:
        if len(held) > 1:
            held = [jnp.concatenate(held, axis=0)]
        held.append(turned(held[0], "col", bit))
        turns += [turn + bit for turn in turns]
        bit //= 2
    *packed, merged = pack(held, levels, turns, targets, 1, plan)
    messages = sent(packed)
    far = turned(merged, "col", bit)
    messages += sent(pack([far], levels, [turn + bit for turn in turns], targets, 0, plan))
    kept, passed = join(messages, plan)
    return outer([kept, turned(passed, "row", 1)], plan)


def solution(mesh):
    placed = (P(("row", "col"), None, None), P(("row", "col"), None, None), P(), P(), P(), P())
    return jax.shard_map(
        on_device, mesh=mesh, in_specs=placed, out_specs=P("row", "col"), check_vma=False
    )
```

```python
import functools
import math

import jax
import jax.numpy as jnp
import numpy as np
from jax import lax
from jax.experimental import pallas as pl
from jax.experimental.pallas import tpu as pltpu
from jax.sharding import PartitionSpec as P

GMAX = 18
STEPS = 2
RADIX = 6
SPAN = 2 * GMAX + 1
KX_ROWS = 40
LANES = 128
OMEGA_SQUARED = 0.0625
TILE = 512
VMEM_LIMIT = 40 * 2**20


COSINE_TERMS = 10


def table_rows(grid):
    width = (grid // RADIX) * grid
    x_first = 4 * width
    return width, x_first, x_first + 2 * KX_ROWS


def cosine(phase, grid):
    phase = phase - (phase * 43691 >> 21) * 48
    angle = (phase - grid // 2).astype(jnp.float32) * np.float32(2.0 * math.pi / grid)
    square = angle * angle
    value = jnp.zeros_like(angle)
    for term in reversed(range(COSINE_TERMS)):
        value = value * square - np.float32((-1.0) ** term / math.factorial(2 * term))
    return value


def in_two(values):
    upper = values.astype(jnp.bfloat16)
    return upper, (values - upper.astype(jnp.float32)).astype(jnp.bfloat16)


def write_tables(grid, table_ref, twiddle_ref):
    width, x_first, x_end = table_rows(grid)
    quarter = grid // 4

    def counted(shape, dimension):
        return lax.broadcasted_iota(jnp.int32, shape, dimension)

    row, lane = counted((2 * KX_ROWS, LANES), 0), counted((2 * KX_ROWS, LANES), 1)
    below = (row >= KX_ROWS).astype(jnp.int32)
    place = jnp.where(lane >= grid, lane - grid, lane)
    place = jnp.where(place >= grid, 0, place)
    frequency = row - KX_ROWS * below + (grid - GMAX)
    upper, lower = in_two(cosine(frequency * place + quarter * below, grid))
    mixed = jnp.where(lane < grid, upper.astype(jnp.float32), lower.astype(jnp.float32))
    table_ref[x_first:x_end, :] = mixed.astype(jnp.bfloat16)

    row, lane = counted((16, width), 0), counted((16, width), 1)
    below = (row >= RADIX).astype(jnp.int32)
    residue = jnp.where(row >= 2 * RADIX, 0, row - RADIX * below)
    twiddle_ref[...] = cosine(residue * (lane * 43691 >> 21) + quarter * below, grid)

    lane = counted((1, LANES), 1)
    q = lane * 57 >> 10
    kz = lane - q * GMAX + 1
    y_phase = RADIX * (q + (grid // RADIX - GMAX // RADIX)) * counted((grid // RADIX, LANES), 0)
    z_phase = kz * counted((grid, LANES), 0)
    cos_y, sin_y = cosine(y_phase, grid), cosine(y_phase + 3 * quarter, grid)
    cos_z, sin_z = cosine(z_phase, grid), cosine(z_phase + 3 * quarter, grid)
    for y in range(grid // RADIX):
        cos_here, sin_here = cos_y[y : y + 1], sin_y[y : y + 1]
        whole = (cos_here * cos_z - sin_here * sin_z, -(sin_here * cos_z + cos_here * sin_z))
        for part, values in enumerate(whole):
            for level, piece in enumerate(in_two(values)):
                first = (2 * level + part) * width + y * grid
                table_ref[first : first + grid, :] = piece


def dft_six(re, im):
    half = 0.5
    root = math.sqrt(3.0) / 2.0
    s_re = [re[h] + re[h + 3] for h in range(3)]
    s_im = [im[h] + im[h + 3] for h in range(3)]
    d_re = [re[h] - re[h + 3] for h in range(3)]
    d_im = [im[h] - im[h + 3] for h in range(3)]
    out = [None] * 6
    sum_re, sum_im = s_re[1] + s_re[2], s_im[1] + s_im[2]
    dif_re, dif_im = (s_re[1] - s_re[2]) * root, (s_im[1] - s_im[2]) * root
    out[0] = (s_re[0] + sum_re, s_im[0] + sum_im)
    mid_re, mid_im = s_re[0] - half * sum_re, s_im[0] - half * sum_im
    out[2] = (mid_re + dif_im, mid_im - dif_re)
    out[4] = (mid_re - dif_im, mid_im + dif_re)
    sum_re, sum_im = (d_re[1] + d_re[2]) * root, (d_im[1] + d_im[2]) * root
    dif_re, dif_im = d_re[1] - d_re[2], d_im[1] - d_im[2]
    out[3] = (d_re[0] - dif_re, d_im[0] - dif_im)
    mid_re, mid_im = d_re[0] + half * dif_re, d_im[0] + half * dif_im
    out[1] = (mid_re + sum_im, mid_im - sum_re)
    out[5] = (mid_re - sum_im, mid_im + sum_re)
    return out


def dot(a, b):
    return jnp.dot(a, b, preferred_element_type=jnp.float32)


def own_place():
    return lax.axis_index("row"), lax.axis_index("col")


def spectrum_of(grid, cond, occ, table_ref, twiddle_ref):
    norm = np.float32(grid ** (-1.5))
    width, x_first, x_end = table_rows(grid)
    density = (cond.astype(jnp.float32) * occ.astype(jnp.float32)).astype(jnp.bfloat16)
    x_table = table_ref[x_first:x_end, : 2 * grid]
    section = dot(x_table, jnp.concatenate([density, density], axis=0))
    re = [section[:KX_ROWS, h * width : (h + 1) * width] for h in range(RADIX)]
    im = [section[KX_ROWS:, h * width : (h + 1) * width] for h in range(RADIX)]
    rows = []
    for residue, (d_re, d_im) in enumerate(dft_six(re, im)):
        if residue > 0:
            t_re = twiddle_ref[residue : residue + 1, :]
            t_im = twiddle_ref[RADIX + residue : RADIX + residue + 1, :]
            d_re, d_im = d_re * t_re - d_im * t_im, d_re * t_im + d_im * t_re
        rows.append(jnp.concatenate([d_re, d_im], axis=1))
    whole = jnp.concatenate(rows, axis=0)
    whole_hi = whole.astype(jnp.bfloat16)
    whole_lo = (whole - whole_hi.astype(jnp.float32)).astype(jnp.bfloat16)

    def rotation(first):
        cos_part = table_ref[first : first + width, :]
        sin_part = table_ref[first + width : first + 2 * width, :]
        upper = jnp.concatenate([cos_part, sin_part], axis=1)
        return jnp.concatenate([upper, jnp.concatenate([-sin_part, cos_part], axis=1)], axis=0)

    upper, lower = rotation(0), rotation(2 * width)
    spectrum = (dot(whole_hi, upper) + dot(whole_lo, upper) + dot(whole_hi, lower)) * norm
    parts = []
    for side in range(2):
        own = spectrum[:, side * LANES : (side + 1) * LANES]
        for group in range(RADIX // 2):
            first = 2 * group * KX_ROWS
            parts.append(jnp.concatenate([own[first : first + KX_ROWS], own[first + KX_ROWS : first + 2 * KX_ROWS]], axis=1))
    return jnp.concatenate(parts, axis=0).astype(jnp.bfloat16)


def pair_weights(sources, levels_ref):
    rows, cols = lax.axis_size("row"), lax.axis_size("col")
    r, _ = own_place()
    devices = rows * cols
    pairs = STEPS * len(sources)
    line = lax.broadcasted_iota(jnp.int32, (pairs, 1), 0)
    band = jnp.zeros((pairs, 1), jnp.int32)
    slot = jnp.zeros((pairs, 1), jnp.int32)
    for j, source in enumerate(sources):
        place = r * cols + source
        for step in range(STEPS):
            here = line == STEPS * j + step
            band = jnp.where(here, place, band)
            slot = jnp.where(here, lax.rem(place - step * cols + devices, devices), slot)
    lane = lax.broadcasted_iota(jnp.int32, (pairs, levels_ref.shape[1]), 1)

    def at(which, chosen):
        return jnp.sum(jnp.where(lane == chosen, levels_ref[which : which + 1, :], 0.0), axis=1, keepdims=True)

    gap = at(0, band) - at(1, at(2, slot).astype(jnp.int32))
    return -4.0 * gap / (gap * gap + OMEGA_SQUARED) / (devices * STEPS)


def first_kernel(grid, orbitals_ref, sphere_ref, coef_ref, places_ref, table_ref, twiddle_ref, cube_ref):
    half = grid // 2
    sx, sy, kz = sphere_ref[0:1, :], sphere_ref[1:2, :], sphere_ref[2:3, :]
    kx = jnp.where(sx >= half, sx - grid, sx) + GMAX
    ky = jnp.where(sy >= half, sy - grid, sy) + GMAX
    q = (ky * 43) >> 8
    residue = ky - q * RADIX
    places_ref[0:1, :] = (residue & 1) * LANES + q * GMAX + kz - 1
    places_ref[1:2, :] = (residue >> 1) * KX_ROWS + kx
    write_tables(grid, table_ref, twiddle_ref)
    cube_ref[...] = spectrum_of(grid, orbitals_ref[0], orbitals_ref[1], table_ref, twiddle_ref)

    @pl.when(on_even_core())
    def _():
        pick(cube_ref, places_ref, coef_ref, [0])


def pick(cube_ref, places_ref, coef_ref, pairs):
    groups = RADIX // 2 * KX_ROWS // 8
    half_count = places_ref.shape[1]
    counted = lax.broadcasted_iota(jnp.int32, (2 * LANES, TILE), 0).astype(jnp.float32).astype(jnp.bfloat16)
    line = lax.broadcasted_iota(jnp.int32, (8, TILE), 0)
    parts = [(pair, side) for pair in pairs for side in range(2)]
    for first in range(0, half_count, TILE):
        here = slice(first, first + TILE)
        lane = places_ref[0:1, here].astype(jnp.float32).astype(jnp.bfloat16)
        one_hot = jnp.where(counted == lane, jnp.bfloat16(1), jnp.bfloat16(0))
        found = dot(cube_ref[...], one_hot)
        away = line - places_ref[1:2, here]
        values = [jnp.zeros((8, TILE), jnp.float32)] * len(parts)
        for group in range(groups):
            chosen = away == -8 * group
            for which in range(len(parts)):
                start = (which * groups + group) * 8
                values[which] = jnp.where(chosen, found[start : start + 8], values[which])
        for (pair, side), value in zip(parts, values):
            value = jnp.sum(value, axis=0, keepdims=True).astype(jnp.bfloat16)
            coef_ref[pair : pair + 1, side * half_count + first : side * half_count + first + TILE] = value


def on_even_core():
    return lax.rem(lax.axis_index("row"), 2) == 0


def second_kernel(
    grid, orbitals_ref, occ_ref, first_ref, places_ref, table_ref, twiddle_ref, first_cube_ref, coef_ref, later_ref, cube_ref
):
    picks = first_cube_ref.shape[0]
    later_ref[...] = jnp.zeros_like(later_ref)
    cube_ref[picks:, :] = spectrum_of(grid, orbitals_ref[0], occ_ref[0], table_ref, twiddle_ref)

    @pl.when(on_even_core())
    def _():
        coef_ref[0:1, :] = first_ref[...]
        pick(cube_ref.at[picks:], places_ref, coef_ref, [1])

    @pl.when(jnp.logical_not(on_even_core()))
    def _():
        cube_ref[:picks, :] = first_cube_ref[...]
        pick(cube_ref, places_ref, coef_ref, [0, 1])


def cost(flops, data):
    return pl.CostEstimate(flops=flops, bytes_accessed=data, transcendentals=0)


def in_vmem(count):
    return [pl.BlockSpec(memory_space=pltpu.VMEM)] * count


def transform(cond_orbitals, occ_orbitals, occ_second, sphere_index, band_shape):
    grid = cond_orbitals.shape[1]
    half_count = sphere_index.shape[1]
    width, _, table_count = table_rows(grid)
    orbitals = jnp.concatenate([cond_orbitals, occ_orbitals], axis=0)
    picks = RADIX * KX_ROWS
    params = dict(
        compiler_params=pltpu.CompilerParams(vmem_limit_bytes=VMEM_LIMIT),
        cost_estimate=cost(2 * 10**9, 2 * 10**6),
    )
    handed = pl.pallas_call(
        functools.partial(first_kernel, grid),
        out_shape=[
            jax.ShapeDtypeStruct((1, 2 * half_count), jnp.bfloat16),
            jax.ShapeDtypeStruct((2, half_count), jnp.int32),
            jax.ShapeDtypeStruct((table_count, LANES), jnp.bfloat16),
            jax.ShapeDtypeStruct((16, width), jnp.float32),
            jax.ShapeDtypeStruct((picks, 2 * LANES), jnp.bfloat16),
        ],
        in_specs=in_vmem(2),
        out_specs=in_vmem(5),
        name="first_pair",
        **params,
    )(orbitals, sphere_index)
    return pl.pallas_call(
        functools.partial(second_kernel, grid),
        out_shape=[
            jax.ShapeDtypeStruct((STEPS, 2 * half_count), jnp.bfloat16),
            jax.ShapeDtypeStruct((1, *band_shape), jnp.int32),
        ],
        in_specs=in_vmem(7),
        out_specs=in_vmem(2),
        scratch_shapes=[pltpu.VMEM((STEPS * picks, 2 * LANES), jnp.bfloat16)],
        name="second_pair",
        **params,
    )(orbitals, occ_second, *handed)


def pack_kernel(plan, turns, targets, merged, levels_ref, *refs):
    rows, cols, row_width, col_width = plan
    count = len(refs) - len(targets) - 1 - merged
    arrived, outs, mixed_ref = refs[:count], refs[count:-1], refs[-1]
    r, c = own_place()
    first = 0
    for ref in arrived:
        mixed_ref[first : first + ref.shape[0], :] = ref[...].astype(jnp.float32)
        first += ref.shape[0]
    if merged:
        outs[-1][...] = mixed_ref[...].astype(jnp.bfloat16)
    weight = pair_weights([c ^ turn for turn in turns], levels_ref)
    columns = []
    for side in range(2):
        start = pl.multiple_of((c ^ side) * col_width, LANES)
        columns.append((weight * mixed_ref[:, pl.ds(start, col_width)]).astype(jnp.bfloat16))
    for (turn, side), out_ref in zip(targets, outs):
        start = pl.multiple_of((r ^ turn) // 2 * (2 * row_width), LANES)
        out_ref[:, : 2 * row_width] = mixed_ref[:, pl.ds(start, 2 * row_width)].astype(jnp.bfloat16)
        out_ref[:, 2 * row_width :] = columns[side]


def pack(arrived, levels, turns, targets, merged, plan):
    rows, cols, row_width, col_width = plan
    pairs = STEPS * len(turns)
    entries = arrived[0].shape[1]
    shapes = [(pairs, 2 * row_width + col_width)] * len(targets) + [(pairs, entries)] * merged
    return pl.pallas_call(
        functools.partial(pack_kernel, plan, turns, targets, merged),
        out_shape=[jax.ShapeDtypeStruct(shape, jnp.bfloat16) for shape in shapes],
        in_specs=in_vmem(1 + len(arrived)),
        out_specs=in_vmem(len(shapes)),
        scratch_shapes=[pltpu.VMEM((pairs, entries), jnp.float32)],
        compiler_params=pltpu.CompilerParams(vmem_limit_bytes=VMEM_LIMIT),
        cost_estimate=cost(10**9, 10**6),
        name="pack",
    )(levels, *arrived)


def stacked(refs, lanes):
    return jnp.concatenate([ref[:, lanes].astype(jnp.float32) for ref in refs], axis=0).astype(jnp.bfloat16)


def join_kernel(row_width, *refs):
    messages, outs = refs[:-2], refs[-2:]
    depth = messages[0].shape[0]
    merge = max(1, 16 // depth)
    r, _ = own_place()
    for j in range(0, len(messages), merge):
        here = slice(depth * j, depth * (j + merge))
        columns = stacked(messages[j : j + merge], slice(2 * row_width, None))
        for side, out_ref in enumerate(outs):
            lanes = pl.ds(pl.multiple_of((r & 1 ^ side) * row_width, LANES), row_width)
            out_ref[here, :row_width] = stacked(messages[j : j + merge], lanes)
            out_ref[here, row_width:] = columns


def join(messages, plan):
    rows, cols, row_width, col_width = plan
    depth = messages[0].shape[0]
    return pl.pallas_call(
        functools.partial(join_kernel, row_width),
        out_shape=[jax.ShapeDtypeStruct((depth * len(messages), row_width + col_width), jnp.bfloat16)] * 2,
        in_specs=in_vmem(len(messages)),
        out_specs=in_vmem(2),
        compiler_params=pltpu.CompilerParams(vmem_limit_bytes=VMEM_LIMIT),
        cost_estimate=cost(10**9, 10**6),
        name="join",
    )(*messages)


def outer_kernel(row_width, block, slots, *refs):
    messages, (out_ref, right_ref, held_ref, sems) = refs[:-4], refs[-4:]
    depth = messages[0].shape[0]
    for j, ref in enumerate(messages):
        right_ref[depth * j : depth * (j + 1), :] = ref[:, row_width:]
    count = row_width // block

    def copy_out(i, slot):
        rows = pl.ds(pl.multiple_of(i * block, block), block)
        return pltpu.make_async_copy(held_ref.at[slot], out_ref.at[rows], sems.at[slot])

    def step(i, carry):
        slot = lax.rem(i, slots)

        @pl.when(i >= slots)
        def _():
            copy_out(i - slots, slot).wait()

        here = pl.ds(pl.multiple_of(i * block, block), block)
        left = jnp.concatenate([ref[:, here] for ref in messages], axis=0)
        held_ref[slot] = lax.dot_general(left, right_ref[...], (((0,), (0,)), ((), ())), preferred_element_type=jnp.float32)
        copy_out(i, slot).start()
        return carry

    lax.fori_loop(0, count, step, 0)
    for i in range(max(0, count - slots), count):
        copy_out(i, i % slots).wait()


def outer(messages, plan):
    rows, cols, row_width, col_width = plan
    depth = messages[0].shape[0]
    block = min(256, row_width)
    slots = min(4, row_width // block)
    return pl.pallas_call(
        functools.partial(outer_kernel, row_width, block, slots),
        out_shape=jax.ShapeDtypeStruct((row_width, col_width), jnp.float32),
        in_specs=in_vmem(len(messages)),
        out_specs=pl.BlockSpec(memory_space=pltpu.HBM),
        scratch_shapes=[
            pltpu.VMEM((depth * len(messages), col_width), jnp.bfloat16),
            pltpu.VMEM((slots, block, col_width), jnp.float32),
            pltpu.SemaphoreType.DMA((slots,)),
        ],
        compiler_params=pltpu.CompilerParams(vmem_limit_bytes=VMEM_LIMIT),
        cost_estimate=cost(10**10, 3 * 10**7),
        name="outer",
    )(*messages)


def shifted(value, axis, by):
    devices = lax.axis_size(axis)
    return lax.ppermute(value, axis, [(i, (i + by) % devices) for i in range(devices)])


def turned(value, axis, turn):
    devices = lax.axis_size(axis)
    return lax.ppermute(value, axis, [(i, i ^ turn) for i in range(devices)])


def sent_across(value, turn, side, rows, cols):
    moves = [(r * cols + c, (r ^ turn) * cols + (c ^ side)) for r in range(rows) for c in range(cols)]
    return lax.ppermute(value, ("row", "col"), moves)


def on_device(cond_orbitals, occ_orbitals, cond_energy, occ_energy, occ_band, sphere_index):
    rows = lax.axis_size("row")
    cols = lax.axis_size("col")
    entries = 2 * sphere_index.shape[1]
    plan = (rows, cols, entries // rows, entries // cols)
    occ_second = shifted(occ_orbitals, "row", 1)
    own, later = transform(cond_orbitals, occ_orbitals, occ_second, sphere_index, occ_band.shape)
    levels = jnp.stack([cond_energy, occ_energy, (occ_band + later[0]).astype(jnp.float32)])
    targets = [(0, 0)] + [(turn, side) for side in (1, 0) for turn in range(rows - 2, -2, -2) if turn or side]
    targets.append(targets.pop(rows // 2))

    def sent(packed):
        return [packed[0]] + [sent_across(value, *target, rows, cols) for value, target in zip(packed[1:], targets[1:])]

    held, turns, bit = [own], [0], cols // 2
    while bit > 2:
        if len(held) > 1:
            held = [jnp.concatenate(held, axis=0)]
        held.append(turned(held[0], "col", bit))
        turns += [turn + bit for turn in turns]
        bit //= 2
    *packed, merged = pack(held, levels, turns, targets, 1, plan)
    messages = sent(packed)
    far = turned(merged, "col", bit)
    messages += sent(pack([far], levels, [turn + bit for turn in turns], targets, 0, plan))
    kept, passed = join(messages, plan)
    return outer([kept, turned(passed, "row", 1)], plan)


def solution(mesh):
    placed = (P(("row", "col"), None, None), P(("row", "col"), None, None), P(), P(), P(), P())
    return jax.shard_map(
        on_device, mesh=mesh, in_specs=placed, out_specs=P("row", "col"), check_vma=False
    )
```

```python
import functools
import math

import jax
import jax.numpy as jnp
import numpy as np
from jax import lax
from jax.experimental import pallas as pl
from jax.experimental.pallas import tpu as pltpu
from jax.sharding import PartitionSpec as P

GMAX = 18
STEPS = 2
RADIX = 6
SPAN = 2 * GMAX + 1
KX_ROWS = 40
LANES = 128
OMEGA_SQUARED = 0.0625
TILE = 512
VMEM_LIMIT = 40 * 2**20


COSINE_TERMS = 10


def table_rows(grid):
    width = (grid // RADIX) * grid
    x_first = 4 * width
    return width, x_first, x_first + 2 * KX_ROWS


def cosine(phase, grid):
    phase = phase - (phase * 43691 >> 21) * 48
    angle = (phase - grid // 2).astype(jnp.float32) * np.float32(2.0 * math.pi / grid)
    square = angle * angle
    value = jnp.zeros_like(angle)
    for term in reversed(range(COSINE_TERMS)):
        value = value * square - np.float32((-1.0) ** term / math.factorial(2 * term))
    return value


def in_two(values):
    upper = values.astype(jnp.bfloat16)
    return upper, (values - upper.astype(jnp.float32)).astype(jnp.bfloat16)


def write_tables(grid, table_ref, twiddle_ref):
    width, x_first, x_end = table_rows(grid)
    quarter = grid // 4

    def counted(shape, dimension):
        return lax.broadcasted_iota(jnp.int32, shape, dimension)

    row, lane = counted((2 * KX_ROWS, LANES), 0), counted((2 * KX_ROWS, LANES), 1)
    below = (row >= KX_ROWS).astype(jnp.int32)
    place = jnp.where(lane >= grid, lane - grid, lane)
    place = jnp.where(place >= grid, 0, place)
    frequency = row - KX_ROWS * below + (grid - GMAX)
    upper, lower = in_two(cosine(frequency * place + quarter * below, grid))
    mixed = jnp.where(lane < grid, upper.astype(jnp.float32), lower.astype(jnp.float32))
    table_ref[x_first:x_end, :] = mixed.astype(jnp.bfloat16)

    row, lane = counted((16, width), 0), counted((16, width), 1)
    below = (row >= RADIX).astype(jnp.int32)
    residue = jnp.where(row >= 2 * RADIX, 0, row - RADIX * below)
    twiddle_ref[...] = cosine(residue * (lane * 43691 >> 21) + quarter * below, grid)

    lane = counted((1, LANES), 1)
    q = lane * 57 >> 10
    kz = lane - q * GMAX + 1
    y_phase = RADIX * (q + (grid // RADIX - GMAX // RADIX)) * counted((grid // RADIX, LANES), 0)
    z_phase = kz * counted((grid, LANES), 0)
    cos_y, sin_y = cosine(y_phase, grid), cosine(y_phase + 3 * quarter, grid)
    cos_z, sin_z = cosine(z_phase, grid), cosine(z_phase + 3 * quarter, grid)
    for y in range(grid // RADIX):
        cos_here, sin_here = cos_y[y : y + 1], sin_y[y : y + 1]
        whole = (cos_here * cos_z - sin_here * sin_z, -(sin_here * cos_z + cos_here * sin_z))
        for part, values in enumerate(whole):
            for level, piece in enumerate(in_two(values)):
                first = (2 * level + part) * width + y * grid
                table_ref[first : first + grid, :] = piece


def dft_six(re, im):
    half = 0.5
    root = math.sqrt(3.0) / 2.0
    s_re = [re[h] + re[h + 3] for h in range(3)]
    s_im = [im[h] + im[h + 3] for h in range(3)]
    d_re = [re[h] - re[h + 3] for h in range(3)]
    d_im = [im[h] - im[h + 3] for h in range(3)]
    out = [None] * 6
    sum_re, sum_im = s_re[1] + s_re[2], s_im[1] + s_im[2]
    dif_re, dif_im = (s_re[1] - s_re[2]) * root, (s_im[1] - s_im[2]) * root
    out[0] = (s_re[0] + sum_re, s_im[0] + sum_im)
    mid_re, mid_im = s_re[0] - half * sum_re, s_im[0] - half * sum_im
    out[2] = (mid_re + dif_im, mid_im - dif_re)
    out[4] = (mid_re - dif_im, mid_im + dif_re)
    sum_re, sum_im = (d_re[1] + d_re[2]) * root, (d_im[1] + d_im[2]) * root
    dif_re, dif_im = d_re[1] - d_re[2], d_im[1] - d_im[2]
    out[3] = (d_re[0] - dif_re, d_im[0] - dif_im)
    mid_re, mid_im = d_re[0] + half * dif_re, d_im[0] + half * dif_im
    out[1] = (mid_re + sum_im, mid_im - sum_re)
    out[5] = (mid_re - sum_im, mid_im + sum_re)
    return out


def dot(a, b):
    return jnp.dot(a, b, preferred_element_type=jnp.float32)


def own_place():
    return lax.axis_index("row"), lax.axis_index("col")


def spectrum_of(grid, cond, occ, table_ref, twiddle_ref):
    norm = np.float32(grid ** (-1.5))
    width, x_first, x_end = table_rows(grid)
    density = (cond.astype(jnp.float32) * occ.astype(jnp.float32)).astype(jnp.bfloat16)
    x_table = table_ref[x_first:x_end, : 2 * grid]
    section = dot(x_table, jnp.concatenate([density, density], axis=0))
    re = [section[:KX_ROWS, h * width : (h + 1) * width] for h in range(RADIX)]
    im = [section[KX_ROWS:, h * width : (h + 1) * width] for h in range(RADIX)]
    rows = []
    for residue, (d_re, d_im) in enumerate(dft_six(re, im)):
        if residue > 0:
            t_re = twiddle_ref[residue : residue + 1, :]
            t_im = twiddle_ref[RADIX + residue : RADIX + residue + 1, :]
            d_re, d_im = d_re * t_re - d_im * t_im, d_re * t_im + d_im * t_re
        rows.append(jnp.concatenate([d_re, d_im], axis=1))
    whole = jnp.concatenate(rows, axis=0)
    whole_hi = whole.astype(jnp.bfloat16)
    whole_lo = (whole - whole_hi.astype(jnp.float32)).astype(jnp.bfloat16)

    def rotation(first):
        cos_part = table_ref[first : first + width, :]
        sin_part = table_ref[first + width : first + 2 * width, :]
        upper = jnp.concatenate([cos_part, sin_part], axis=1)
        return jnp.concatenate([upper, jnp.concatenate([-sin_part, cos_part], axis=1)], axis=0)

    upper, lower = rotation(0), rotation(2 * width)
    spectrum = (dot(whole_hi, upper) + dot(whole_lo, upper) + dot(whole_hi, lower)) * norm
    parts = []
    for side in range(2):
        own = spectrum[:, side * LANES : (side + 1) * LANES]
        for group in range(RADIX // 2):
            first = 2 * group * KX_ROWS
            parts.append(jnp.concatenate([own[first : first + KX_ROWS], own[first + KX_ROWS : first + 2 * KX_ROWS]], axis=1))
    return jnp.concatenate(parts, axis=0).astype(jnp.bfloat16)


def pair_weights(sources, levels_ref):
    rows, cols = lax.axis_size("row"), lax.axis_size("col")
    r, _ = own_place()
    devices = rows * cols
    pairs = STEPS * len(sources)
    line = lax.broadcasted_iota(jnp.int32, (pairs, 1), 0)
    band = jnp.zeros((pairs, 1), jnp.int32)
    slot = jnp.zeros((pairs, 1), jnp.int32)
    for j, source in enumerate(sources):
        place = r * cols + source
        for step in range(STEPS):
            here = line == STEPS * j + step
            band = jnp.where(here, place, band)
            slot = jnp.where(here, lax.rem(place - step * cols + devices, devices), slot)
    lane = lax.broadcasted_iota(jnp.int32, (pairs, levels_ref.shape[1]), 1)

    def at(which, chosen):
        return jnp.sum(jnp.where(lane == chosen, levels_ref[which : which + 1, :], 0.0), axis=1, keepdims=True)

    gap = at(0, band) - at(1, at(2, slot).astype(jnp.int32))
    return -4.0 * gap / (gap * gap + OMEGA_SQUARED) / (devices * STEPS)


def first_kernel(grid, orbitals_ref, sphere_ref, coef_ref, places_ref, table_ref, twiddle_ref, cube_ref):
    half = grid // 2
    sx, sy, kz = sphere_ref[0:1, :], sphere_ref[1:2, :], sphere_ref[2:3, :]
    kx = jnp.where(sx >= half, sx - grid, sx) + GMAX
    ky = jnp.where(sy >= half, sy - grid, sy) + GMAX
    q = (ky * 43) >> 8
    residue = ky - q * RADIX
    places_ref[0:1, :] = (residue & 1) * LANES + q * GMAX + kz - 1
    places_ref[1:2, :] = (residue >> 1) * KX_ROWS + kx
    write_tables(grid, table_ref, twiddle_ref)
    cube_ref[...] = spectrum_of(grid, orbitals_ref[0], orbitals_ref[1], table_ref, twiddle_ref)

    @pl.when(on_even_core())
    def _():
        pick(cube_ref, places_ref, coef_ref, [0])


def pick(cube_ref, places_ref, coef_ref, pairs):
    groups = RADIX // 2 * KX_ROWS // 8
    half_count = places_ref.shape[1]
    counted = lax.broadcasted_iota(jnp.int32, (2 * LANES, TILE), 0).astype(jnp.float32).astype(jnp.bfloat16)
    line = lax.broadcasted_iota(jnp.int32, (8, TILE), 0)
    parts = [(pair, side) for pair in pairs for side in range(2)]
    for first in range(0, half_count, TILE):
        here = slice(first, first + TILE)
        lane = places_ref[0:1, here].astype(jnp.float32).astype(jnp.bfloat16)
        one_hot = jnp.where(counted == lane, jnp.bfloat16(1), jnp.bfloat16(0))
        found = dot(cube_ref[...], one_hot)
        away = line - places_ref[1:2, here]
        values = [jnp.zeros((8, TILE), jnp.float32)] * len(parts)
        for group in range(groups):
            chosen = away == -8 * group
            for which in range(len(parts)):
                start = (which * groups + group) * 8
                values[which] = jnp.where(chosen, found[start : start + 8], values[which])
        for (pair, side), value in zip(parts, values):
            value = jnp.sum(value, axis=0, keepdims=True).astype(jnp.bfloat16)
            coef_ref[pair : pair + 1, side * half_count + first : side * half_count + first + TILE] = value


def on_even_core():
    return lax.rem(lax.axis_index("row"), 2) == 0


def second_kernel(
    grid, orbitals_ref, occ_ref, first_ref, places_ref, table_ref, twiddle_ref, first_cube_ref, coef_ref, later_ref, cube_ref
):
    picks = first_cube_ref.shape[0]
    later_ref[...] = jnp.zeros_like(later_ref)
    cube_ref[picks:, :] = spectrum_of(grid, orbitals_ref[0], occ_ref[0], table_ref, twiddle_ref)

    @pl.when(on_even_core())
    def _():
        coef_ref[0:1, :] = first_ref[...]
        pick(cube_ref.at[picks:], places_ref, coef_ref, [1])

    @pl.when(jnp.logical_not(on_even_core()))
    def _():
        cube_ref[:picks, :] = first_cube_ref[...]
        pick(cube_ref, places_ref, coef_ref, [0, 1])


def cost(flops, data):
    return pl.CostEstimate(flops=flops, bytes_accessed=data, transcendentals=0)


def in_vmem(count):
    return [pl.BlockSpec(memory_space=pltpu.VMEM)] * count


def transform(cond_orbitals, occ_orbitals, occ_second, sphere_index, band_shape):
    grid = cond_orbitals.shape[1]
    half_count = sphere_index.shape[1]
    width, _, table_count = table_rows(grid)
    orbitals = jnp.concatenate([cond_orbitals, occ_orbitals], axis=0)
    picks = RADIX * KX_ROWS
    params = dict(
        compiler_params=pltpu.CompilerParams(vmem_limit_bytes=VMEM_LIMIT),
        cost_estimate=cost(2 * 10**9, 2 * 10**6),
    )
    handed = pl.pallas_call(
        functools.partial(first_kernel, grid),
        out_shape=[
            jax.ShapeDtypeStruct((1, 2 * half_count), jnp.bfloat16),
            jax.ShapeDtypeStruct((2, half_count), jnp.int32),
            jax.ShapeDtypeStruct((table_count, LANES), jnp.bfloat16),
            jax.ShapeDtypeStruct((16, width), jnp.float32),
            jax.ShapeDtypeStruct((picks, 2 * LANES), jnp.bfloat16),
        ],
        in_specs=in_vmem(2),
        out_specs=in_vmem(5),
        name="first_pair",
        **params,
    )(orbitals, sphere_index)
    return pl.pallas_call(
        functools.partial(second_kernel, grid),
        out_shape=[
            jax.ShapeDtypeStruct((STEPS, 2 * half_count), jnp.bfloat16),
            jax.ShapeDtypeStruct((1, *band_shape), jnp.int32),
        ],
        in_specs=in_vmem(7),
        out_specs=in_vmem(2),
        scratch_shapes=[pltpu.VMEM((STEPS * picks, 2 * LANES), jnp.bfloat16)],
        name="second_pair",
        **params,
    )(orbitals, occ_second, *handed)


def pack_kernel(plan, turns, targets, merged, levels_ref, *refs):
    rows, cols, row_width, col_width = plan
    count = len(refs) - len(targets) - 1 - merged
    arrived, outs, mixed_ref = refs[:count], refs[count:-1], refs[-1]
    r, c = own_place()
    first = 0
    for ref in arrived:
        mixed_ref[first : first + ref.shape[0], :] = ref[...].astype(jnp.float32)
        first += ref.shape[0]
    if merged:
        outs[-1][...] = mixed_ref[...].astype(jnp.bfloat16)
    weight = pair_weights([c ^ turn for turn in turns], levels_ref)
    for (even, odd), out_ref in zip(targets, outs):
        turn, side = (jnp.where(on_even_core(), *choice) for choice in zip(even, odd))
        start = pl.multiple_of((r ^ turn) // 2 * (2 * row_width), LANES)
        out_ref[:, : 2 * row_width] = mixed_ref[:, pl.ds(start, 2 * row_width)].astype(jnp.bfloat16)
        start = pl.multiple_of((c ^ side) * col_width, LANES)
        out_ref[:, 2 * row_width :] = (weight * mixed_ref[:, pl.ds(start, col_width)]).astype(jnp.bfloat16)


def pack(arrived, levels, turns, targets, merged, plan):
    rows, cols, row_width, col_width = plan
    pairs = STEPS * len(turns)
    entries = arrived[0].shape[1]
    shapes = [(pairs, 2 * row_width + col_width)] * len(targets) + [(pairs, entries)] * merged
    return pl.pallas_call(
        functools.partial(pack_kernel, plan, turns, targets, merged),
        out_shape=[jax.ShapeDtypeStruct(shape, jnp.bfloat16) for shape in shapes],
        in_specs=in_vmem(1 + len(arrived)),
        out_specs=in_vmem(len(shapes)),
        scratch_shapes=[pltpu.VMEM((pairs, entries), jnp.float32)],
        compiler_params=pltpu.CompilerParams(vmem_limit_bytes=VMEM_LIMIT),
        cost_estimate=cost(10**9, 10**6),
        name="pack",
    )(levels, *arrived)


def stacked(refs, lanes):
    return jnp.concatenate([ref[:, lanes].astype(jnp.float32) for ref in refs], axis=0).astype(jnp.bfloat16)


def join_kernel(row_width, *refs):
    messages, outs = refs[:-2], refs[-2:]
    depth = messages[0].shape[0]
    merge = max(1, 16 // depth)
    r, _ = own_place()
    for j in range(0, len(messages), merge):
        here = slice(depth * j, depth * (j + merge))
        columns = stacked(messages[j : j + merge], slice(2 * row_width, None))
        for side, out_ref in enumerate(outs):
            lanes = pl.ds(pl.multiple_of((r & 1 ^ side) * row_width, LANES), row_width)
            out_ref[here, :row_width] = stacked(messages[j : j + merge], lanes)
            out_ref[here, row_width:] = columns


def join(messages, plan):
    rows, cols, row_width, col_width = plan
    depth = messages[0].shape[0]
    return pl.pallas_call(
        functools.partial(join_kernel, row_width),
        out_shape=[jax.ShapeDtypeStruct((depth * len(messages), row_width + col_width), jnp.bfloat16)] * 2,
        in_specs=in_vmem(len(messages)),
        out_specs=in_vmem(2),
        compiler_params=pltpu.CompilerParams(vmem_limit_bytes=VMEM_LIMIT),
        cost_estimate=cost(10**9, 10**6),
        name="join",
    )(*messages)


def outer_kernel(row_width, block, slots, *refs):
    messages, (out_ref, right_ref, held_ref, sems) = refs[:-4], refs[-4:]
    depth = messages[0].shape[0]
    for j, ref in enumerate(messages):
        right_ref[depth * j : depth * (j + 1), :] = ref[:, row_width:]
    count = row_width // block

    def copy_out(i, slot):
        rows = pl.ds(pl.multiple_of(i * block, block), block)
        return pltpu.make_async_copy(held_ref.at[slot], out_ref.at[rows], sems.at[slot])

    def step(i, carry):
        slot = lax.rem(i, slots)

        @pl.when(i >= slots)
        def _():
            copy_out(i - slots, slot).wait()

        here = pl.ds(pl.multiple_of(i * block, block), block)
        left = jnp.concatenate([ref[:, here] for ref in messages], axis=0)
        held_ref[slot] = lax.dot_general(left, right_ref[...], (((0,), (0,)), ((), ())), preferred_element_type=jnp.float32)
        copy_out(i, slot).start()
        return carry

    lax.fori_loop(0, count, step, 0)
    for i in range(max(0, count - slots), count):
        copy_out(i, i % slots).wait()


def outer(messages, plan):
    rows, cols, row_width, col_width = plan
    depth = messages[0].shape[0]
    block = min(256, row_width)
    slots = min(4, row_width // block)
    return pl.pallas_call(
        functools.partial(outer_kernel, row_width, block, slots),
        out_shape=jax.ShapeDtypeStruct((row_width, col_width), jnp.float32),
        in_specs=in_vmem(len(messages)),
        out_specs=pl.BlockSpec(memory_space=pltpu.HBM),
        scratch_shapes=[
            pltpu.VMEM((depth * len(messages), col_width), jnp.bfloat16),
            pltpu.VMEM((slots, block, col_width), jnp.float32),
            pltpu.SemaphoreType.DMA((slots,)),
        ],
        compiler_params=pltpu.CompilerParams(vmem_limit_bytes=VMEM_LIMIT),
        cost_estimate=cost(10**10, 3 * 10**7),
        name="outer",
    )(*messages)


def shifted(value, axis, by):
    devices = lax.axis_size(axis)
    return lax.ppermute(value, axis, [(i, (i + by) % devices) for i in range(devices)])


def turned(value, axis, turn):
    devices = lax.axis_size(axis)
    return lax.ppermute(value, axis, [(i, i ^ turn) for i in range(devices)])


def sent_across(value, target, rows, cols):
    moves = []
    for r in range(rows):
        turn, side = target[r % 2]
        moves += [(r * cols + c, (r ^ turn) * cols + (c ^ side)) for c in range(cols)]
    return lax.ppermute(value, ("row", "col"), moves)


def on_device(cond_orbitals, occ_orbitals, cond_energy, occ_energy, occ_band, sphere_index):
    rows = lax.axis_size("row")
    cols = lax.axis_size("col")
    entries = 2 * sphere_index.shape[1]
    plan = (rows, cols, entries // rows, entries // cols)
    occ_second = shifted(occ_orbitals, "row", 1)
    own, later = transform(cond_orbitals, occ_orbitals, occ_second, sphere_index, occ_band.shape)
    levels = jnp.stack([cond_energy, occ_energy, (occ_band + later[0]).astype(jnp.float32)])
    even = [(0, 0)] + [(turn, 1) for turn in range(rows - 2, 0, -2)] + [(turn, 0) for turn in range(rows - 2, 0, -2)] + [(0, 1)]
    odd = even[:-2] + even[:-3:-1]
    targets = list(zip(even, odd))

    def sent(packed):
        return [packed[0]] + [sent_across(value, target, rows, cols) for value, target in zip(packed[1:], targets[1:])]

    held, turns, bit = [own], [0], cols // 2
    while bit > 2:
        if len(held) > 1:
            held = [jnp.concatenate(held, axis=0)]
        held.append(turned(held[0], "col", bit))
        turns += [turn + bit for turn in turns]
        bit //= 2
    *packed, merged = pack(held, levels, turns, targets, 1, plan)
    messages = sent(packed)
    far = turned(merged, "col", bit)
    messages += sent(pack([far], levels, [turn + bit for turn in turns], targets, 0, plan))
    kept, passed = join(messages, plan)
    return outer([kept, turned(passed, "row", 1)], plan)


def solution(mesh):
    placed = (P(("row", "col"), None, None), P(("row", "col"), None, None), P(), P(), P(), P())
    return jax.shard_map(
        on_device, mesh=mesh, in_specs=placed, out_specs=P("row", "col"), check_vma=False
    )
```

```python
import functools
import math

import jax
import jax.numpy as jnp
import numpy as np
from jax import lax
from jax.experimental import pallas as pl
from jax.experimental.pallas import tpu as pltpu
from jax.sharding import PartitionSpec as P

GMAX = 18
STEPS = 2
RADIX = 6
SPAN = 2 * GMAX + 1
KX_ROWS = 40
LANES = 128
OMEGA_SQUARED = 0.0625
TILE = 512
VMEM_LIMIT = 40 * 2**20


COSINE_TERMS = 10


def table_rows(grid):
    width = (grid // RADIX) * grid
    x_first = 4 * width
    return width, x_first, x_first + 2 * KX_ROWS


def cosine(phase, grid):
    phase = phase - (phase * 43691 >> 21) * 48
    angle = (phase - grid // 2).astype(jnp.float32) * np.float32(2.0 * math.pi / grid)
    square = angle * angle
    value = jnp.zeros_like(angle)
    for term in reversed(range(COSINE_TERMS)):
        value = value * square - np.float32((-1.0) ** term / math.factorial(2 * term))
    return value


def in_two(values):
    upper = values.astype(jnp.bfloat16)
    return upper, (values - upper.astype(jnp.float32)).astype(jnp.bfloat16)


def write_tables(grid, table_ref, twiddle_ref):
    width, x_first, x_end = table_rows(grid)
    quarter = grid // 4

    def counted(shape, dimension):
        return lax.broadcasted_iota(jnp.int32, shape, dimension)

    row, lane = counted((2 * KX_ROWS, LANES), 0), counted((2 * KX_ROWS, LANES), 1)
    below = (row >= KX_ROWS).astype(jnp.int32)
    place = jnp.where(lane >= grid, lane - grid, lane)
    place = jnp.where(place >= grid, 0, place)
    frequency = row - KX_ROWS * below + (grid - GMAX)
    upper, lower = in_two(cosine(frequency * place + quarter * below, grid))
    mixed = jnp.where(lane < grid, upper.astype(jnp.float32), lower.astype(jnp.float32))
    table_ref[x_first:x_end, :] = mixed.astype(jnp.bfloat16)

    row, lane = counted((16, width), 0), counted((16, width), 1)
    below = (row >= RADIX).astype(jnp.int32)
    residue = jnp.where(row >= 2 * RADIX, 0, row - RADIX * below)
    twiddle_ref[...] = cosine(residue * (lane * 43691 >> 21) + quarter * below, grid)

    lane = counted((1, LANES), 1)
    q = lane * 57 >> 10
    kz = lane - q * GMAX + 1
    y_phase = RADIX * (q + (grid // RADIX - GMAX // RADIX)) * counted((grid // RADIX, LANES), 0)
    z_phase = kz * counted((grid, LANES), 0)
    cos_y, sin_y = cosine(y_phase, grid), cosine(y_phase + 3 * quarter, grid)
    cos_z, sin_z = cosine(z_phase, grid), cosine(z_phase + 3 * quarter, grid)
    for y in range(grid // RADIX):
        cos_here, sin_here = cos_y[y : y + 1], sin_y[y : y + 1]
        whole = (cos_here * cos_z - sin_here * sin_z, -(sin_here * cos_z + cos_here * sin_z))
        for part, values in enumerate(whole):
            for level, piece in enumerate(in_two(values)):
                first = (2 * level + part) * width + y * grid
                table_ref[first : first + grid, :] = piece


def dft_six(re, im):
    half = 0.5
    root = math.sqrt(3.0) / 2.0
    s_re = [re[h] + re[h + 3] for h in range(3)]
    s_im = [im[h] + im[h + 3] for h in range(3)]
    d_re = [re[h] - re[h + 3] for h in range(3)]
    d_im = [im[h] - im[h + 3] for h in range(3)]
    out = [None] * 6
    sum_re, sum_im = s_re[1] + s_re[2], s_im[1] + s_im[2]
    dif_re, dif_im = (s_re[1] - s_re[2]) * root, (s_im[1] - s_im[2]) * root
    out[0] = (s_re[0] + sum_re, s_im[0] + sum_im)
    mid_re, mid_im = s_re[0] - half * sum_re, s_im[0] - half * sum_im
    out[2] = (mid_re + dif_im, mid_im - dif_re)
    out[4] = (mid_re - dif_im, mid_im + dif_re)
    sum_re, sum_im = (d_re[1] + d_re[2]) * root, (d_im[1] + d_im[2]) * root
    dif_re, dif_im = d_re[1] - d_re[2], d_im[1] - d_im[2]
    out[3] = (d_re[0] - dif_re, d_im[0] - dif_im)
    mid_re, mid_im = d_re[0] + half * dif_re, d_im[0] + half * dif_im
    out[1] = (mid_re + sum_im, mid_im - sum_re)
    out[5] = (mid_re - sum_im, mid_im + sum_re)
    return out


def dot(a, b):
    return jnp.dot(a, b, preferred_element_type=jnp.float32)


def own_place():
    return lax.axis_index("row"), lax.axis_index("col")


def spectrum_of(grid, cond, occ, table_ref, twiddle_ref):
    norm = np.float32(grid ** (-1.5))
    width, x_first, x_end = table_rows(grid)
    density = (cond.astype(jnp.float32) * occ.astype(jnp.float32)).astype(jnp.bfloat16)
    x_table = table_ref[x_first:x_end, : 2 * grid]
    section = dot(x_table, jnp.concatenate([density, density], axis=0))
    re = [section[:KX_ROWS, h * width : (h + 1) * width] for h in range(RADIX)]
    im = [section[KX_ROWS:, h * width : (h + 1) * width] for h in range(RADIX)]
    rows = []
    for residue, (d_re, d_im) in enumerate(dft_six(re, im)):
        if residue > 0:
            t_re = twiddle_ref[residue : residue + 1, :]
            t_im = twiddle_ref[RADIX + residue : RADIX + residue + 1, :]
            d_re, d_im = d_re * t_re - d_im * t_im, d_re * t_im + d_im * t_re
        rows.append(jnp.concatenate([d_re, d_im], axis=1))
    whole = jnp.concatenate(rows, axis=0)
    whole_hi = whole.astype(jnp.bfloat16)
    whole_lo = (whole - whole_hi.astype(jnp.float32)).astype(jnp.bfloat16)

    def rotation(first):
        cos_part = table_ref[first : first + width, :]
        sin_part = table_ref[first + width : first + 2 * width, :]
        upper = jnp.concatenate([cos_part, sin_part], axis=1)
        return jnp.concatenate([upper, jnp.concatenate([-sin_part, cos_part], axis=1)], axis=0)

    upper, lower = rotation(0), rotation(2 * width)
    spectrum = (dot(whole_hi, upper) + dot(whole_lo, upper) + dot(whole_hi, lower)) * norm
    parts = []
    for side in range(2):
        own = spectrum[:, side * LANES : (side + 1) * LANES]
        for group in range(RADIX // 2):
            first = 2 * group * KX_ROWS
            parts.append(jnp.concatenate([own[first : first + KX_ROWS], own[first + KX_ROWS : first + 2 * KX_ROWS]], axis=1))
    return jnp.concatenate(parts, axis=0).astype(jnp.bfloat16)


def pair_weights(sources, levels_ref):
    rows, cols = lax.axis_size("row"), lax.axis_size("col")
    r, _ = own_place()
    devices = rows * cols
    pairs = STEPS * len(sources)
    line = lax.broadcasted_iota(jnp.int32, (pairs, 1), 0)
    band = jnp.zeros((pairs, 1), jnp.int32)
    slot = jnp.zeros((pairs, 1), jnp.int32)
    for j, source in enumerate(sources):
        place = r * cols + source
        for step in range(STEPS):
            here = line == STEPS * j + step
            band = jnp.where(here, place, band)
            slot = jnp.where(here, lax.rem(place - step * cols + devices, devices), slot)
    lane = lax.broadcasted_iota(jnp.int32, (pairs, levels_ref.shape[1]), 1)

    def at(which, chosen):
        return jnp.sum(jnp.where(lane == chosen, levels_ref[which : which + 1, :], 0.0), axis=1, keepdims=True)

    gap = at(0, band) - at(1, at(2, slot).astype(jnp.int32))
    return -4.0 * gap / (gap * gap + OMEGA_SQUARED) / (devices * STEPS)


def first_kernel(grid, orbitals_ref, sphere_ref, coef_ref, places_ref, table_ref, twiddle_ref, cube_ref):
    half = grid // 2
    sx, sy, kz = sphere_ref[0:1, :], sphere_ref[1:2, :], sphere_ref[2:3, :]
    kx = jnp.where(sx >= half, sx - grid, sx) + GMAX
    ky = jnp.where(sy >= half, sy - grid, sy) + GMAX
    q = (ky * 43) >> 8
    residue = ky - q * RADIX
    places_ref[0:1, :] = (residue & 1) * LANES + q * GMAX + kz - 1
    places_ref[1:2, :] = (residue >> 1) * KX_ROWS + kx
    write_tables(grid, table_ref, twiddle_ref)
    cube_ref[...] = spectrum_of(grid, orbitals_ref[0], orbitals_ref[1], table_ref, twiddle_ref)

    @pl.when(on_even_core())
    def _():
        pick(cube_ref, places_ref, coef_ref, [0])


def pick(cube_ref, places_ref, coef_ref, pairs):
    groups = RADIX // 2 * KX_ROWS // 8
    half_count = places_ref.shape[1]
    counted = lax.broadcasted_iota(jnp.int32, (2 * LANES, TILE), 0).astype(jnp.float32).astype(jnp.bfloat16)
    line = lax.broadcasted_iota(jnp.int32, (8, TILE), 0)
    parts = [(pair, side) for pair in pairs for side in range(2)]
    for first in range(0, half_count, TILE):
        here = slice(first, first + TILE)
        lane = places_ref[0:1, here].astype(jnp.float32).astype(jnp.bfloat16)
        one_hot = jnp.where(counted == lane, jnp.bfloat16(1), jnp.bfloat16(0))
        found = dot(cube_ref[...], one_hot)
        away = line - places_ref[1:2, here]
        values = [jnp.zeros((8, TILE), jnp.float32)] * len(parts)
        for group in range(groups):
            chosen = away == -8 * group
            for which in range(len(parts)):
                start = (which * groups + group) * 8
                values[which] = jnp.where(chosen, found[start : start + 8], values[which])
        for (pair, side), value in zip(parts, values):
            value = jnp.sum(value, axis=0, keepdims=True).astype(jnp.bfloat16)
            coef_ref[pair : pair + 1, side * half_count + first : side * half_count + first + TILE] = value


def on_even_core():
    return lax.rem(lax.axis_index("row"), 2) == 0


def second_kernel(
    grid, orbitals_ref, occ_ref, first_ref, places_ref, table_ref, twiddle_ref, first_cube_ref, coef_ref, later_ref, cube_ref
):
    picks = first_cube_ref.shape[0]
    later_ref[...] = jnp.zeros_like(later_ref)
    cube_ref[picks:, :] = spectrum_of(grid, orbitals_ref[0], occ_ref[0], table_ref, twiddle_ref)

    @pl.when(on_even_core())
    def _():
        coef_ref[0:1, :] = first_ref[...]
        pick(cube_ref.at[picks:], places_ref, coef_ref, [1])

    @pl.when(jnp.logical_not(on_even_core()))
    def _():
        cube_ref[:picks, :] = first_cube_ref[...]
        pick(cube_ref, places_ref, coef_ref, [0, 1])


def cost(flops, data):
    return pl.CostEstimate(flops=flops, bytes_accessed=data, transcendentals=0)


def in_vmem(count):
    return [pl.BlockSpec(memory_space=pltpu.VMEM)] * count


def transform(cond_orbitals, occ_orbitals, occ_second, sphere_index, band_shape):
    grid = cond_orbitals.shape[1]
    half_count = sphere_index.shape[1]
    width, _, table_count = table_rows(grid)
    orbitals = jnp.concatenate([cond_orbitals, occ_orbitals], axis=0)
    picks = RADIX * KX_ROWS
    params = dict(
        compiler_params=pltpu.CompilerParams(vmem_limit_bytes=VMEM_LIMIT),
        cost_estimate=cost(2 * 10**9, 2 * 10**6),
    )
    handed = pl.pallas_call(
        functools.partial(first_kernel, grid),
        out_shape=[
            jax.ShapeDtypeStruct((1, 2 * half_count), jnp.bfloat16),
            jax.ShapeDtypeStruct((2, half_count), jnp.int32),
            jax.ShapeDtypeStruct((table_count, LANES), jnp.bfloat16),
            jax.ShapeDtypeStruct((16, width), jnp.float32),
            jax.ShapeDtypeStruct((picks, 2 * LANES), jnp.bfloat16),
        ],
        in_specs=in_vmem(2),
        out_specs=in_vmem(5),
        name="first_pair",
        **params,
    )(orbitals, sphere_index)
    return pl.pallas_call(
        functools.partial(second_kernel, grid),
        out_shape=[
            jax.ShapeDtypeStruct((STEPS, 2 * half_count), jnp.bfloat16),
            jax.ShapeDtypeStruct((1, *band_shape), jnp.int32),
        ],
        in_specs=in_vmem(7),
        out_specs=in_vmem(2),
        scratch_shapes=[pltpu.VMEM((STEPS * picks, 2 * LANES), jnp.bfloat16)],
        name="second_pair",
        **params,
    )(orbitals, occ_second, *handed)


def pack_kernel(plan, turns, targets, levels_ref, *refs):
    rows, cols, row_width, col_width = plan
    count = len(refs) - len(targets) - 1
    arrived, outs, mixed_ref = refs[:count], refs[count:-1], refs[-1]
    r, c = own_place()
    first = 0
    for ref in arrived:
        mixed_ref[first : first + ref.shape[0], :] = ref[...].astype(jnp.float32)
        first += ref.shape[0]
    weight = pair_weights([c ^ turn for turn in turns], levels_ref)
    columns = []
    for side in range(2):
        start = pl.multiple_of((c ^ side) * col_width, LANES)
        columns.append((weight * mixed_ref[:, pl.ds(start, col_width)]).astype(jnp.bfloat16))
    for (turn, side), out_ref in zip(targets, outs):
        start = pl.multiple_of((r ^ turn) // 2 * (2 * row_width), LANES)
        out_ref[:, : 2 * row_width] = mixed_ref[:, pl.ds(start, 2 * row_width)].astype(jnp.bfloat16)
        out_ref[:, 2 * row_width :] = columns[side]


def pack(arrived, levels, turns, targets, plan):
    rows, cols, row_width, col_width = plan
    pairs = STEPS * len(turns)
    entries = arrived[0].shape[1]
    shapes = [(pairs, 2 * row_width + col_width)] * len(targets)
    return pl.pallas_call(
        functools.partial(pack_kernel, plan, turns, targets),
        out_shape=[jax.ShapeDtypeStruct(shape, jnp.bfloat16) for shape in shapes],
        in_specs=in_vmem(1 + len(arrived)),
        out_specs=in_vmem(len(shapes)),
        scratch_shapes=[pltpu.VMEM((pairs, entries), jnp.float32)],
        compiler_params=pltpu.CompilerParams(vmem_limit_bytes=VMEM_LIMIT),
        cost_estimate=cost(10**9, 10**6),
        name="pack",
    )(levels, *arrived)


def stacked(refs, lanes):
    return jnp.concatenate([ref[:, lanes].astype(jnp.float32) for ref in refs], axis=0).astype(jnp.bfloat16)


def join_kernel(row_width, *refs):
    messages, outs = refs[:-2], refs[-2:]
    depth = messages[0].shape[0]
    merge = max(1, 16 // depth)
    r, _ = own_place()
    for j in range(0, len(messages), merge):
        here = slice(depth * j, depth * (j + merge))
        columns = stacked(messages[j : j + merge], slice(2 * row_width, None))
        for side, out_ref in enumerate(outs):
            lanes = pl.ds(pl.multiple_of((r & 1 ^ side) * row_width, LANES), row_width)
            out_ref[here, :row_width] = stacked(messages[j : j + merge], lanes)
            out_ref[here, row_width:] = columns


def join(messages, plan):
    rows, cols, row_width, col_width = plan
    depth = messages[0].shape[0]
    return pl.pallas_call(
        functools.partial(join_kernel, row_width),
        out_shape=[jax.ShapeDtypeStruct((depth * len(messages), row_width + col_width), jnp.bfloat16)] * 2,
        in_specs=in_vmem(len(messages)),
        out_specs=in_vmem(2),
        compiler_params=pltpu.CompilerParams(vmem_limit_bytes=VMEM_LIMIT),
        cost_estimate=cost(10**9, 10**6),
        name="join",
    )(*messages)


def outer_kernel(row_width, block, slots, *refs):
    messages, (out_ref, right_ref, held_ref, sems) = refs[:-4], refs[-4:]
    depth = messages[0].shape[0]
    for j, ref in enumerate(messages):
        right_ref[depth * j : depth * (j + 1), :] = ref[:, row_width:]
    count = row_width // block

    def copy_out(i, slot):
        rows = pl.ds(pl.multiple_of(i * block, block), block)
        return pltpu.make_async_copy(held_ref.at[slot], out_ref.at[rows], sems.at[slot])

    def step(i, carry):
        slot = lax.rem(i, slots)

        @pl.when(i >= slots)
        def _():
            copy_out(i - slots, slot).wait()

        here = pl.ds(pl.multiple_of(i * block, block), block)
        left = jnp.concatenate([ref[:, here] for ref in messages], axis=0)
        held_ref[slot] = lax.dot_general(left, right_ref[...], (((0,), (0,)), ((), ())), preferred_element_type=jnp.float32)
        copy_out(i, slot).start()
        return carry

    lax.fori_loop(0, count, step, 0)
    for i in range(max(0, count - slots), count):
        copy_out(i, i % slots).wait()


def outer(messages, plan):
    rows, cols, row_width, col_width = plan
    depth = messages[0].shape[0]
    block = min(256, row_width)
    slots = min(4, row_width // block)
    return pl.pallas_call(
        functools.partial(outer_kernel, row_width, block, slots),
        out_shape=jax.ShapeDtypeStruct((row_width, col_width), jnp.float32),
        in_specs=in_vmem(len(messages)),
        out_specs=pl.BlockSpec(memory_space=pltpu.HBM),
        scratch_shapes=[
            pltpu.VMEM((depth * len(messages), col_width), jnp.bfloat16),
            pltpu.VMEM((slots, block, col_width), jnp.float32),
            pltpu.SemaphoreType.DMA((slots,)),
        ],
        compiler_params=pltpu.CompilerParams(vmem_limit_bytes=VMEM_LIMIT),
        cost_estimate=cost(10**10, 3 * 10**7),
        name="outer",
    )(*messages)


def copy_kernel(value_ref, behind_ref, out_ref):
    out_ref[...] = value_ref[...]


def copied(value, behind):
    return pl.pallas_call(
        copy_kernel,
        out_shape=jax.ShapeDtypeStruct(value.shape, value.dtype),
        in_specs=in_vmem(2),
        out_specs=in_vmem(1)[0],
        compiler_params=pltpu.CompilerParams(vmem_limit_bytes=VMEM_LIMIT),
        cost_estimate=cost(10**6, 10**5),
        name="copied",
    )(value, behind)


def shifted(value, axis, by):
    devices = lax.axis_size(axis)
    return lax.ppermute(value, axis, [(i, (i + by) % devices) for i in range(devices)])


def turned(value, axis, turn):
    devices = lax.axis_size(axis)
    return lax.ppermute(value, axis, [(i, i ^ turn) for i in range(devices)])


def sent_across(value, turn, side, rows, cols):
    moves = [(r * cols + c, (r ^ turn) * cols + (c ^ side)) for r in range(rows) for c in range(cols)]
    return lax.ppermute(value, ("row", "col"), moves)


def on_device(cond_orbitals, occ_orbitals, cond_energy, occ_energy, occ_band, sphere_index):
    rows = lax.axis_size("row")
    cols = lax.axis_size("col")
    entries = 2 * sphere_index.shape[1]
    plan = (rows, cols, entries // rows, entries // cols)
    occ_second = shifted(occ_orbitals, "row", 1)
    own, later = transform(cond_orbitals, occ_orbitals, occ_second, sphere_index, occ_band.shape)
    levels = jnp.stack([cond_energy, occ_energy, (occ_band + later[0]).astype(jnp.float32)])
    targets = [(0, 0)] + [(turn, side) for side in (1, 0) for turn in range(rows - 2, -2, -2) if turn or side]
    targets.append(targets.pop(rows // 2))

    def sent(packed):
        return [packed[0]] + [sent_across(value, *target, rows, cols) for value, target in zip(packed[1:], targets[1:])]

    others, other_turns, bit = [], [], cols // 2
    while bit > 2:
        held = jnp.concatenate([own, *others], axis=0) if others else own
        others.append(turned(held, "col", bit))
        other_turns += [turn + bit for turn in [0, *other_turns]]
        bit //= 2
    turns = [0, *other_turns]
    messages = sent(pack([own, *others], levels, turns, targets, plan))
    relayed = turned(jnp.concatenate(others, axis=0) if len(others) > 1 else others[0], "col", bit)
    beside = turned(copied(own, levels), "col", bit)
    messages += sent(pack([beside, relayed], levels, [turn + bit for turn in turns], targets, plan))
    kept, passed = join(messages, plan)
    return outer([kept, turned(passed, "row", 1)], plan)


def solution(mesh):
    placed = (P(("row", "col"), None, None), P(("row", "col"), None, None), P(), P(), P(), P())
    return jax.shard_map(
        on_device, mesh=mesh, in_specs=placed, out_specs=P("row", "col"), check_vma=False
    )
```

```python
import functools
import math

import jax
import jax.numpy as jnp
import numpy as np
from jax import lax
from jax.experimental import pallas as pl
from jax.experimental.pallas import tpu as pltpu
from jax.sharding import PartitionSpec as P

GMAX = 18
STEPS = 2
RADIX = 6
SPAN = 2 * GMAX + 1
KX_ROWS = 40
LANES = 128
OMEGA_SQUARED = 0.0625
TILE = 512
VMEM_LIMIT = 40 * 2**20


COSINE_TERMS = 10


def table_rows(grid):
    width = (grid // RADIX) * grid
    x_first = 4 * width
    return width, x_first, x_first + 2 * KX_ROWS


def cosine(phase, grid):
    phase = phase - (phase * 43691 >> 21) * 48
    angle = (phase - grid // 2).astype(jnp.float32) * np.float32(2.0 * math.pi / grid)
    square = angle * angle
    value = jnp.zeros_like(angle)
    for term in reversed(range(COSINE_TERMS)):
        value = value * square - np.float32((-1.0) ** term / math.factorial(2 * term))
    return value


def in_two(values):
    upper = values.astype(jnp.bfloat16)
    return upper, (values - upper.astype(jnp.float32)).astype(jnp.bfloat16)


def write_tables(grid, table_ref, twiddle_ref):
    width, x_first, x_end = table_rows(grid)
    quarter = grid // 4

    def counted(shape, dimension):
        return lax.broadcasted_iota(jnp.int32, shape, dimension)

    row, lane = counted((2 * KX_ROWS, LANES), 0), counted((2 * KX_ROWS, LANES), 1)
    below = (row >= KX_ROWS).astype(jnp.int32)
    place = jnp.where(lane >= grid, lane - grid, lane)
    place = jnp.where(place >= grid, 0, place)
    frequency = row - KX_ROWS * below + (grid - GMAX)
    upper, lower = in_two(cosine(frequency * place + quarter * below, grid))
    mixed = jnp.where(lane < grid, upper.astype(jnp.float32), lower.astype(jnp.float32))
    table_ref[x_first:x_end, :] = mixed.astype(jnp.bfloat16)

    row, lane = counted((16, width), 0), counted((16, width), 1)
    below = (row >= RADIX).astype(jnp.int32)
    residue = jnp.where(row >= 2 * RADIX, 0, row - RADIX * below)
    twiddle_ref[...] = cosine(residue * (lane * 43691 >> 21) + quarter * below, grid)

    lane = counted((1, LANES), 1)
    q = lane * 57 >> 10
    kz = lane - q * GMAX + 1
    y_phase = RADIX * (q + (grid // RADIX - GMAX // RADIX)) * counted((grid // RADIX, LANES), 0)
    z_phase = kz * counted((grid, LANES), 0)
    cos_y, sin_y = cosine(y_phase, grid), cosine(y_phase + 3 * quarter, grid)
    cos_z, sin_z = cosine(z_phase, grid), cosine(z_phase + 3 * quarter, grid)
    for y in range(grid // RADIX):
        cos_here, sin_here = cos_y[y : y + 1], sin_y[y : y + 1]
        whole = (cos_here * cos_z - sin_here * sin_z, -(sin_here * cos_z + cos_here * sin_z))
        for part, values in enumerate(whole):
            for level, piece in enumerate(in_two(values)):
                first = (2 * level + part) * width + y * grid
                table_ref[first : first + grid, :] = piece


def dft_six(re, im):
    half = 0.5
    root = math.sqrt(3.0) / 2.0
    s_re = [re[h] + re[h + 3] for h in range(3)]
    s_im = [im[h] + im[h + 3] for h in range(3)]
    d_re = [re[h] - re[h + 3] for h in range(3)]
    d_im = [im[h] - im[h + 3] for h in range(3)]
    out = [None] * 6
    sum_re, sum_im = s_re[1] + s_re[2], s_im[1] + s_im[2]
    dif_re, dif_im = (s_re[1] - s_re[2]) * root, (s_im[1] - s_im[2]) * root
    out[0] = (s_re[0] + sum_re, s_im[0] + sum_im)
    mid_re, mid_im = s_re[0] - half * sum_re, s_im[0] - half * sum_im
    out[2] = (mid_re + dif_im, mid_im - dif_re)
    out[4] = (mid_re - dif_im, mid_im + dif_re)
    sum_re, sum_im = (d_re[1] + d_re[2]) * root, (d_im[1] + d_im[2]) * root
    dif_re, dif_im = d_re[1] - d_re[2], d_im[1] - d_im[2]
    out[3] = (d_re[0] - dif_re, d_im[0] - dif_im)
    mid_re, mid_im = d_re[0] + half * dif_re, d_im[0] + half * dif_im
    out[1] = (mid_re + sum_im, mid_im - sum_re)
    out[5] = (mid_re - sum_im, mid_im + sum_re)
    return out


def dot(a, b):
    return jnp.dot(a, b, preferred_element_type=jnp.float32)


def own_place():
    return lax.axis_index("row"), lax.axis_index("col")


def spectrum_of(grid, cond, occ, table_ref, twiddle_ref):
    norm = np.float32(grid ** (-1.5))
    width, x_first, x_end = table_rows(grid)
    density = (cond.astype(jnp.float32) * occ.astype(jnp.float32)).astype(jnp.bfloat16)
    x_table = table_ref[x_first:x_end, : 2 * grid]
    section = dot(x_table, jnp.concatenate([density, density], axis=0))
    re = [section[:KX_ROWS, h * width : (h + 1) * width] for h in range(RADIX)]
    im = [section[KX_ROWS:, h * width : (h + 1) * width] for h in range(RADIX)]
    rows = []
    for residue, (d_re, d_im) in enumerate(dft_six(re, im)):
        if residue > 0:
            t_re = twiddle_ref[residue : residue + 1, :]
            t_im = twiddle_ref[RADIX + residue : RADIX + residue + 1, :]
            d_re, d_im = d_re * t_re - d_im * t_im, d_re * t_im + d_im * t_re
        rows.append(jnp.concatenate([d_re, d_im], axis=1))
    whole = jnp.concatenate(rows, axis=0)
    whole_hi = whole.astype(jnp.bfloat16)
    whole_lo = (whole - whole_hi.astype(jnp.float32)).astype(jnp.bfloat16)

    def rotation(first):
        cos_part = table_ref[first : first + width, :]
        sin_part = table_ref[first + width : first + 2 * width, :]
        upper = jnp.concatenate([cos_part, sin_part], axis=1)
        return jnp.concatenate([upper, jnp.concatenate([-sin_part, cos_part], axis=1)], axis=0)

    upper, lower = rotation(0), rotation(2 * width)
    spectrum = (dot(whole_hi, upper) + dot(whole_lo, upper) + dot(whole_hi, lower)) * norm
    parts = []
    for side in range(2):
        own = spectrum[:, side * LANES : (side + 1) * LANES]
        for group in range(RADIX // 2):
            first = 2 * group * KX_ROWS
            parts.append(jnp.concatenate([own[first : first + KX_ROWS], own[first + KX_ROWS : first + 2 * KX_ROWS]], axis=1))
    return jnp.concatenate(parts, axis=0).astype(jnp.bfloat16)


def pair_weights(sources, levels_ref):
    rows, cols = lax.axis_size("row"), lax.axis_size("col")
    r, _ = own_place()
    devices = rows * cols
    pairs = STEPS * len(sources)
    line = lax.broadcasted_iota(jnp.int32, (pairs, 1), 0)
    band = jnp.zeros((pairs, 1), jnp.int32)
    slot = jnp.zeros((pairs, 1), jnp.int32)
    for j, source in enumerate(sources):
        place = r * cols + source
        for step in range(STEPS):
            here = line == STEPS * j + step
            band = jnp.where(here, place, band)
            slot = jnp.where(here, lax.rem(place - step * cols + devices, devices), slot)
    lane = lax.broadcasted_iota(jnp.int32, (pairs, levels_ref.shape[1]), 1)

    def at(which, chosen):
        return jnp.sum(jnp.where(lane == chosen, levels_ref[which : which + 1, :], 0.0), axis=1, keepdims=True)

    gap = at(0, band) - at(1, at(2, slot).astype(jnp.int32))
    return -4.0 * gap / (gap * gap + OMEGA_SQUARED) / (devices * STEPS)


def first_kernel(grid, orbitals_ref, sphere_ref, coef_ref, places_ref, table_ref, twiddle_ref, cube_ref):
    half = grid // 2
    sx, sy, kz = sphere_ref[0:1, :], sphere_ref[1:2, :], sphere_ref[2:3, :]
    kx = jnp.where(sx >= half, sx - grid, sx) + GMAX
    ky = jnp.where(sy >= half, sy - grid, sy) + GMAX
    q = (ky * 43) >> 8
    residue = ky - q * RADIX
    places_ref[0:1, :] = (residue & 1) * LANES + q * GMAX + kz - 1
    places_ref[1:2, :] = (residue >> 1) * KX_ROWS + kx
    write_tables(grid, table_ref, twiddle_ref)
    cube_ref[...] = spectrum_of(grid, orbitals_ref[0], orbitals_ref[1], table_ref, twiddle_ref)

    @pl.when(on_even_core())
    def _():
        pick(cube_ref, places_ref, coef_ref, [0])


def pick(cube_ref, places_ref, coef_ref, pairs):
    groups = RADIX // 2 * KX_ROWS // 8
    half_count = places_ref.shape[1]
    counted = lax.broadcasted_iota(jnp.int32, (2 * LANES, TILE), 0).astype(jnp.float32).astype(jnp.bfloat16)
    line = lax.broadcasted_iota(jnp.int32, (8, TILE), 0)
    parts = [(pair, side) for pair in pairs for side in range(2)]
    for first in range(0, half_count, TILE):
        here = slice(first, first + TILE)
        lane = places_ref[0:1, here].astype(jnp.float32).astype(jnp.bfloat16)
        one_hot = jnp.where(counted == lane, jnp.bfloat16(1), jnp.bfloat16(0))
        found = dot(cube_ref[...], one_hot)
        away = line - places_ref[1:2, here]
        values = [jnp.zeros((8, TILE), jnp.float32)] * len(parts)
        for group in range(groups):
            chosen = away == -8 * group
            for which in range(len(parts)):
                start = (which * groups + group) * 8
                values[which] = jnp.where(chosen, found[start : start + 8], values[which])
        for (pair, side), value in zip(parts, values):
            value = jnp.sum(value, axis=0, keepdims=True).astype(jnp.bfloat16)
            coef_ref[pair : pair + 1, side * half_count + first : side * half_count + first + TILE] = value


def on_even_core():
    return lax.rem(lax.axis_index("row"), 2) == 0


def second_kernel(
    grid, orbitals_ref, occ_ref, first_ref, places_ref, table_ref, twiddle_ref, first_cube_ref, coef_ref, later_ref, cube_ref
):
    picks = first_cube_ref.shape[0]
    later_ref[...] = jnp.zeros_like(later_ref)
    cube_ref[picks:, :] = spectrum_of(grid, orbitals_ref[0], occ_ref[0], table_ref, twiddle_ref)

    @pl.when(on_even_core())
    def _():
        coef_ref[0:1, :] = first_ref[...]
        pick(cube_ref.at[picks:], places_ref, coef_ref, [1])

    @pl.when(jnp.logical_not(on_even_core()))
    def _():
        cube_ref[:picks, :] = first_cube_ref[...]
        pick(cube_ref, places_ref, coef_ref, [0, 1])


def cost(flops, data):
    return pl.CostEstimate(flops=flops, bytes_accessed=data, transcendentals=0)


def in_vmem(count):
    return [pl.BlockSpec(memory_space=pltpu.VMEM)] * count


def transform(cond_orbitals, occ_orbitals, occ_second, sphere_index, band_shape):
    grid = cond_orbitals.shape[1]
    half_count = sphere_index.shape[1]
    width, _, table_count = table_rows(grid)
    which = lax.broadcasted_iota(jnp.int32, (2, *cond_orbitals.shape[1:]), 0)
    orbitals = jnp.where(which == 0, cond_orbitals, occ_orbitals)
    picks = RADIX * KX_ROWS
    params = dict(
        compiler_params=pltpu.CompilerParams(vmem_limit_bytes=VMEM_LIMIT),
        cost_estimate=cost(2 * 10**9, 2 * 10**6),
    )
    handed = pl.pallas_call(
        functools.partial(first_kernel, grid),
        out_shape=[
            jax.ShapeDtypeStruct((1, 2 * half_count), jnp.bfloat16),
            jax.ShapeDtypeStruct((2, half_count), jnp.int32),
            jax.ShapeDtypeStruct((table_count, LANES), jnp.bfloat16),
            jax.ShapeDtypeStruct((16, width), jnp.float32),
            jax.ShapeDtypeStruct((picks, 2 * LANES), jnp.bfloat16),
        ],
        in_specs=in_vmem(2),
        out_specs=in_vmem(5),
        name="first_pair",
        **params,
    )(orbitals, sphere_index)
    return pl.pallas_call(
        functools.partial(second_kernel, grid),
        out_shape=[
            jax.ShapeDtypeStruct((STEPS, 2 * half_count), jnp.bfloat16),
            jax.ShapeDtypeStruct((1, *band_shape), jnp.int32),
        ],
        in_specs=in_vmem(7),
        out_specs=in_vmem(2),
        scratch_shapes=[pltpu.VMEM((STEPS * picks, 2 * LANES), jnp.bfloat16)],
        name="second_pair",
        **params,
    )(orbitals, occ_second, *handed)


def pack_kernel(plan, turns, targets, levels_ref, *refs):
    rows, cols, row_width, col_width = plan
    count = len(refs) - len(targets) - 1
    arrived, outs, mixed_ref = refs[:count], refs[count:-1], refs[-1]
    r, c = own_place()
    first = 0
    for ref in arrived:
        mixed_ref[first : first + ref.shape[0], :] = ref[...].astype(jnp.float32)
        first += ref.shape[0]
    weight = pair_weights([c ^ turn for turn in turns], levels_ref)
    columns = []
    for side in range(2):
        start = pl.multiple_of((c ^ side) * col_width, LANES)
        columns.append((weight * mixed_ref[:, pl.ds(start, col_width)]).astype(jnp.bfloat16))
    for (turn, side), out_ref in zip(targets, outs):
        start = pl.multiple_of((r ^ turn) // 2 * (2 * row_width), LANES)
        out_ref[:, : 2 * row_width] = mixed_ref[:, pl.ds(start, 2 * row_width)].astype(jnp.bfloat16)
        out_ref[:, 2 * row_width :] = columns[side]


def pack(arrived, levels, turns, targets, plan):
    rows, cols, row_width, col_width = plan
    pairs = STEPS * len(turns)
    entries = arrived[0].shape[1]
    shapes = [(pairs, 2 * row_width + col_width)] * len(targets)
    return pl.pallas_call(
        functools.partial(pack_kernel, plan, turns, targets),
        out_shape=[jax.ShapeDtypeStruct(shape, jnp.bfloat16) for shape in shapes],
        in_specs=in_vmem(1 + len(arrived)),
        out_specs=in_vmem(len(shapes)),
        scratch_shapes=[pltpu.VMEM((pairs, entries), jnp.float32)],
        compiler_params=pltpu.CompilerParams(vmem_limit_bytes=VMEM_LIMIT),
        cost_estimate=cost(10**9, 10**6),
        name="pack",
    )(levels, *arrived)


def stacked(refs, lanes):
    return jnp.concatenate([ref[:, lanes].astype(jnp.float32) for ref in refs], axis=0).astype(jnp.bfloat16)


def join_kernel(row_width, *refs):
    messages, outs = refs[:-2], refs[-2:]
    depth = messages[0].shape[0]
    merge = max(1, 16 // depth)
    r, _ = own_place()
    for j in range(0, len(messages), merge):
        here = slice(depth * j, depth * (j + merge))
        columns = stacked(messages[j : j + merge], slice(2 * row_width, None))
        for side, out_ref in enumerate(outs):
            lanes = pl.ds(pl.multiple_of((r & 1 ^ side) * row_width, LANES), row_width)
            out_ref[here, :row_width] = stacked(messages[j : j + merge], lanes)
            out_ref[here, row_width:] = columns


def join(messages, plan):
    rows, cols, row_width, col_width = plan
    depth = messages[0].shape[0]
    return pl.pallas_call(
        functools.partial(join_kernel, row_width),
        out_shape=[jax.ShapeDtypeStruct((depth * len(messages), row_width + col_width), jnp.bfloat16)] * 2,
        in_specs=in_vmem(len(messages)),
        out_specs=in_vmem(2),
        compiler_params=pltpu.CompilerParams(vmem_limit_bytes=VMEM_LIMIT),
        cost_estimate=cost(10**9, 10**6),
        name="join",
    )(*messages)


def outer_kernel(row_width, block, slots, *refs):
    messages, (out_ref, right_ref, held_ref, sems) = refs[:-4], refs[-4:]
    depth = messages[0].shape[0]
    for j, ref in enumerate(messages):
        right_ref[depth * j : depth * (j + 1), :] = ref[:, row_width:]
    count = row_width // block

    def copy_out(i, slot):
        rows = pl.ds(pl.multiple_of(i * block, block), block)
        return pltpu.make_async_copy(held_ref.at[slot], out_ref.at[rows], sems.at[slot])

    def step(i, carry):
        slot = lax.rem(i, slots)

        @pl.when(i >= slots)
        def _():
            copy_out(i - slots, slot).wait()

        here = pl.ds(pl.multiple_of(i * block, block), block)
        left = jnp.concatenate([ref[:, here] for ref in messages], axis=0)
        held_ref[slot] = lax.dot_general(left, right_ref[...], (((0,), (0,)), ((), ())), preferred_element_type=jnp.float32)
        copy_out(i, slot).start()
        return carry

    lax.fori_loop(0, count, step, 0)
    for i in range(max(0, count - slots), count):
        copy_out(i, i % slots).wait()


def outer(messages, plan):
    rows, cols, row_width, col_width = plan
    depth = messages[0].shape[0]
    block = min(256, row_width)
    slots = min(4, row_width // block)
    return pl.pallas_call(
        functools.partial(outer_kernel, row_width, block, slots),
        out_shape=jax.ShapeDtypeStruct((row_width, col_width), jnp.float32),
        in_specs=in_vmem(len(messages)),
        out_specs=pl.BlockSpec(memory_space=pltpu.HBM),
        scratch_shapes=[
            pltpu.VMEM((depth * len(messages), col_width), jnp.bfloat16),
            pltpu.VMEM((slots, block, col_width), jnp.float32),
            pltpu.SemaphoreType.DMA((slots,)),
        ],
        compiler_params=pltpu.CompilerParams(vmem_limit_bytes=VMEM_LIMIT),
        cost_estimate=cost(10**10, 3 * 10**7),
        name="outer",
    )(*messages)


def copy_kernel(value_ref, behind_ref, out_ref):
    out_ref[...] = value_ref[...]


def copied(value, behind):
    return pl.pallas_call(
        copy_kernel,
        out_shape=jax.ShapeDtypeStruct(value.shape, value.dtype),
        in_specs=in_vmem(2),
        out_specs=in_vmem(1)[0],
        compiler_params=pltpu.CompilerParams(vmem_limit_bytes=VMEM_LIMIT),
        cost_estimate=cost(10**6, 10**5),
        name="copied",
    )(value, behind)


def shifted(value, axis, by):
    devices = lax.axis_size(axis)
    return lax.ppermute(value, axis, [(i, (i + by) % devices) for i in range(devices)])


def turned(value, axis, turn):
    devices = lax.axis_size(axis)
    return lax.ppermute(value, axis, [(i, i ^ turn) for i in range(devices)])


def sent_across(value, turn, side, rows, cols):
    moves = [(r * cols + c, (r ^ turn) * cols + (c ^ side)) for r in range(rows) for c in range(cols)]
    return lax.ppermute(value, ("row", "col"), moves)


def on_device(cond_orbitals, occ_orbitals, cond_energy, occ_energy, occ_band, sphere_index):
    rows = lax.axis_size("row")
    cols = lax.axis_size("col")
    entries = 2 * sphere_index.shape[1]
    plan = (rows, cols, entries // rows, entries // cols)
    occ_second = shifted(occ_orbitals, "row", 1)
    own, later = transform(cond_orbitals, occ_orbitals, occ_second, sphere_index, occ_band.shape)
    levels = jnp.stack([cond_energy, occ_energy, (occ_band + later[0]).astype(jnp.float32)])
    targets = [(0, 0)] + [(turn, side) for side in (1, 0) for turn in range(rows - 2, -2, -2) if turn or side]
    targets.append(targets.pop(rows // 2))

    def sent(packed):
        return [packed[0]] + [sent_across(value, *target, rows, cols) for value, target in zip(packed[1:], targets[1:])]

    others, other_turns, bit = [], [], cols // 2
    while bit > 2:
        held = jnp.concatenate([own, *others], axis=0) if others else own
        others.append(turned(held, "col", bit))
        other_turns += [turn + bit for turn in [0, *other_turns]]
        bit //= 2
    turns = [0, *other_turns]
    messages = sent(pack([own, *others], levels, turns, targets, plan))
    relayed = turned(jnp.concatenate(others, axis=0) if len(others) > 1 else others[0], "col", bit)
    beside = turned(copied(own, levels), "col", bit)
    messages += sent(pack([beside, relayed], levels, [turn + bit for turn in turns], targets, plan))
    kept, passed = join(messages, plan)
    return outer([kept, turned(passed, "row", 1)], plan)


def solution(mesh):
    placed = (P(("row", "col"), None, None), P(("row", "col"), None, None), P(), P(), P(), P())
    return jax.shard_map(
        on_device, mesh=mesh, in_specs=placed, out_specs=P("row", "col"), check_vma=False
    )
```

```python
import functools
import math

import jax
import jax.numpy as jnp
import numpy as np
from jax import lax
from jax.experimental import pallas as pl
from jax.experimental.pallas import tpu as pltpu
from jax.sharding import PartitionSpec as P

GMAX = 18
STEPS = 2
RADIX = 6
SPAN = 2 * GMAX + 1
KX_ROWS = 40
LANES = 128
OMEGA_SQUARED = 0.0625
TILE = 512
VMEM_LIMIT = 40 * 2**20


COSINE_TERMS = 10


def table_rows(grid):
    width = (grid // RADIX) * grid
    x_first = 4 * width
    return width, x_first, x_first + 2 * KX_ROWS


def cosine(phase, grid):
    phase = phase - (phase * 43691 >> 21) * 48
    angle = (phase - grid // 2).astype(jnp.float32) * np.float32(2.0 * math.pi / grid)
    square = angle * angle
    value = jnp.zeros_like(angle)
    for term in reversed(range(COSINE_TERMS)):
        value = value * square - np.float32((-1.0) ** term / math.factorial(2 * term))
    return value


def in_two(values):
    upper = values.astype(jnp.bfloat16)
    return upper, (values - upper.astype(jnp.float32)).astype(jnp.bfloat16)


def write_tables(grid, table_ref, twiddle_ref):
    width, x_first, x_end = table_rows(grid)
    quarter = grid // 4

    def counted(shape, dimension):
        return lax.broadcasted_iota(jnp.int32, shape, dimension)

    row, lane = counted((2 * KX_ROWS, LANES), 0), counted((2 * KX_ROWS, LANES), 1)
    below = (row >= KX_ROWS).astype(jnp.int32)
    place = jnp.where(lane >= grid, lane - grid, lane)
    place = jnp.where(place >= grid, 0, place)
    frequency = row - KX_ROWS * below + (grid - GMAX)
    upper, lower = in_two(cosine(frequency * place + quarter * below, grid))
    mixed = jnp.where(lane < grid, upper.astype(jnp.float32), lower.astype(jnp.float32))
    table_ref[x_first:x_end, :] = mixed.astype(jnp.bfloat16)

    row, lane = counted((16, width), 0), counted((16, width), 1)
    below = (row >= RADIX).astype(jnp.int32)
    residue = jnp.where(row >= 2 * RADIX, 0, row - RADIX * below)
    twiddle_ref[...] = cosine(residue * (lane * 43691 >> 21) + quarter * below, grid)

    lane = counted((1, LANES), 1)
    q = lane * 57 >> 10
    kz = lane - q * GMAX + 1
    y_phase = RADIX * (q + (grid // RADIX - GMAX // RADIX)) * counted((grid // RADIX, LANES), 0)
    z_phase = kz * counted((grid, LANES), 0)
    cos_y, sin_y = cosine(y_phase, grid), cosine(y_phase + 3 * quarter, grid)
    cos_z, sin_z = cosine(z_phase, grid), cosine(z_phase + 3 * quarter, grid)
    for y in range(grid // RADIX):
        cos_here, sin_here = cos_y[y : y + 1], sin_y[y : y + 1]
        whole = (cos_here * cos_z - sin_here * sin_z, -(sin_here * cos_z + cos_here * sin_z))
        for part, values in enumerate(whole):
            for level, piece in enumerate(in_two(values)):
                first = (2 * level + part) * width + y * grid
                table_ref[first : first + grid, :] = piece


def dft_six(re, im):
    half = 0.5
    root = math.sqrt(3.0) / 2.0
    s_re = [re[h] + re[h + 3] for h in range(3)]
    s_im = [im[h] + im[h + 3] for h in range(3)]
    d_re = [re[h] - re[h + 3] for h in range(3)]
    d_im = [im[h] - im[h + 3] for h in range(3)]
    out = [None] * 6
    sum_re, sum_im = s_re[1] + s_re[2], s_im[1] + s_im[2]
    dif_re, dif_im = (s_re[1] - s_re[2]) * root, (s_im[1] - s_im[2]) * root
    out[0] = (s_re[0] + sum_re, s_im[0] + sum_im)
    mid_re, mid_im = s_re[0] - half * sum_re, s_im[0] - half * sum_im
    out[2] = (mid_re + dif_im, mid_im - dif_re)
    out[4] = (mid_re - dif_im, mid_im + dif_re)
    sum_re, sum_im = (d_re[1] + d_re[2]) * root, (d_im[1] + d_im[2]) * root
    dif_re, dif_im = d_re[1] - d_re[2], d_im[1] - d_im[2]
    out[3] = (d_re[0] - dif_re, d_im[0] - dif_im)
    mid_re, mid_im = d_re[0] + half * dif_re, d_im[0] + half * dif_im
    out[1] = (mid_re + sum_im, mid_im - sum_re)
    out[5] = (mid_re - sum_im, mid_im + sum_re)
    return out


def dot(a, b):
    return jnp.dot(a, b, preferred_element_type=jnp.float32)


def own_place():
    return lax.axis_index("row"), lax.axis_index("col")


def spectrum_of(grid, cond, occ, table_ref, twiddle_ref):
    norm = np.float32(grid ** (-1.5))
    width, x_first, x_end = table_rows(grid)
    density = (cond.astype(jnp.float32) * occ.astype(jnp.float32)).astype(jnp.bfloat16)
    x_table = table_ref[x_first:x_end, : 2 * grid]
    section = dot(x_table, jnp.concatenate([density, density], axis=0))
    re = [section[:KX_ROWS, h * width : (h + 1) * width] for h in range(RADIX)]
    im = [section[KX_ROWS:, h * width : (h + 1) * width] for h in range(RADIX)]
    rows = []
    for residue, (d_re, d_im) in enumerate(dft_six(re, im)):
        if residue > 0:
            t_re = twiddle_ref[residue : residue + 1, :]
            t_im = twiddle_ref[RADIX + residue : RADIX + residue + 1, :]
            d_re, d_im = d_re * t_re - d_im * t_im, d_re * t_im + d_im * t_re
        rows.append(jnp.concatenate([d_re, d_im], axis=1))
    whole = jnp.concatenate(rows, axis=0)
    whole_hi = whole.astype(jnp.bfloat16)
    whole_lo = (whole - whole_hi.astype(jnp.float32)).astype(jnp.bfloat16)

    def rotation(first):
        cos_part = table_ref[first : first + width, :]
        sin_part = table_ref[first + width : first + 2 * width, :]
        upper = jnp.concatenate([cos_part, sin_part], axis=1)
        return jnp.concatenate([upper, jnp.concatenate([-sin_part, cos_part], axis=1)], axis=0)

    upper, lower = rotation(0), rotation(2 * width)
    spectrum = (dot(whole_hi, upper) + dot(whole_lo, upper) + dot(whole_hi, lower)) * norm
    parts = []
    for side in range(2):
        own = spectrum[:, side * LANES : (side + 1) * LANES]
        for group in range(RADIX // 2):
            first = 2 * group * KX_ROWS
            parts.append(jnp.concatenate([own[first : first + KX_ROWS], own[first + KX_ROWS : first + 2 * KX_ROWS]], axis=1))
    return jnp.concatenate(parts, axis=0).astype(jnp.bfloat16)


def pair_weights(sources, levels_ref):
    rows, cols = lax.axis_size("row"), lax.axis_size("col")
    r, _ = own_place()
    devices = rows * cols
    pairs = STEPS * len(sources)
    line = lax.broadcasted_iota(jnp.int32, (pairs, 1), 0)
    band = jnp.zeros((pairs, 1), jnp.int32)
    slot = jnp.zeros((pairs, 1), jnp.int32)
    for j, source in enumerate(sources):
        place = r * cols + source
        for step in range(STEPS):
            here = line == STEPS * j + step
            band = jnp.where(here, place, band)
            slot = jnp.where(here, lax.rem(place - step * cols + devices, devices), slot)
    lane = lax.broadcasted_iota(jnp.int32, (pairs, levels_ref.shape[1]), 1)

    def at(which, chosen):
        return jnp.sum(jnp.where(lane == chosen, levels_ref[which : which + 1, :], 0.0), axis=1, keepdims=True)

    gap = at(0, band) - at(1, at(2, slot).astype(jnp.int32))
    return -4.0 * gap / (gap * gap + OMEGA_SQUARED) / (devices * STEPS)


def first_kernel(grid, orbitals_ref, sphere_ref, coef_ref, places_ref, table_ref, twiddle_ref, cube_ref):
    half = grid // 2
    sx, sy, kz = sphere_ref[0:1, :], sphere_ref[1:2, :], sphere_ref[2:3, :]
    kx = jnp.where(sx >= half, sx - grid, sx) + GMAX
    ky = jnp.where(sy >= half, sy - grid, sy) + GMAX
    q = (ky * 43) >> 8
    residue = ky - q * RADIX
    places_ref[0:1, :] = (residue & 1) * LANES + q * GMAX + kz - 1
    places_ref[1:2, :] = (residue >> 1) * KX_ROWS + kx
    write_tables(grid, table_ref, twiddle_ref)
    cube_ref[...] = spectrum_of(grid, orbitals_ref[0], orbitals_ref[1], table_ref, twiddle_ref)

    @pl.when(on_even_core())
    def _():
        pick(cube_ref, places_ref, coef_ref, [0])


def pick(cube_ref, places_ref, coef_ref, pairs):
    groups = RADIX // 2 * KX_ROWS // 8
    half_count = places_ref.shape[1]
    counted = lax.broadcasted_iota(jnp.int32, (2 * LANES, TILE), 0).astype(jnp.float32).astype(jnp.bfloat16)
    line = lax.broadcasted_iota(jnp.int32, (8, TILE), 0)
    parts = [(pair, side) for pair in pairs for side in range(2)]
    for first in range(0, half_count, TILE):
        here = slice(first, first + TILE)
        lane = places_ref[0:1, here].astype(jnp.float32).astype(jnp.bfloat16)
        one_hot = jnp.where(counted == lane, jnp.bfloat16(1), jnp.bfloat16(0))
        found = dot(cube_ref[...], one_hot)
        away = line - places_ref[1:2, here]
        values = [jnp.zeros((8, TILE), jnp.float32)] * len(parts)
        for group in range(groups):
            chosen = away == -8 * group
            for which in range(len(parts)):
                start = (which * groups + group) * 8
                values[which] = jnp.where(chosen, found[start : start + 8], values[which])
        for (pair, side), value in zip(parts, values):
            value = jnp.sum(value, axis=0, keepdims=True).astype(jnp.bfloat16)
            coef_ref[pair : pair + 1, side * half_count + first : side * half_count + first + TILE] = value


def on_even_core():
    return lax.rem(lax.axis_index("row"), 2) == 0


def second_kernel(
    grid, orbitals_ref, occ_ref, first_ref, places_ref, table_ref, twiddle_ref, first_cube_ref, coef_ref, later_ref, cube_ref
):
    picks = first_cube_ref.shape[0]
    later_ref[...] = jnp.zeros_like(later_ref)
    cube_ref[picks:, :] = spectrum_of(grid, orbitals_ref[0], occ_ref[0], table_ref, twiddle_ref)

    @pl.when(on_even_core())
    def _():
        coef_ref[0:1, :] = first_ref[...]
        pick(cube_ref.at[picks:], places_ref, coef_ref, [1])

    @pl.when(jnp.logical_not(on_even_core()))
    def _():
        cube_ref[:picks, :] = first_cube_ref[...]
        pick(cube_ref, places_ref, coef_ref, [0, 1])


def cost(flops, data):
    return pl.CostEstimate(flops=flops, bytes_accessed=data, transcendentals=0)


def in_vmem(count):
    return [pl.BlockSpec(memory_space=pltpu.VMEM)] * count


def transform(cond_orbitals, occ_orbitals, occ_second, sphere_index, band_shape):
    grid = cond_orbitals.shape[1]
    half_count = sphere_index.shape[1]
    width, _, table_count = table_rows(grid)
    which = lax.broadcasted_iota(jnp.int32, (2, *cond_orbitals.shape[1:]), 0)
    orbitals = jnp.where(which == 0, cond_orbitals, occ_orbitals)
    picks = RADIX * KX_ROWS
    params = dict(
        compiler_params=pltpu.CompilerParams(vmem_limit_bytes=VMEM_LIMIT),
        cost_estimate=cost(2 * 10**9, 2 * 10**6),
    )
    handed = pl.pallas_call(
        functools.partial(first_kernel, grid),
        out_shape=[
            jax.ShapeDtypeStruct((1, 2 * half_count), jnp.bfloat16),
            jax.ShapeDtypeStruct((2, half_count), jnp.int32),
            jax.ShapeDtypeStruct((table_count, LANES), jnp.bfloat16),
            jax.ShapeDtypeStruct((16, width), jnp.float32),
            jax.ShapeDtypeStruct((picks, 2 * LANES), jnp.bfloat16),
        ],
        in_specs=in_vmem(2),
        out_specs=in_vmem(5),
        name="first_pair",
        **params,
    )(orbitals, sphere_index)
    return pl.pallas_call(
        functools.partial(second_kernel, grid),
        out_shape=[
            jax.ShapeDtypeStruct((STEPS, 2 * half_count), jnp.bfloat16),
            jax.ShapeDtypeStruct((1, *band_shape), jnp.int32),
        ],
        in_specs=in_vmem(7),
        out_specs=in_vmem(2),
        scratch_shapes=[pltpu.VMEM((STEPS * picks, 2 * LANES), jnp.bfloat16)],
        name="second_pair",
        **params,
    )(orbitals, occ_second, *handed)


def pack_kernel(plan, turns, targets, levels_ref, *refs):
    rows, cols, row_width, col_width = plan
    count = len(refs) - len(targets) - 1
    arrived, outs, mixed_ref = refs[:count], refs[count:-1], refs[-1]
    r, c = own_place()
    first = 0
    for ref in arrived:
        mixed_ref[first : first + ref.shape[0], :] = ref[...].astype(jnp.float32)
        first += ref.shape[0]
    weight = pair_weights([c ^ turn for turn in turns], levels_ref)
    columns = []
    for side in range(2):
        start = pl.multiple_of((c ^ side) * col_width, LANES)
        columns.append((weight * mixed_ref[:, pl.ds(start, col_width)]).astype(jnp.bfloat16))
    for (turn, side), out_ref in zip(targets, outs):
        start = pl.multiple_of((r ^ turn) // 2 * (2 * row_width), LANES)
        out_ref[:, : 2 * row_width] = mixed_ref[:, pl.ds(start, 2 * row_width)].astype(jnp.bfloat16)
        out_ref[:, 2 * row_width :] = columns[side]


def pack(arrived, levels, turns, targets, plan):
    rows, cols, row_width, col_width = plan
    pairs = STEPS * len(turns)
    entries = arrived[0].shape[1]
    shapes = [(pairs, 2 * row_width + col_width)] * len(targets)
    return pl.pallas_call(
        functools.partial(pack_kernel, plan, turns, targets),
        out_shape=[jax.ShapeDtypeStruct(shape, jnp.bfloat16) for shape in shapes],
        in_specs=in_vmem(1 + len(arrived)),
        out_specs=in_vmem(len(shapes)),
        scratch_shapes=[pltpu.VMEM((pairs, entries), jnp.float32)],
        compiler_params=pltpu.CompilerParams(vmem_limit_bytes=VMEM_LIMIT),
        cost_estimate=cost(10**9, 10**6),
        name="pack",
    )(levels, *arrived)


def stacked(refs, lanes):
    return jnp.concatenate([ref[:, lanes].astype(jnp.float32) for ref in refs], axis=0).astype(jnp.bfloat16)


def join_kernel(row_width, *refs):
    messages, outs = refs[:-2], refs[-2:]
    depth = messages[0].shape[0]
    merge = max(1, 16 // depth)
    r, _ = own_place()
    for j in range(0, len(messages), merge):
        here = slice(depth * j, depth * (j + merge))
        columns = stacked(messages[j : j + merge], slice(2 * row_width, None))
        for side, out_ref in enumerate(outs):
            lanes = pl.ds(pl.multiple_of((r & 1 ^ side) * row_width, LANES), row_width)
            out_ref[here, :row_width] = stacked(messages[j : j + merge], lanes)
            out_ref[here, row_width:] = columns


def join(messages, plan):
    rows, cols, row_width, col_width = plan
    depth = messages[0].shape[0]
    return pl.pallas_call(
        functools.partial(join_kernel, row_width),
        out_shape=[jax.ShapeDtypeStruct((depth * len(messages), row_width + col_width), jnp.bfloat16)] * 2,
        in_specs=in_vmem(len(messages)),
        out_specs=in_vmem(2),
        compiler_params=pltpu.CompilerParams(vmem_limit_bytes=VMEM_LIMIT),
        cost_estimate=cost(10**9, 10**6),
        name="join",
    )(*messages)


def outer_kernel(row_width, block, slots, *refs):
    messages, (out_ref, right_ref, held_ref, sems) = refs[:-4], refs[-4:]
    depth = messages[0].shape[0]
    for j, ref in enumerate(messages):
        right_ref[depth * j : depth * (j + 1), :] = ref[:, row_width:]
    count = row_width // block

    def copy_out(i, slot):
        rows = pl.ds(pl.multiple_of(i * block, block), block)
        return pltpu.make_async_copy(held_ref.at[slot], out_ref.at[rows], sems.at[slot])

    def product(first, size):
        left = jnp.concatenate([ref[:, pl.ds(first, size)] for ref in messages], axis=0)
        return lax.dot_general(left, right_ref[...], (((0,), (0,)), ((), ())), preferred_element_type=jnp.float32)

    def step(i, carry):
        slot = lax.rem(i, slots)

        @pl.when(i >= slots)
        def _():
            copy_out(i - slots, slot).wait()

        held_ref[slot] = product(pl.multiple_of(i * block, block), block)
        copy_out(i, slot).start()
        return carry

    half = block // 2
    for part in range(2):
        here = pl.ds(part * half, half)
        held_ref[0, part * half : (part + 1) * half, :] = product(part * half, half)
        pltpu.make_async_copy(held_ref.at[0, here], out_ref.at[here], sems.at[0]).start()
    lax.fori_loop(1, count, step, 0)
    for i in range(max(0, count - slots), count):
        copy_out(i, i % slots).wait()


def outer(messages, plan):
    rows, cols, row_width, col_width = plan
    depth = messages[0].shape[0]
    block = min(256, row_width)
    slots = min(4, row_width // block)
    return pl.pallas_call(
        functools.partial(outer_kernel, row_width, block, slots),
        out_shape=jax.ShapeDtypeStruct((row_width, col_width), jnp.float32),
        in_specs=in_vmem(len(messages)),
        out_specs=pl.BlockSpec(memory_space=pltpu.HBM),
        scratch_shapes=[
            pltpu.VMEM((depth * len(messages), col_width), jnp.bfloat16),
            pltpu.VMEM((slots, block, col_width), jnp.float32),
            pltpu.SemaphoreType.DMA((slots,)),
        ],
        compiler_params=pltpu.CompilerParams(vmem_limit_bytes=VMEM_LIMIT),
        cost_estimate=cost(10**10, 3 * 10**7),
        name="outer",
    )(*messages)


def copy_kernel(value_ref, behind_ref, out_ref):
    out_ref[...] = value_ref[...]


def copied(value, behind):
    return pl.pallas_call(
        copy_kernel,
        out_shape=jax.ShapeDtypeStruct(value.shape, value.dtype),
        in_specs=in_vmem(2),
        out_specs=in_vmem(1)[0],
        compiler_params=pltpu.CompilerParams(vmem_limit_bytes=VMEM_LIMIT),
        cost_estimate=cost(10**6, 10**5),
        name="copied",
    )(value, behind)


def shifted(value, axis, by):
    devices = lax.axis_size(axis)
    return lax.ppermute(value, axis, [(i, (i + by) % devices) for i in range(devices)])


def turned(value, axis, turn):
    devices = lax.axis_size(axis)
    return lax.ppermute(value, axis, [(i, i ^ turn) for i in range(devices)])


def sent_across(value, turn, side, rows, cols):
    moves = [(r * cols + c, (r ^ turn) * cols + (c ^ side)) for r in range(rows) for c in range(cols)]
    return lax.ppermute(value, ("row", "col"), moves)


def on_device(cond_orbitals, occ_orbitals, cond_energy, occ_energy, occ_band, sphere_index):
    rows = lax.axis_size("row")
    cols = lax.axis_size("col")
    entries = 2 * sphere_index.shape[1]
    plan = (rows, cols, entries // rows, entries // cols)
    occ_second = shifted(occ_orbitals, "row", 1)
    own, later = transform(cond_orbitals, occ_orbitals, occ_second, sphere_index, occ_band.shape)
    levels = jnp.stack([cond_energy, occ_energy, (occ_band + later[0]).astype(jnp.float32)])
    targets = [(0, 0)] + [(turn, side) for side in (1, 0) for turn in range(rows - 2, -2, -2) if turn or side]
    targets.append(targets.pop(rows // 2))

    def sent(packed):
        return [packed[0]] + [sent_across(value, *target, rows, cols) for value, target in zip(packed[1:], targets[1:])]

    others, other_turns, bit = [], [], cols // 2
    while bit > 2:
        held = jnp.concatenate([own, *others], axis=0) if others else own
        others.append(turned(held, "col", bit))
        other_turns += [turn + bit for turn in [0, *other_turns]]
        bit //= 2
    turns = [0, *other_turns]
    early = sent(pack([own, *others], levels, turns, targets, plan))
    relayed = turned(jnp.concatenate(others, axis=0) if len(others) > 1 else others[0], "col", bit)
    beside = turned(copied(own, levels), "col", bit)
    late = sent(pack([beside, relayed], levels, [turn + bit for turn in turns], targets, plan))
    joined = []
    for messages in (early, late):
        kept, passed = join(messages, plan)
        joined += [kept, turned(passed, "row", 1)]
    return outer(joined, plan)


def solution(mesh):
    placed = (P(("row", "col"), None, None), P(("row", "col"), None, None), P(), P(), P(), P())
    return jax.shard_map(
        on_device, mesh=mesh, in_specs=placed, out_specs=P("row", "col"), check_vma=False
    )
```

```python
import functools
import math

import jax
import jax.numpy as jnp
import numpy as np
from jax import lax
from jax.experimental import pallas as pl
from jax.experimental.pallas import tpu as pltpu
from jax.sharding import PartitionSpec as P

GMAX = 18
STEPS = 2
RADIX = 6
SPAN = 2 * GMAX + 1
KX_ROWS = 40
LANES = 128
OMEGA_SQUARED = 0.0625
TILE = 512
VMEM_LIMIT = 40 * 2**20


COSINE_TERMS = 10


def table_rows(grid):
    width = (grid // RADIX) * grid
    x_first = 4 * width
    return width, x_first, x_first + 2 * KX_ROWS


def cosine(phase, grid):
    phase = phase - (phase * 43691 >> 21) * 48
    angle = (phase - grid // 2).astype(jnp.float32) * np.float32(2.0 * math.pi / grid)
    square = angle * angle
    value = jnp.zeros_like(angle)
    for term in reversed(range(COSINE_TERMS)):
        value = value * square - np.float32((-1.0) ** term / math.factorial(2 * term))
    return value


def in_two(values):
    upper = values.astype(jnp.bfloat16)
    return upper, (values - upper.astype(jnp.float32)).astype(jnp.bfloat16)


def write_tables(grid, table_ref, twiddle_ref):
    width, x_first, x_end = table_rows(grid)
    quarter = grid // 4

    def counted(shape, dimension):
        return lax.broadcasted_iota(jnp.int32, shape, dimension)

    row, lane = counted((2 * KX_ROWS, LANES), 0), counted((2 * KX_ROWS, LANES), 1)
    below = (row >= KX_ROWS).astype(jnp.int32)
    place = jnp.where(lane >= grid, lane - grid, lane)
    place = jnp.where(place >= grid, 0, place)
    frequency = row - KX_ROWS * below + (grid - GMAX)
    upper, lower = in_two(cosine(frequency * place + quarter * below, grid))
    mixed = jnp.where(lane < grid, upper.astype(jnp.float32), lower.astype(jnp.float32))
    table_ref[x_first:x_end, :] = mixed.astype(jnp.bfloat16)

    row, lane = counted((16, width), 0), counted((16, width), 1)
    below = (row >= RADIX).astype(jnp.int32)
    residue = jnp.where(row >= 2 * RADIX, 0, row - RADIX * below)
    twiddle_ref[...] = cosine(residue * (lane * 43691 >> 21) + quarter * below, grid)

    lane = counted((1, LANES), 1)
    q = lane * 57 >> 10
    kz = lane - q * GMAX + 1
    y_phase = RADIX * (q + (grid // RADIX - GMAX // RADIX)) * counted((grid // RADIX, LANES), 0)
    z_phase = kz * counted((grid, LANES), 0)
    cos_y, sin_y = cosine(y_phase, grid), cosine(y_phase + 3 * quarter, grid)
    cos_z, sin_z = cosine(z_phase, grid), cosine(z_phase + 3 * quarter, grid)
    for y in range(grid // RADIX):
        cos_here, sin_here = cos_y[y : y + 1], sin_y[y : y + 1]
        whole = (cos_here * cos_z - sin_here * sin_z, -(sin_here * cos_z + cos_here * sin_z))
        for part, values in enumerate(whole):
            for level, piece in enumerate(in_two(values)):
                first = (2 * level + part) * width + y * grid
                table_ref[first : first + grid, :] = piece


def dft_six(re, im):
    half = 0.5
    root = math.sqrt(3.0) / 2.0
    s_re = [re[h] + re[h + 3] for h in range(3)]
    s_im = [im[h] + im[h + 3] for h in range(3)]
    d_re = [re[h] - re[h + 3] for h in range(3)]
    d_im = [im[h] - im[h + 3] for h in range(3)]
    out = [None] * 6
    sum_re, sum_im = s_re[1] + s_re[2], s_im[1] + s_im[2]
    dif_re, dif_im = (s_re[1] - s_re[2]) * root, (s_im[1] - s_im[2]) * root
    out[0] = (s_re[0] + sum_re, s_im[0] + sum_im)
    mid_re, mid_im = s_re[0] - half * sum_re, s_im[0] - half * sum_im
    out[2] = (mid_re + dif_im, mid_im - dif_re)
    out[4] = (mid_re - dif_im, mid_im + dif_re)
    sum_re, sum_im = (d_re[1] + d_re[2]) * root, (d_im[1] + d_im[2]) * root
    dif_re, dif_im = d_re[1] - d_re[2], d_im[1] - d_im[2]
    out[3] = (d_re[0] - dif_re, d_im[0] - dif_im)
    mid_re, mid_im = d_re[0] + half * dif_re, d_im[0] + half * dif_im
    out[1] = (mid_re + sum_im, mid_im - sum_re)
    out[5] = (mid_re - sum_im, mid_im + sum_re)
    return out


def dot(a, b):
    return jnp.dot(a, b, preferred_element_type=jnp.float32)


def own_place():
    return lax.axis_index("row"), lax.axis_index("col")


def spectrum_of(grid, cond, occ, table_ref, twiddle_ref):
    norm = np.float32(grid ** (-1.5))
    width, x_first, x_end = table_rows(grid)
    density = (cond.astype(jnp.float32) * occ.astype(jnp.float32)).astype(jnp.bfloat16)
    x_table = table_ref[x_first:x_end, : 2 * grid]
    section = dot(x_table, jnp.concatenate([density, density], axis=0))
    re = [section[:KX_ROWS, h * width : (h + 1) * width] for h in range(RADIX)]
    im = [section[KX_ROWS:, h * width : (h + 1) * width] for h in range(RADIX)]
    rows = []
    for residue, (d_re, d_im) in enumerate(dft_six(re, im)):
        if residue > 0:
            t_re = twiddle_ref[residue : residue + 1, :]
            t_im = twiddle_ref[RADIX + residue : RADIX + residue + 1, :]
            d_re, d_im = d_re * t_re - d_im * t_im, d_re * t_im + d_im * t_re
        rows.append(jnp.concatenate([d_re, d_im], axis=1))
    whole = jnp.concatenate(rows, axis=0)
    whole_hi = whole.astype(jnp.bfloat16)
    whole_lo = (whole - whole_hi.astype(jnp.float32)).astype(jnp.bfloat16)

    def rotation(first):
        cos_part = table_ref[first : first + width, :]
        sin_part = table_ref[first + width : first + 2 * width, :]
        upper = jnp.concatenate([cos_part, sin_part], axis=1)
        return jnp.concatenate([upper, jnp.concatenate([-sin_part, cos_part], axis=1)], axis=0)

    upper, lower = rotation(0), rotation(2 * width)
    spectrum = (dot(whole_hi, upper) + dot(whole_lo, upper) + dot(whole_hi, lower)) * norm
    parts = []
    for side in range(2):
        own = spectrum[:, side * LANES : (side + 1) * LANES]
        for group in range(RADIX // 2):
            first = 2 * group * KX_ROWS
            parts.append(jnp.concatenate([own[first : first + KX_ROWS], own[first + KX_ROWS : first + 2 * KX_ROWS]], axis=1))
    return jnp.concatenate(parts, axis=0).astype(jnp.bfloat16)


def pair_weights(sources, levels_ref):
    rows, cols = lax.axis_size("row"), lax.axis_size("col")
    r, _ = own_place()
    devices = rows * cols
    pairs = STEPS * len(sources)
    line = lax.broadcasted_iota(jnp.int32, (pairs, 1), 0)
    band = jnp.zeros((pairs, 1), jnp.int32)
    slot = jnp.zeros((pairs, 1), jnp.int32)
    for j, source in enumerate(sources):
        place = r * cols + source
        for step in range(STEPS):
            here = line == STEPS * j + step
            band = jnp.where(here, place, band)
            slot = jnp.where(here, lax.rem(place - step * cols + devices, devices), slot)
    lane = lax.broadcasted_iota(jnp.int32, (pairs, levels_ref.shape[1]), 1)

    def at(which, chosen):
        return jnp.sum(jnp.where(lane == chosen, levels_ref[which : which + 1, :], 0.0), axis=1, keepdims=True)

    gap = at(0, band) - at(1, at(2, slot).astype(jnp.int32))
    return -4.0 * gap / (gap * gap + OMEGA_SQUARED) / (devices * STEPS)


def first_kernel(grid, orbitals_ref, sphere_ref, coef_ref, places_ref, table_ref, twiddle_ref, cube_ref):
    half = grid // 2
    sx, sy, kz = sphere_ref[0:1, :], sphere_ref[1:2, :], sphere_ref[2:3, :]
    kx = jnp.where(sx >= half, sx - grid, sx) + GMAX
    ky = jnp.where(sy >= half, sy - grid, sy) + GMAX
    q = (ky * 43) >> 8
    residue = ky - q * RADIX
    places_ref[0:1, :] = (residue & 1) * LANES + q * GMAX + kz - 1
    places_ref[1:2, :] = (residue >> 1) * KX_ROWS + kx
    write_tables(grid, table_ref, twiddle_ref)
    cube_ref[...] = spectrum_of(grid, orbitals_ref[0], orbitals_ref[1], table_ref, twiddle_ref)

    @pl.when(on_even_core())
    def _():
        pick(cube_ref, places_ref, coef_ref, [0])


def pick(cube_ref, places_ref, coef_ref, pairs):
    groups = RADIX // 2 * KX_ROWS // 8
    half_count = places_ref.shape[1]
    counted = lax.broadcasted_iota(jnp.int32, (2 * LANES, TILE), 0).astype(jnp.float32).astype(jnp.bfloat16)
    line = lax.broadcasted_iota(jnp.int32, (8, TILE), 0)
    parts = [(pair, side) for pair in pairs for side in range(2)]
    for first in range(0, half_count, TILE):
        here = slice(first, first + TILE)
        lane = places_ref[0:1, here].astype(jnp.float32).astype(jnp.bfloat16)
        one_hot = jnp.where(counted == lane, jnp.bfloat16(1), jnp.bfloat16(0))
        found = dot(cube_ref[...], one_hot)
        away = line - places_ref[1:2, here]
        values = [jnp.zeros((8, TILE), jnp.float32)] * len(parts)
        for group in range(groups):
            chosen = away == -8 * group
            for which in range(len(parts)):
                start = (which * groups + group) * 8
                values[which] = jnp.where(chosen, found[start : start + 8], values[which])
        for (pair, side), value in zip(parts, values):
            value = jnp.sum(value, axis=0, keepdims=True).astype(jnp.bfloat16)
            coef_ref[pair : pair + 1, side * half_count + first : side * half_count + first + TILE] = value


def on_even_core():
    return lax.rem(lax.axis_index("row"), 2) == 0


def second_kernel(
    grid, orbitals_ref, occ_ref, first_ref, places_ref, table_ref, twiddle_ref, first_cube_ref, coef_ref, later_ref, cube_ref
):
    picks = first_cube_ref.shape[0]
    later_ref[...] = jnp.zeros_like(later_ref)
    cube_ref[picks:, :] = spectrum_of(grid, orbitals_ref[0], occ_ref[0], table_ref, twiddle_ref)

    @pl.when(on_even_core())
    def _():
        coef_ref[0:1, :] = first_ref[...]
        pick(cube_ref.at[picks:], places_ref, coef_ref, [1])

    @pl.when(jnp.logical_not(on_even_core()))
    def _():
        cube_ref[:picks, :] = first_cube_ref[...]
        pick(cube_ref, places_ref, coef_ref, [0, 1])


def cost(flops, data):
    return pl.CostEstimate(flops=flops, bytes_accessed=data, transcendentals=0)


def in_vmem(count):
    return [pl.BlockSpec(memory_space=pltpu.VMEM)] * count


def transform(cond_orbitals, occ_orbitals, occ_second, sphere_index, band_shape):
    grid = cond_orbitals.shape[1]
    half_count = sphere_index.shape[1]
    width, _, table_count = table_rows(grid)
    which = lax.broadcasted_iota(jnp.int32, (2, *cond_orbitals.shape[1:]), 0)
    orbitals = jnp.where(which == 0, cond_orbitals, occ_orbitals)
    picks = RADIX * KX_ROWS
    params = dict(
        compiler_params=pltpu.CompilerParams(vmem_limit_bytes=VMEM_LIMIT),
        cost_estimate=cost(2 * 10**9, 2 * 10**6),
    )
    handed = pl.pallas_call(
        functools.partial(first_kernel, grid),
        out_shape=[
            jax.ShapeDtypeStruct((1, 2 * half_count), jnp.bfloat16),
            jax.ShapeDtypeStruct((2, half_count), jnp.int32),
            jax.ShapeDtypeStruct((table_count, LANES), jnp.bfloat16),
            jax.ShapeDtypeStruct((16, width), jnp.float32),
            jax.ShapeDtypeStruct((picks, 2 * LANES), jnp.bfloat16),
        ],
        in_specs=in_vmem(2),
        out_specs=in_vmem(5),
        name="first_pair",
        **params,
    )(orbitals, sphere_index)
    return pl.pallas_call(
        functools.partial(second_kernel, grid),
        out_shape=[
            jax.ShapeDtypeStruct((STEPS, 2 * half_count), jnp.bfloat16),
            jax.ShapeDtypeStruct((1, *band_shape), jnp.int32),
        ],
        in_specs=in_vmem(7),
        out_specs=in_vmem(2),
        scratch_shapes=[pltpu.VMEM((STEPS * picks, 2 * LANES), jnp.bfloat16)],
        name="second_pair",
        **params,
    )(orbitals, occ_second, *handed)


def pack_kernel(plan, turns, targets, levels_ref, *refs):
    rows, cols, row_width, col_width = plan
    count = len(refs) - len(targets) - 1
    arrived, outs, mixed_ref = refs[:count], refs[count:-1], refs[-1]
    r, c = own_place()
    first = 0
    for ref in arrived:
        mixed_ref[first : first + ref.shape[0], :] = ref[...].astype(jnp.float32)
        first += ref.shape[0]
    weight = pair_weights([c ^ turn for turn in turns], levels_ref)
    columns = []
    for side in range(2):
        start = pl.multiple_of((c ^ side) * col_width, LANES)
        columns.append((weight * mixed_ref[:, pl.ds(start, col_width)]).astype(jnp.bfloat16))
    for (turn, side), out_ref in zip(targets, outs):
        start = pl.multiple_of((r ^ turn) // 2 * (2 * row_width), LANES)
        out_ref[:, : 2 * row_width] = mixed_ref[:, pl.ds(start, 2 * row_width)].astype(jnp.bfloat16)
        out_ref[:, 2 * row_width :] = columns[side]


def pack(arrived, levels, turns, targets, plan):
    rows, cols, row_width, col_width = plan
    pairs = STEPS * len(turns)
    entries = arrived[0].shape[1]
    shapes = [(pairs, 2 * row_width + col_width)] * len(targets)
    return pl.pallas_call(
        functools.partial(pack_kernel, plan, turns, targets),
        out_shape=[jax.ShapeDtypeStruct(shape, jnp.bfloat16) for shape in shapes],
        in_specs=in_vmem(1 + len(arrived)),
        out_specs=in_vmem(len(shapes)),
        scratch_shapes=[pltpu.VMEM((pairs, entries), jnp.float32)],
        compiler_params=pltpu.CompilerParams(vmem_limit_bytes=VMEM_LIMIT),
        cost_estimate=cost(10**9, 10**6),
        name="pack",
    )(levels, *arrived)


def stacked(refs, lanes):
    return jnp.concatenate([ref[:, lanes].astype(jnp.float32) for ref in refs], axis=0).astype(jnp.bfloat16)


def join_kernel(row_width, *refs):
    messages, outs = refs[:-2], refs[-2:]
    depth = messages[0].shape[0]
    merge = max(1, 16 // depth)
    r, _ = own_place()
    for j in range(0, len(messages), merge):
        here = slice(depth * j, depth * (j + merge))
        columns = stacked(messages[j : j + merge], slice(2 * row_width, None))
        for side, out_ref in enumerate(outs):
            lanes = pl.ds(pl.multiple_of((r & 1 ^ side) * row_width, LANES), row_width)
            out_ref[here, :row_width] = stacked(messages[j : j + merge], lanes)
            out_ref[here, row_width:] = columns


def join(messages, plan):
    rows, cols, row_width, col_width = plan
    depth = messages[0].shape[0]
    return pl.pallas_call(
        functools.partial(join_kernel, row_width),
        out_shape=[jax.ShapeDtypeStruct((depth * len(messages), row_width + col_width), jnp.bfloat16)] * 2,
        in_specs=in_vmem(len(messages)),
        out_specs=in_vmem(2),
        compiler_params=pltpu.CompilerParams(vmem_limit_bytes=VMEM_LIMIT),
        cost_estimate=cost(10**9, 10**6),
        name="join",
    )(*messages)


def outer_kernel(row_width, block, slots, *refs):
    messages, (out_ref, right_ref, held_ref, sems) = refs[:-4], refs[-4:]
    depth = messages[0].shape[0]
    for j, ref in enumerate(messages):
        right_ref[depth * j : depth * (j + 1), :] = ref[:, row_width:]
    count = row_width // block

    def copy_out(i, slot):
        rows = pl.ds(pl.multiple_of(i * block, block), block)
        return pltpu.make_async_copy(held_ref.at[slot], out_ref.at[rows], sems.at[slot])

    def product(first, size):
        left = jnp.concatenate([ref[:, pl.ds(first, size)] for ref in messages], axis=0)
        return lax.dot_general(left, right_ref[...], (((0,), (0,)), ((), ())), preferred_element_type=jnp.float32)

    def step(i, carry):
        slot = lax.rem(i, slots)

        @pl.when(i >= slots)
        def _():
            copy_out(i - slots, slot).wait()

        held_ref[slot] = product(pl.multiple_of(i * block, block), block)
        copy_out(i, slot).start()
        return carry

    half = block // 2
    for part in range(2):
        here = pl.ds(part * half, half)
        held_ref[0, part * half : (part + 1) * half, :] = product(part * half, half)
        pltpu.make_async_copy(held_ref.at[0, here], out_ref.at[here], sems.at[0]).start()
    lax.fori_loop(1, count, step, 0)
    for i in range(max(0, count - slots), count):
        copy_out(i, i % slots).wait()


def outer(messages, plan):
    rows, cols, row_width, col_width = plan
    depth = messages[0].shape[0]
    block = min(256, row_width)
    slots = min(4, row_width // block)
    return pl.pallas_call(
        functools.partial(outer_kernel, row_width, block, slots),
        out_shape=jax.ShapeDtypeStruct((row_width, col_width), jnp.float32),
        in_specs=in_vmem(len(messages)),
        out_specs=pl.BlockSpec(memory_space=pltpu.HBM),
        scratch_shapes=[
            pltpu.VMEM((depth * len(messages), col_width), jnp.bfloat16),
            pltpu.VMEM((slots, block, col_width), jnp.float32),
            pltpu.SemaphoreType.DMA((slots,)),
        ],
        compiler_params=pltpu.CompilerParams(vmem_limit_bytes=VMEM_LIMIT),
        cost_estimate=cost(10**10, 3 * 10**7),
        name="outer",
    )(*messages)


def copy_kernel(value_ref, behind_ref, out_ref):
    out_ref[...] = value_ref[...]


def copied(value, behind):
    return pl.pallas_call(
        copy_kernel,
        out_shape=jax.ShapeDtypeStruct(value.shape, value.dtype),
        in_specs=in_vmem(2),
        out_specs=in_vmem(1)[0],
        compiler_params=pltpu.CompilerParams(vmem_limit_bytes=VMEM_LIMIT),
        cost_estimate=cost(10**6, 10**5),
        name="copied",
    )(value, behind)


def shifted(value, axis, by):
    devices = lax.axis_size(axis)
    return lax.ppermute(value, axis, [(i, (i + by) % devices) for i in range(devices)])


def turned(value, axis, turn):
    devices = lax.axis_size(axis)
    return lax.ppermute(value, axis, [(i, i ^ turn) for i in range(devices)])


def sent_across(value, turn, side, rows, cols):
    moves = [(r * cols + c, (r ^ turn) * cols + (c ^ side)) for r in range(rows) for c in range(cols)]
    return lax.ppermute(value, ("row", "col"), moves)


def on_device(cond_orbitals, occ_orbitals, cond_energy, occ_energy, occ_band, sphere_index):
    rows = lax.axis_size("row")
    cols = lax.axis_size("col")
    entries = 2 * sphere_index.shape[1]
    plan = (rows, cols, entries // rows, entries // cols)
    occ_second = shifted(occ_orbitals, "row", 1)
    own, later = transform(cond_orbitals, occ_orbitals, occ_second, sphere_index, occ_band.shape)
    levels = jnp.stack([cond_energy, occ_energy, (occ_band + later[0]).astype(jnp.float32)])
    targets = [(0, 0)] + [(turn, side) for side in range(2) for turn in range(rows - 2, 0, -2)] + [(0, 1)]

    def sent(packed):
        return [packed[0]] + [sent_across(value, *target, rows, cols) for value, target in zip(packed[1:], targets[1:])]

    others, other_turns, bit = [], [], cols // 2
    while bit > 2:
        held = jnp.concatenate([own, *others], axis=0) if others else own
        others.append(turned(held, "col", bit))
        other_turns += [turn + bit for turn in [0, *other_turns]]
        bit //= 2
    turns = [0, *other_turns]
    early = sent(pack([own, *others], levels, turns, targets, plan))
    relayed = turned(jnp.concatenate(others, axis=0) if len(others) > 1 else others[0], "col", bit)
    beside = turned(copied(own, levels), "col", bit)
    late = sent(pack([beside, relayed], levels, [turn + bit for turn in turns], targets, plan))
    joined = []
    for messages in (early, late):
        kept, passed = join(messages, plan)
        joined += [kept, turned(passed, "row", 1)]
    return outer(joined, plan)


def solution(mesh):
    placed = (P(("row", "col"), None, None), P(("row", "col"), None, None), P(), P(), P(), P())
    return jax.shard_map(
        on_device, mesh=mesh, in_specs=placed, out_specs=P("row", "col"), check_vma=False
    )
```

```python
import functools
import math

import jax
import jax.numpy as jnp
import numpy as np
from jax import lax
from jax.experimental import pallas as pl
from jax.experimental.pallas import tpu as pltpu
from jax.sharding import PartitionSpec as P

GMAX = 18
STEPS = 2
RADIX = 6
SPAN = 2 * GMAX + 1
KX_ROWS = 40
LANES = 128
OMEGA_SQUARED = 0.0625
TILE = 512
VMEM_LIMIT = 40 * 2**20


COSINE_TERMS = 10


def table_rows(grid):
    width = (grid // RADIX) * grid
    x_first = 4 * width
    return width, x_first, x_first + 2 * KX_ROWS


def cosine(phase, grid):
    phase = phase - (phase * 43691 >> 21) * 48
    angle = (phase - grid // 2).astype(jnp.float32) * np.float32(2.0 * math.pi / grid)
    square = angle * angle
    value = jnp.zeros_like(angle)
    for term in reversed(range(COSINE_TERMS)):
        value = value * square - np.float32((-1.0) ** term / math.factorial(2 * term))
    return value


def in_two(values):
    upper = values.astype(jnp.bfloat16)
    return upper, (values - upper.astype(jnp.float32)).astype(jnp.bfloat16)


def write_tables(grid, table_ref, twiddle_ref):
    width, x_first, x_end = table_rows(grid)
    quarter = grid // 4

    def counted(shape, dimension):
        return lax.broadcasted_iota(jnp.int32, shape, dimension)

    row, lane = counted((2 * KX_ROWS, LANES), 0), counted((2 * KX_ROWS, LANES), 1)
    below = (row >= KX_ROWS).astype(jnp.int32)
    place = jnp.where(lane >= grid, lane - grid, lane)
    place = jnp.where(place >= grid, 0, place)
    frequency = row - KX_ROWS * below + (grid - GMAX)
    upper, lower = in_two(cosine(frequency * place + quarter * below, grid))
    mixed = jnp.where(lane < grid, upper.astype(jnp.float32), lower.astype(jnp.float32))
    table_ref[x_first:x_end, :] = mixed.astype(jnp.bfloat16)

    row, lane = counted((16, width), 0), counted((16, width), 1)
    below = (row >= RADIX).astype(jnp.int32)
    residue = jnp.where(row >= 2 * RADIX, 0, row - RADIX * below)
    twiddle_ref[...] = cosine(residue * (lane * 43691 >> 21) + quarter * below, grid)

    lane = counted((1, LANES), 1)
    q = lane * 57 >> 10
    kz = lane - q * GMAX + 1
    y_phase = RADIX * (q + (grid // RADIX - GMAX // RADIX)) * counted((grid // RADIX, LANES), 0)
    z_phase = kz * counted((grid, LANES), 0)
    cos_y, sin_y = cosine(y_phase, grid), cosine(y_phase + 3 * quarter, grid)
    cos_z, sin_z = cosine(z_phase, grid), cosine(z_phase + 3 * quarter, grid)
    for y in range(grid // RADIX):
        cos_here, sin_here = cos_y[y : y + 1], sin_y[y : y + 1]
        whole = (cos_here * cos_z - sin_here * sin_z, -(sin_here * cos_z + cos_here * sin_z))
        for part, values in enumerate(whole):
            for level, piece in enumerate(in_two(values)):
                first = (2 * level + part) * width + y * grid
                table_ref[first : first + grid, :] = piece


def dft_six(re, im):
    half = 0.5
    root = math.sqrt(3.0) / 2.0
    s_re = [re[h] + re[h + 3] for h in range(3)]
    s_im = [im[h] + im[h + 3] for h in range(3)]
    d_re = [re[h] - re[h + 3] for h in range(3)]
    d_im = [im[h] - im[h + 3] for h in range(3)]
    out = [None] * 6
    sum_re, sum_im = s_re[1] + s_re[2], s_im[1] + s_im[2]
    dif_re, dif_im = (s_re[1] - s_re[2]) * root, (s_im[1] - s_im[2]) * root
    out[0] = (s_re[0] + sum_re, s_im[0] + sum_im)
    mid_re, mid_im = s_re[0] - half * sum_re, s_im[0] - half * sum_im
    out[2] = (mid_re + dif_im, mid_im - dif_re)
    out[4] = (mid_re - dif_im, mid_im + dif_re)
    sum_re, sum_im = (d_re[1] + d_re[2]) * root, (d_im[1] + d_im[2]) * root
    dif_re, dif_im = d_re[1] - d_re[2], d_im[1] - d_im[2]
    out[3] = (d_re[0] - dif_re, d_im[0] - dif_im)
    mid_re, mid_im = d_re[0] + half * dif_re, d_im[0] + half * dif_im
    out[1] = (mid_re + sum_im, mid_im - sum_re)
    out[5] = (mid_re - sum_im, mid_im + sum_re)
    return out


def dot(a, b):
    return jnp.dot(a, b, preferred_element_type=jnp.float32)


def own_place():
    return lax.axis_index("row"), lax.axis_index("col")


def spectrum_of(grid, cond, occ, table_ref, twiddle_ref):
    norm = np.float32(grid ** (-1.5))
    width, x_first, x_end = table_rows(grid)
    density = (cond.astype(jnp.float32) * occ.astype(jnp.float32)).astype(jnp.bfloat16)
    x_table = table_ref[x_first:x_end, : 2 * grid]
    section = dot(x_table, jnp.concatenate([density, density], axis=0))
    re = [section[:KX_ROWS, h * width : (h + 1) * width] for h in range(RADIX)]
    im = [section[KX_ROWS:, h * width : (h + 1) * width] for h in range(RADIX)]
    rows = []
    for residue, (d_re, d_im) in enumerate(dft_six(re, im)):
        if residue > 0:
            t_re = twiddle_ref[residue : residue + 1, :]
            t_im = twiddle_ref[RADIX + residue : RADIX + residue + 1, :]
            d_re, d_im = d_re * t_re - d_im * t_im, d_re * t_im + d_im * t_re
        rows.append(jnp.concatenate([d_re, d_im], axis=1))
    whole = jnp.concatenate(rows, axis=0)
    whole_hi = whole.astype(jnp.bfloat16)
    whole_lo = (whole - whole_hi.astype(jnp.float32)).astype(jnp.bfloat16)

    def rotation(first):
        cos_part = table_ref[first : first + width, :]
        sin_part = table_ref[first + width : first + 2 * width, :]
        upper = jnp.concatenate([cos_part, sin_part], axis=1)
        return jnp.concatenate([upper, jnp.concatenate([-sin_part, cos_part], axis=1)], axis=0)

    upper, lower = rotation(0), rotation(2 * width)
    spectrum = (dot(whole_hi, upper) + dot(whole_lo, upper) + dot(whole_hi, lower)) * norm
    parts = []
    for side in range(2):
        own = spectrum[:, side * LANES : (side + 1) * LANES]
        for group in range(RADIX // 2):
            first = 2 * group * KX_ROWS
            parts.append(jnp.concatenate([own[first : first + KX_ROWS], own[first + KX_ROWS : first + 2 * KX_ROWS]], axis=1))
    return jnp.concatenate(parts, axis=0).astype(jnp.bfloat16)


def pair_weights(sources, levels_ref):
    rows, cols = lax.axis_size("row"), lax.axis_size("col")
    r, _ = own_place()
    devices = rows * cols
    pairs = STEPS * len(sources)
    line = lax.broadcasted_iota(jnp.int32, (pairs, 1), 0)
    band = jnp.zeros((pairs, 1), jnp.int32)
    slot = jnp.zeros((pairs, 1), jnp.int32)
    for j, source in enumerate(sources):
        place = r * cols + source
        for step in range(STEPS):
            here = line == STEPS * j + step
            band = jnp.where(here, place, band)
            slot = jnp.where(here, lax.rem(place - step * cols + devices, devices), slot)
    lane = lax.broadcasted_iota(jnp.int32, (pairs, levels_ref.shape[1]), 1)

    def at(which, chosen):
        return jnp.sum(jnp.where(lane == chosen, levels_ref[which : which + 1, :], 0.0), axis=1, keepdims=True)

    gap = at(0, band) - at(1, at(2, slot).astype(jnp.int32))
    return -4.0 * gap / (gap * gap + OMEGA_SQUARED) / (devices * STEPS)


def first_kernel(grid, orbitals_ref, sphere_ref, coef_ref, places_ref, table_ref, twiddle_ref, cube_ref):
    half = grid // 2
    sx, sy, kz = sphere_ref[0:1, :], sphere_ref[1:2, :], sphere_ref[2:3, :]
    kx = jnp.where(sx >= half, sx - grid, sx) + GMAX
    ky = jnp.where(sy >= half, sy - grid, sy) + GMAX
    q = (ky * 43) >> 8
    residue = ky - q * RADIX
    places_ref[0:1, :] = (residue & 1) * LANES + q * GMAX + kz - 1
    places_ref[1:2, :] = (residue >> 1) * KX_ROWS + kx
    write_tables(grid, table_ref, twiddle_ref)
    cube_ref[...] = spectrum_of(grid, orbitals_ref[0], orbitals_ref[1], table_ref, twiddle_ref)

    @pl.when(on_even_core())
    def _():
        pick(cube_ref, places_ref, coef_ref, [0])


def pick(cube_ref, places_ref, coef_ref, pairs):
    groups = RADIX // 2 * KX_ROWS // 8
    half_count = places_ref.shape[1]
    counted = lax.broadcasted_iota(jnp.int32, (2 * LANES, TILE), 0).astype(jnp.float32).astype(jnp.bfloat16)
    line = lax.broadcasted_iota(jnp.int32, (8, TILE), 0)
    parts = [(pair, side) for pair in pairs for side in range(2)]
    for first in range(0, half_count, TILE):
        here = slice(first, first + TILE)
        lane = places_ref[0:1, here].astype(jnp.float32).astype(jnp.bfloat16)
        one_hot = jnp.where(counted == lane, jnp.bfloat16(1), jnp.bfloat16(0))
        found = dot(cube_ref[...], one_hot)
        away = line - places_ref[1:2, here]
        values = [jnp.zeros((8, TILE), jnp.float32)] * len(parts)
        for group in range(groups):
            chosen = away == -8 * group
            for which in range(len(parts)):
                start = (which * groups + group) * 8
                values[which] = jnp.where(chosen, found[start : start + 8], values[which])
        for (pair, side), value in zip(parts, values):
            value = jnp.sum(value, axis=0, keepdims=True).astype(jnp.bfloat16)
            coef_ref[pair : pair + 1, side * half_count + first : side * half_count + first + TILE] = value


def on_even_core():
    return lax.rem(lax.axis_index("row"), 2) == 0


def second_kernel(
    grid, orbitals_ref, occ_ref, first_ref, places_ref, table_ref, twiddle_ref, first_cube_ref, coef_ref, later_ref, cube_ref
):
    picks = first_cube_ref.shape[0]
    later_ref[...] = jnp.zeros_like(later_ref)
    cube_ref[picks:, :] = spectrum_of(grid, orbitals_ref[0], occ_ref[0], table_ref, twiddle_ref)

    @pl.when(on_even_core())
    def _():
        coef_ref[0:1, :] = first_ref[...]
        pick(cube_ref.at[picks:], places_ref, coef_ref, [1])

    @pl.when(jnp.logical_not(on_even_core()))
    def _():
        cube_ref[:picks, :] = first_cube_ref[...]
        pick(cube_ref, places_ref, coef_ref, [0, 1])


def cost(flops, data):
    return pl.CostEstimate(flops=flops, bytes_accessed=data, transcendentals=0)


def in_vmem(count):
    return [pl.BlockSpec(memory_space=pltpu.VMEM)] * count


def transform(cond_orbitals, occ_orbitals, occ_second, sphere_index, band_shape):
    grid = cond_orbitals.shape[1]
    half_count = sphere_index.shape[1]
    width, _, table_count = table_rows(grid)
    which = lax.broadcasted_iota(jnp.int32, (2, *cond_orbitals.shape[1:]), 0)
    orbitals = jnp.where(which == 0, cond_orbitals, occ_orbitals)
    picks = RADIX * KX_ROWS
    params = dict(
        compiler_params=pltpu.CompilerParams(vmem_limit_bytes=VMEM_LIMIT),
        cost_estimate=cost(2 * 10**9, 2 * 10**6),
    )
    handed = pl.pallas_call(
        functools.partial(first_kernel, grid),
        out_shape=[
            jax.ShapeDtypeStruct((1, 2 * half_count), jnp.bfloat16),
            jax.ShapeDtypeStruct((2, half_count), jnp.int32),
            jax.ShapeDtypeStruct((table_count, LANES), jnp.bfloat16),
            jax.ShapeDtypeStruct((16, width), jnp.float32),
            jax.ShapeDtypeStruct((picks, 2 * LANES), jnp.bfloat16),
        ],
        in_specs=in_vmem(2),
        out_specs=in_vmem(5),
        name="first_pair",
        **params,
    )(orbitals, sphere_index)
    return pl.pallas_call(
        functools.partial(second_kernel, grid),
        out_shape=[
            jax.ShapeDtypeStruct((STEPS, 2 * half_count), jnp.bfloat16),
            jax.ShapeDtypeStruct((3, *band_shape), jnp.int32),
        ],
        in_specs=in_vmem(7),
        out_specs=in_vmem(2),
        scratch_shapes=[pltpu.VMEM((STEPS * picks, 2 * LANES), jnp.bfloat16)],
        name="second_pair",
        **params,
    )(orbitals, occ_second, *handed)


def pack_kernel(plan, turns, targets, levels_ref, *refs):
    rows, cols, row_width, col_width = plan
    count = len(refs) - len(targets) - 1
    arrived, outs, mixed_ref = refs[:count], refs[count:-1], refs[-1]
    r, c = own_place()
    first = 0
    for ref in arrived:
        mixed_ref[first : first + ref.shape[0], :] = ref[...].astype(jnp.float32)
        first += ref.shape[0]
    weight = pair_weights([c ^ turn for turn in turns], levels_ref)
    columns = []
    for side in range(2):
        start = pl.multiple_of((c ^ side) * col_width, LANES)
        columns.append((weight * mixed_ref[:, pl.ds(start, col_width)]).astype(jnp.bfloat16))
    for (turn, side), out_ref in zip(targets, outs):
        start = pl.multiple_of((r ^ turn) // 2 * (2 * row_width), LANES)
        out_ref[:, : 2 * row_width] = mixed_ref[:, pl.ds(start, 2 * row_width)].astype(jnp.bfloat16)
        out_ref[:, 2 * row_width :] = columns[side]


def pack(arrived, levels, turns, targets, plan):
    rows, cols, row_width, col_width = plan
    pairs = STEPS * len(turns)
    entries = arrived[0].shape[1]
    shapes = [(pairs, 2 * row_width + col_width)] * len(targets)
    return pl.pallas_call(
        functools.partial(pack_kernel, plan, turns, targets),
        out_shape=[jax.ShapeDtypeStruct(shape, jnp.bfloat16) for shape in shapes],
        in_specs=in_vmem(1 + len(arrived)),
        out_specs=in_vmem(len(shapes)),
        scratch_shapes=[pltpu.VMEM((pairs, entries), jnp.float32)],
        compiler_params=pltpu.CompilerParams(vmem_limit_bytes=VMEM_LIMIT),
        cost_estimate=cost(10**9, 10**6),
        name="pack",
    )(levels, *arrived)


def stacked(refs, lanes):
    return jnp.concatenate([ref[:, lanes].astype(jnp.float32) for ref in refs], axis=0).astype(jnp.bfloat16)


def join_kernel(row_width, *refs):
    messages, outs = refs[:-2], refs[-2:]
    depth = messages[0].shape[0]
    merge = max(1, 16 // depth)
    r, _ = own_place()
    for j in range(0, len(messages), merge):
        here = slice(depth * j, depth * (j + merge))
        columns = stacked(messages[j : j + merge], slice(2 * row_width, None))
        for side, out_ref in enumerate(outs):
            lanes = pl.ds(pl.multiple_of((r & 1 ^ side) * row_width, LANES), row_width)
            out_ref[here, :row_width] = stacked(messages[j : j + merge], lanes)
            out_ref[here, row_width:] = columns


def join(messages, plan):
    rows, cols, row_width, col_width = plan
    depth = messages[0].shape[0]
    return pl.pallas_call(
        functools.partial(join_kernel, row_width),
        out_shape=[jax.ShapeDtypeStruct((depth * len(messages), row_width + col_width), jnp.bfloat16)] * 2,
        in_specs=in_vmem(len(messages)),
        out_specs=in_vmem(2),
        compiler_params=pltpu.CompilerParams(vmem_limit_bytes=VMEM_LIMIT),
        cost_estimate=cost(10**9, 10**6),
        name="join",
    )(*messages)


def outer_kernel(row_width, block, slots, *refs):
    messages, (out_ref, right_ref, held_ref, sems) = refs[:-4], refs[-4:]
    depth = messages[0].shape[0]
    for j, ref in enumerate(messages):
        right_ref[depth * j : depth * (j + 1), :] = ref[:, row_width:]
    count = row_width // block

    def copy_out(i, slot):
        rows = pl.ds(pl.multiple_of(i * block, block), block)
        return pltpu.make_async_copy(held_ref.at[slot], out_ref.at[rows], sems.at[slot])

    def product(first, size):
        left = jnp.concatenate([ref[:, pl.ds(first, size)] for ref in messages], axis=0)
        return lax.dot_general(left, right_ref[...], (((0,), (0,)), ((), ())), preferred_element_type=jnp.float32)

    def step(i, carry):
        slot = lax.rem(i, slots)

        @pl.when(i >= slots)
        def _():
            copy_out(i - slots, slot).wait()

        held_ref[slot] = product(pl.multiple_of(i * block, block), block)
        copy_out(i, slot).start()
        return carry

    half = block // 2
    for part in range(2):
        here = pl.ds(part * half, half)
        held_ref[0, part * half : (part + 1) * half, :] = product(part * half, half)
        pltpu.make_async_copy(held_ref.at[0, here], out_ref.at[here], sems.at[0]).start()
    lax.fori_loop(1, count, step, 0)
    for i in range(max(0, count - slots), count):
        copy_out(i, i % slots).wait()


def outer(messages, plan):
    rows, cols, row_width, col_width = plan
    depth = messages[0].shape[0]
    block = min(256, row_width)
    slots = min(4, row_width // block)
    return pl.pallas_call(
        functools.partial(outer_kernel, row_width, block, slots),
        out_shape=jax.ShapeDtypeStruct((row_width, col_width), jnp.float32),
        in_specs=in_vmem(len(messages)),
        out_specs=pl.BlockSpec(memory_space=pltpu.HBM),
        scratch_shapes=[
            pltpu.VMEM((depth * len(messages), col_width), jnp.bfloat16),
            pltpu.VMEM((slots, block, col_width), jnp.float32),
            pltpu.SemaphoreType.DMA((slots,)),
        ],
        compiler_params=pltpu.CompilerParams(vmem_limit_bytes=VMEM_LIMIT),
        cost_estimate=cost(10**10, 3 * 10**7),
        name="outer",
    )(*messages)


def copy_kernel(value_ref, behind_ref, out_ref):
    out_ref[...] = value_ref[...]


def copied(value, behind):
    return pl.pallas_call(
        copy_kernel,
        out_shape=jax.ShapeDtypeStruct(value.shape, value.dtype),
        in_specs=in_vmem(2),
        out_specs=in_vmem(1)[0],
        compiler_params=pltpu.CompilerParams(vmem_limit_bytes=VMEM_LIMIT),
        cost_estimate=cost(10**6, 10**5),
        name="copied",
    )(value, behind)


def shifted(value, axis, by):
    devices = lax.axis_size(axis)
    return lax.ppermute(value, axis, [(i, (i + by) % devices) for i in range(devices)])


def turned(value, axis, turn):
    devices = lax.axis_size(axis)
    return lax.ppermute(value, axis, [(i, i ^ turn) for i in range(devices)])


def sent_across(value, turn, side, rows, cols):
    moves = [(r * cols + c, (r ^ turn) * cols + (c ^ side)) for r in range(rows) for c in range(cols)]
    return lax.ppermute(value, ("row", "col"), moves)


def on_device(cond_orbitals, occ_orbitals, cond_energy, occ_energy, occ_band, sphere_index):
    rows = lax.axis_size("row")
    cols = lax.axis_size("col")
    entries = 2 * sphere_index.shape[1]
    plan = (rows, cols, entries // rows, entries // cols)
    occ_second = shifted(occ_orbitals, "row", 1)
    own, later = transform(cond_orbitals, occ_orbitals, occ_second, sphere_index, occ_band.shape)
    line = lax.broadcasted_iota(jnp.int32, (3, occ_band.shape[0]), 0)
    bands = (occ_band + later).astype(jnp.float32)
    levels = jnp.where(line == 0, cond_energy, jnp.where(line == 1, occ_energy, bands))
    targets = [(0, 0)] + [(turn, side) for side in (1, 0) for turn in range(rows - 2, -2, -2) if turn or side]
    targets.append(targets.pop(rows // 2))

    def sent(packed):
        return [packed[0]] + [sent_across(value, *target, rows, cols) for value, target in zip(packed[1:], targets[1:])]

    others, other_turns, bit = [], [], cols // 2
    while bit > 2:
        held = jnp.concatenate([own, *others], axis=0) if others else own
        others.append(turned(held, "col", bit))
        other_turns += [turn + bit for turn in [0, *other_turns]]
        bit //= 2
    turns = [0, *other_turns]
    early = sent(pack([own, *others], levels, turns, targets, plan))
    relayed = turned(jnp.concatenate(others, axis=0) if len(others) > 1 else others[0], "col", bit)
    beside = turned(copied(own, levels), "col", bit)
    late = sent(pack([beside, relayed], levels, [turn + bit for turn in turns], targets, plan))
    joined = []
    for messages in (early, late):
        kept, passed = join(messages, plan)
        joined += [kept, turned(passed, "row", 1)]
    return outer(joined, plan)


def solution(mesh):
    placed = (P(("row", "col"), None, None), P(("row", "col"), None, None), P(), P(), P(), P())
    return jax.shard_map(
        on_device, mesh=mesh, in_specs=placed, out_specs=P("row", "col"), check_vma=False
    )
```
